32 devices in a mesh: groups: 2 (over x), hi: 8 (over z, y), lo: 2 (over core).
Axes of the slice: x: 2, y: 2, z: 4, core: 2. Of those that a mesh axis runs over, the one named last changes fastest.
Arguments:
- vectors: float32 [64, 65536], P(None, ('groups', 'hi', 'lo')), parts along dimension 1, may hold values from -6 to 6
- tile_values: float32 [2048, 128, 128], P(('groups', 'hi', 'lo')), parts along dimension 0, may hold values from -0.25 to 0.25
- tile_cols: int32 [1024], P(('hi', 'lo')), may hold values from 0 to 15, as said below
- live_rows: int32 [16], P(('hi', 'lo')), may hold values from 512 to 2048
- boundary_map: int32 [32768], P(('hi', 'lo')), may hold values from -1 to 2047
- field_levels: int32 [8], P('groups'), parts along dimension 0, may hold values from -8 to 8
Outputs:
- filtered: float32 [64, 65536], P(None, ('groups', 'hi', 'lo')), parts along dimension 1
- correlation: float32 [128, 64], P('groups'), parts along dimension 0
- projected: float32 [128, 64], P('groups'), parts along dimension 0
The draws below stay inside these ranges and needn't reach their ends.
There are 2 independent parts, one for each index of `groups`. The reference program is written for one: setup_inputs(seed, part) draws one part's arguments, and reference() takes and returns one part's arrays. A program takes and returns all parts, laid end to end along the dimension named above; an argument that names none is the same for every part. Nothing has to cross between parts.
Inputs may be any that keep to these rules, and one draw needn't show every extreme that they name: `tile_cols`: each row block's 4 column blocks are distinct.
All inputs are finite; a program needn't handle non-finite values.
Results may differ from the reference program's by a relative error of at most 0.0001.
Values sent between devices are 32-bit elements; how exact they have to be, the bound alone decides.
No kernel may reach another device: no remote copies, remote signals or barrier semaphores. Data moves between devices by JAX's collectives and lax.ppermute only.
A program may use at most 64 MiB of HBM per device.

```python
import jax
import jax.numpy as jnp
from jax import lax

NV = 64
TILE = 128
TPR = 4
RB_DEV = 16
DEVS = 16
BITS = 4
ROWS = 2048
STATES = 32768


def draw_tile_cols(key, part):
    key = jax.random.fold_in(key, 11)
    scores = jax.random.randint(key, (DEVS * RB_DEV, RB_DEV), 0, 1 << 20, dtype=jnp.int32)
    scores = scores * RB_DEV + jnp.arange(RB_DEV, dtype=jnp.int32)[None, :]
    order = jnp.argsort(scores, axis=1, stable=True)
    return order[:, :TPR].reshape(DEVS * RB_DEV * TPR).astype(jnp.int32)


def draw_live_rows(key, part):
    key = jax.random.fold_in(key, 12)
    first_key, second_key, third_key = jax.random.split(key, 3)
    counts = jax.random.randint(first_key, (DEVS,), ROWS // 4, ROWS + 1, dtype=jnp.int32)
    fullest = jax.random.randint(second_key, (), 0, DEVS, dtype=jnp.int32)
    emptiest = (fullest + 1 + jax.random.randint(third_key, (), 0, DEVS - 1, dtype=jnp.int32)) % DEVS
    places = jnp.arange(DEVS, dtype=jnp.int32)
    counts = jnp.where(places == fullest, ROWS, counts)
    counts = jnp.where(places == emptiest, ROWS // 4, counts)
    return counts.astype(jnp.int32)


def draw_boundary_map(key, part):
    key = jax.random.fold_in(key, 13)
    first_key, second_key, third_key = jax.random.split(key, 3)
    targets = jax.random.randint(first_key, (STATES,), 0, ROWS, dtype=jnp.int32)
    linked = jax.random.randint(second_key, (STATES,), 0, 2, dtype=jnp.int32)
    targets = jnp.where(linked == 1, targets, -1)
    chosen = jax.random.randint(third_key, (), 0, STATES - 1, dtype=jnp.int32)
    places = jnp.arange(STATES, dtype=jnp.int32)
    targets = jnp.where(places == chosen, ROWS - 1, targets)
    targets = jnp.where(places == chosen + 1, -1, targets)
    return targets.astype(jnp.int32)


def touch_ends(drawn, own_key, smallest, largest):
    longest = drawn.shape.index(max(drawn.shape))
    spots = []
    for shift in (0, 1):
        where = [jax.random.randint(jax.random.fold_in(own_key, axis), (), 0, length) for axis, length in enumerate(drawn.shape)]
        where[longest] = (where[longest] + shift) % drawn.shape[longest]
        spots.append(tuple(where))
    return drawn.at[spots[0]].set(smallest).at[spots[1]].set(largest)


def level_of(rng, shape, cuts, least, top_value):
    level, own = 1.0, jax.random.fold_in(rng, 6)
    for position, parts in cuts:
        heights = jnp.exp(jax.random.uniform(jax.random.fold_in(own, position), (parts,), jnp.float32, least / len(cuts), top_value / len(cuts)))
        level = level * jnp.repeat(heights, shape[position] // parts).reshape([-1 if axis == position else 1 for axis in range(len(shape))])
    return level


def centred(rng, shape, spread, reach, cuts=(), kind=jnp.bfloat16):
    array = jax.random.normal(rng, shape, jnp.float32) * spread
    if len(cuts) > 0:
        array = level_of(rng, shape, cuts, -0.22, 0.18) * array
    return jnp.clip(array, min=-reach, max=reach).astype(kind)


def setup_inputs(seed: int = 0, part: int = 0) -> dict:
    keys = jax.random.split(jax.random.key(seed), 7)
    part_splits = jax.random.split(jax.random.fold_in(keys[6], part), 7)
    vectors = centred(part_splits[0], (NV, STATES), 1.0, 6.0, ((1, 16),), jnp.float32)
    tile_values = centred(part_splits[1], (DEVS * RB_DEV * TPR, TILE, TILE), (TILE * TPR) ** -0.5, 0.25, ((0, 16),), jnp.float32)
    tile_cols = draw_tile_cols(jax.random.fold_in(keys[6], 71), part)
    live_rows = draw_live_rows(jax.random.fold_in(keys[6], 71), part)
    boundary_map = draw_boundary_map(jax.random.fold_in(keys[6], 71), part)
    field_levels = touch_ends(jax.random.randint(part_splits[5], (BITS,), -8, 9), jax.random.fold_in(part_splits[5], 1), -8, 8).astype(jnp.int32)
    return dict(vectors=vectors, tile_values=tile_values, tile_cols=tile_cols, live_rows=live_rows, boundary_map=boundary_map, field_levels=field_levels)


HOP_SCALE = 0.5
ANISOTROPY = 1.0
FIELD_STEP = 0.25
HALF_WIDTH = 4.0


def onsite_shift(configs, field_levels):
    places = jnp.arange(BITS, dtype=jnp.int32)
    bitrows = jnp.right_shift(configs[:, None], places[None, :]) & 1
    spins = bitrows.astype(jnp.float32) - 0.5
    fields = field_levels.astype(jnp.float32) * FIELD_STEP
    single = jnp.sum(fields[None, :] * spins, axis=1)
    paired = jnp.sum(spins[:, :-1] * spins[:, 1:], axis=1)
    return single + ANISOTROPY * paired


def local_part(field, tile_values, tile_cols):
    blocked = field.reshape(NV, DEVS, RB_DEV, TILE).transpose(1, 0, 2, 3)
    weights = tile_values.reshape(DEVS, RB_DEV, TPR, TILE, TILE)
    columns = tile_cols.reshape(DEVS, RB_DEV, TPR)

    def one_device(pieces):
        block_rows, tiles, chosen = pieces
        picked = block_rows[:, chosen]
        return jnp.einsum("vbtj,btij->vbi", picked, tiles, precision=lax.Precision.HIGHEST)

    result = lax.map(one_device, (blocked, weights, columns))
    return result.transpose(1, 0, 2, 3).reshape(NV, DEVS, ROWS)


def operate(field, tile_values, tile_cols, shifts, alive, boundary_map):
    total = local_part(field, tile_values, tile_cols)
    shaped = field.reshape(NV, DEVS, ROWS)
    total = total + shifts[None, :, None] * shaped
    indices = jnp.arange(DEVS, dtype=jnp.int32)
    configs = indices ^ ((DEVS - 1) // 3)
    for bond in range(BITS - 1):
        partner = indices ^ (3 << bond)
        differ = (jnp.right_shift(configs, bond) & 1) != (jnp.right_shift(configs, bond + 1) & 1)
        coupling = HOP_SCALE * differ.astype(jnp.float32)
        total = total + coupling[None, :, None] * shaped[:, partner, :]
    flipped = shaped[:, indices ^ 1, :]
    targets = boundary_map.reshape(DEVS, ROWS)
    safe = jnp.broadcast_to(jnp.maximum(targets, 0)[None], (NV, DEVS, ROWS))
    picked = jnp.take_along_axis(flipped, safe, axis=2)
    total = total + HOP_SCALE * jnp.where(targets[None] >= 0, picked, 0.0)
    return (alive[None] * total / HALF_WIDTH).reshape(NV, DEVS * ROWS)


def reference(vectors, tile_values, tile_cols, live_rows, boundary_map, field_levels):
    indices = jnp.arange(DEVS, dtype=jnp.int32)
    configs = indices ^ ((DEVS - 1) // 3)
    shifts = onsite_shift(configs, field_levels)
    alive = (jnp.arange(ROWS, dtype=jnp.int32)[None, :] < live_rows[:, None]).astype(jnp.float32)
    start = vectors * alive.reshape(DEVS * ROWS)[None, :]
    first = operate(start, tile_values, tile_cols, shifts, alive, boundary_map)
    second = 2.0 * operate(first, tile_values, tile_cols, shifts, alive, boundary_map) - start
    image = operate(second, tile_values, tile_cols, shifts, alive, boundary_map)
    correlation = jnp.dot(second, second.T, precision=lax.Precision.HIGHEST, preferred_element_type=jnp.float32) / STATES
    projected = jnp.dot(second, image.T, precision=lax.Precision.HIGHEST, preferred_element_type=jnp.float32) / STATES
    return (second, correlation, projected)
```

```python
import jax
import jax.numpy as jnp
from jax import lax
from jax.sharding import PartitionSpec as P

HOP_SCALE = 0.5
ANISOTROPY = 1.0
FIELD_STEP = 0.25
HALF_WIDTH = 4.0
AXES = ("hi", "lo")
EXACT = lax.Precision.HIGHEST


def bit(number, place):
    return (number >> place) & 1


def gram(left, right):
    return lax.dot_general(
        left, right, (((1,), (1,)), ((), ())), precision=EXACT, preferred_element_type=jnp.float32
    )


def local(vectors, tile_values, tile_cols, live_rows, boundary_map, field_levels):
    dev_count = lax.axis_size(AXES)
    high_bits = dev_count.bit_length() - 1
    flip = (dev_count - 1) // 3
    config_index = lax.axis_index(AXES) ^ flip
    vec_count, row_count = vectors.shape
    tile_size = tile_values.shape[1]
    block_count = row_count // tile_size
    per_block = tile_values.shape[0] // block_count
    weights = tile_values.reshape(block_count, per_block, tile_size, tile_size)
    columns = tile_cols.reshape(block_count, per_block)
    places = jnp.arange(high_bits, dtype=jnp.int32)
    bitrow = jnp.right_shift(config_index, places) & 1
    spins = bitrow.astype(jnp.float32) - 0.5
    fields = field_levels.astype(jnp.float32) * FIELD_STEP
    onsite = jnp.sum(fields * spins) + ANISOTROPY * jnp.sum(spins[:-1] * spins[1:])
    alive = (jnp.arange(row_count, dtype=jnp.int32) < live_rows[0]).astype(jnp.float32)
    linked = boundary_map >= 0
    targets = jnp.maximum(boundary_map, 0)

    def bond_pairs(bond):
        return [
            (source, source ^ (3 << bond))
            for source in range(dev_count)
            if bit(source ^ flip, bond) != bit(source ^ flip, bond + 1)
        ]

    def exchange(value, mask):
        pairs = [(source, source ^ mask) for source in range(dev_count)]
        return lax.ppermute(value, AXES, pairs)

    def own_part(field, flipped):
        picked = field.reshape(vec_count, block_count, tile_size)[:, columns]
        total = jnp.einsum("vbtj,btij->vbi", picked, weights, precision=EXACT)
        total = total.reshape(vec_count, row_count) + onsite * field
        neighbour = jnp.take(flipped, targets, axis=1)
        return total + HOP_SCALE * jnp.where(linked[None, :], neighbour, 0.0)

    def operate(field):
        flipped = exchange(field, 1)
        hops = [
            lax.ppermute(field, AXES, bond_pairs(bond)) for bond in reversed(range(high_bits - 1))
        ]
        total = own_part(field, flipped)
        for hop in reversed(hops):
            total = total + HOP_SCALE * hop
        return alive[None, :] * total / HALF_WIDTH

    def hop_gram(field):
        sent = []
        for bond in reversed(range(high_bits - 1)):
            if bond >= 2:
                cut = row_count * 3 // 4
                leads = [pair for pair in bond_pairs(bond) if bit(pair[0], bond - 1) == bit(pair[0], bond)]
            else:
                cut = row_count // 2
                leads = [pair for pair in bond_pairs(bond) if bit(pair[0], bond) == 0]
            follows = [(target, source) for source, target in leads]
            for pairs, begin, end in ((leads, 0, cut), (follows, cut, row_count)):
                part = field[:, begin:end]
                sent.append((part, lax.ppermute(part, AXES, pairs)))
        return sent

    start = vectors * alive[None, :]
    first = operate(start)
    second = 2.0 * operate(first) - start
    states = dev_count * row_count
    flipped = exchange(second, 1)
    sent = hop_gram(second)
    correlation = gram(second, second)
    own = own_part(second, flipped)
    projected = gram(second, alive[None, :] * own)
    crossed = sum(gram(mine, theirs) for mine, theirs in sent)
    projected = (projected + HOP_SCALE * (crossed + crossed.T)) / HALF_WIDTH
    sums = jnp.concatenate([correlation, projected], axis=1)
    for place in range(high_bits):
        sums = sums + exchange(sums, 1 << place)
    sums = sums / states
    return (second, sums[:, :vec_count], sums[:, vec_count:])


def solution(mesh):
    in_specs = (
        P(None, ("groups", "hi", "lo")),
        P(("groups", "hi", "lo"), None, None),
        P(("hi", "lo")),
        P(("hi", "lo")),
        P(("hi", "lo")),
        P("groups"),
    )
    out_specs = (P(None, ("groups", "hi", "lo")), P("groups", None), P("groups", None))
    return jax.shard_map(local, mesh=mesh, in_specs=in_specs, out_specs=out_specs, check_vma=False)
```

```python
import functools

import jax
import jax.numpy as jnp
from jax import lax
from jax.experimental import pallas as pl
from jax.experimental.pallas import tpu as pltpu
from jax.sharding import PartitionSpec as P

HOP_SCALE = 0.5
ANISOTROPY = 1.0
FIELD_STEP = 0.25
HALF_WIDTH = 4.0
AXES = ("hi", "lo")
STEPS = 4
F32, BF16 = jnp.float32, jnp.bfloat16
SMEM = pl.BlockSpec(memory_space=pltpu.SMEM)
LIMIT = 32 * 1024 * 1024


def bit(number, place):
    return (number >> place) & 1


def halves(value):
    head = value.astype(BF16)
    return head, (value - head.astype(F32)).astype(BF16)


def stacked(value):
    return jnp.concatenate(halves(value), axis=0)


def product(left, right):
    rows, columns = left.shape[0] // 2, right.shape[0] // 2
    whole = lax.dot_general(left, right, (((1,), (1,)), ((), ())), preferred_element_type=F32)
    tails = whole[:rows, columns:] + whole[rows:, :columns] + whole[rows:, columns:]
    return whole[:rows, :columns] + tails


def coupling(config, bond):
    differ = bit(config, bond) ^ bit(config, bond + 1)
    return jnp.where(differ == 1, HOP_SCALE, 0.0)


def onsite_of(config, fields_ref):
    count = fields_ref.shape[0]
    spins = [bit(config, place).astype(F32) - 0.5 for place in range(count)]
    total = jnp.float32(0.0)
    for place in range(count):
        total += fields_ref[place].astype(F32) * FIELD_STEP * spins[place]
    for place in range(count - 1):
        total += ANISOTROPY * spins[place] * spins[place + 1]
    return total


def alive_of(live_ref, first, count):
    rows = lax.broadcasted_iota(jnp.int32, (1, count), 1) + first
    return (rows < live_ref[0]).astype(F32)


def own_block(block, row, config, cols_ref, fields_ref, field_ref, split_ref, flipped_ref, tiles_ref, map_ref):
    per_block, tile = tiles_ref.shape[1], tiles_ref.shape[2]
    span = pl.ds(pl.multiple_of(block * tile, tile), tile)
    picked = []
    for which in range(per_block):
        column = cols_ref[block * per_block + which]
        picked.append(split_ref[:, pl.ds(pl.multiple_of(column * tile, tile), tile)])
    weights = jnp.concatenate([tiles_ref[row, which] for which in range(per_block)], axis=1)
    total = product(jnp.concatenate(picked, axis=1), stacked(weights))
    total += onsite_of(config, fields_ref) * field_ref[:, span]
    targets = jnp.broadcast_to(map_ref[:, span], (8, tile))
    inside, outside = targets & (tile - 1), targets // tile
    outside = jnp.where(targets < 0, -1, outside)
    groups = []
    for group in range(field_ref.shape[0] // 8):
        found = jnp.zeros((8, tile), F32)
        for source in range(field_ref.shape[1] // tile):
            values = flipped_ref[group * 8 : group * 8 + 8, source * tile : (source + 1) * tile]
            moved = jnp.take_along_axis(values, inside, axis=1)
            found = jnp.where(outside == source, moved, found)
        groups.append(found)
    return span, total + HOP_SCALE * jnp.concatenate(groups, axis=0)


def own_kernel(place_ref, cols_ref, fields_ref, field_ref, flipped_ref, tiles_ref, map_ref, out_ref, split_ref):
    step, blocks = pl.program_id(0), tiles_ref.shape[0]

    @pl.when(step == 0)
    def _():
        split_ref[...] = stacked(field_ref[...])

    for row in range(blocks):
        span, total = own_block(
            step * blocks + row, row, place_ref[0], cols_ref, fields_ref, field_ref, split_ref, flipped_ref, tiles_ref, map_ref
        )
        out_ref[:, span] = total


def own_gram_kernel(
    place_ref, cols_ref, fields_ref, live_ref, field_ref, flipped_ref, tiles_ref, map_ref, out_ref, split_ref
):
    step, blocks, tile = pl.program_id(0), tiles_ref.shape[0], tiles_ref.shape[2]
    count = field_ref.shape[0]

    @pl.when(step == 0)
    def _():
        split_ref[...] = stacked(field_ref[...])
        out_ref[:, :count] = product(split_ref[...], split_ref[...])
        out_ref[:, count:] = jnp.zeros((count, count), F32)

    parts = []
    for row in range(blocks):
        span, total = own_block(
            step * blocks + row, row, place_ref[0], cols_ref, fields_ref, field_ref, split_ref, flipped_ref, tiles_ref, map_ref
        )
        parts.append(alive_of(live_ref, (step * blocks + row) * tile, tile) * total)
    image = stacked(jnp.concatenate(parts, axis=1))
    width = blocks * tile
    out_ref[:, count:] += product(split_ref[:, pl.ds(pl.multiple_of(step * width, width), width)], image)


def combine_kernel(bonds, place_ref, live_ref, own_ref, *refs):
    hops, out_ref = refs[:bonds], refs[-1]
    total = own_ref[...]
    for bond in range(bonds):
        total += coupling(place_ref[0], bond) * hops[bond][...]
    out_ref[...] = alive_of(live_ref, 0, total.shape[1]) * total * (1.0 / HALF_WIDTH)


def filter_kernel(bonds, place_ref, live_ref, own_ref, *refs):
    hops, start_ref, out_ref, sent_ref = refs[:bonds], refs[bonds], refs[-2], refs[-1]
    total = own_ref[...]
    for bond in range(bonds):
        total += coupling(place_ref[0], bond) * hops[bond][...]
    image = alive_of(live_ref, 0, total.shape[1]) * total * (1.0 / HALF_WIDTH)
    second = 2.0 * image - start_ref[...]
    out_ref[...] = second
    width = sent_ref.shape[1]
    sent_ref[...] = jnp.where(place_ref[1] == 0, second[:, :width], second[:, width:])


def crossed_kernel(bonds, states, place_ref, own_ref, field_ref, *refs):
    hops, out_ref = refs[:bonds], refs[-1]
    width, count = hops[0].shape[1], own_ref.shape[0]
    theirs = jnp.zeros((count, width), F32)
    for bond in range(bonds):
        theirs += coupling(place_ref[0], bond) * hops[bond][...]
    mine = jnp.where(place_ref[1] == 0, field_ref[:, width:], field_ref[:, :width])
    crossed = product(stacked(mine), stacked(theirs))
    out_ref[:, :count] = own_ref[:, :count] * (1.0 / states)
    projected = own_ref[:, count:] + crossed + crossed.T
    out_ref[:, count:] = projected * (1.0 / (HALF_WIDTH * states))


def local(vectors, tile_values, tile_cols, live_rows, boundary_map, field_levels):
    dev_count = lax.axis_size(AXES)
    bonds = dev_count.bit_length() - 2
    flip = (dev_count - 1) // 3
    position = lax.axis_index(AXES)
    parity = sum(bit(position, place) for place in range(0, bonds + 1, 2)) & 1
    place = jnp.stack([position ^ flip, parity]).astype(jnp.int32)
    vec_count, row_count = vectors.shape
    tile_size = tile_values.shape[1]
    block_count = row_count // tile_size
    per_block = tile_values.shape[0] // block_count
    tiles = tile_values.reshape(block_count, per_block, tile_size, tile_size)
    targets = boundary_map.reshape(1, row_count)
    params = pltpu.CompilerParams(vmem_limit_bytes=LIMIT)

    def hop(value, bond):
        pairs = [
            (source, source ^ (3 << bond))
            if bit(source ^ flip, bond) != bit(source ^ flip, bond + 1)
            else (source, source)
            for source in range(dev_count)
        ]
        return lax.ppermute(value, AXES, pairs)

    def exchange(value, mask):
        return lax.ppermute(value, AXES, [(source, source ^ mask) for source in range(dev_count)])

    def whole(shape):
        return pl.BlockSpec(shape, lambda step: (0,) * len(shape))

    full = whole((vec_count, row_count))
    tile_spec = pl.BlockSpec(
        (block_count // STEPS, per_block, tile_size, tile_size), lambda step: (step, 0, 0, 0)
    )
    own_cost = pl.CostEstimate(
        flops=8 * vec_count * row_count * per_block * tile_size,
        bytes_accessed=4 * tile_values.size + 12 * vec_count * row_count,
        transcendentals=0,
    )
    split = pltpu.VMEM((2 * vec_count, row_count), BF16)

    def own_part(field, flipped):
        return pl.pallas_call(
            own_kernel,
            grid=(STEPS,),
            out_shape=jax.ShapeDtypeStruct((vec_count, row_count), F32),
            in_specs=[SMEM, SMEM, SMEM, full, full, tile_spec, whole((1, row_count))],
            out_specs=full,
            scratch_shapes=[split],
            compiler_params=params,
            cost_estimate=own_cost,
            name="own",
        )(place, tile_cols, field_levels, field, flipped, tiles, targets)

    def own_gram(field, flipped):
        return pl.pallas_call(
            own_gram_kernel,
            grid=(STEPS,),
            out_shape=jax.ShapeDtypeStruct((vec_count, 2 * vec_count), F32),
            in_specs=[SMEM, SMEM, SMEM, SMEM, full, full, tile_spec, whole((1, row_count))],
            out_specs=whole((vec_count, 2 * vec_count)),
            scratch_shapes=[split],
            compiler_params=params,
            cost_estimate=own_cost,
            name="own_gram",
        )(place, tile_cols, field_levels, live_rows, field, flipped, tiles, targets)

    rows = pl.BlockSpec((vec_count // STEPS, row_count), lambda step: (step, 0))
    half = pl.BlockSpec((vec_count // STEPS, row_count // 2), lambda step: (step, 0))

    def exchanged(field):
        flipped = exchange(field, 1)
        hops = [hop(field, bond) for bond in reversed(range(bonds))][::-1]
        return flipped, hops

    start = vectors * alive_of(live_rows, 0, row_count)
    flipped, hops = exchanged(start)
    own = own_part(start, flipped)
    first = pl.pallas_call(
        functools.partial(combine_kernel, bonds),
        grid=(STEPS,),
        out_shape=jax.ShapeDtypeStruct((vec_count, row_count), F32),
        in_specs=[SMEM, SMEM] + [rows] * (bonds + 1),
        out_specs=rows,
        compiler_params=params,
        name="combine",
    )(place, live_rows, own, *hops)
    flipped, hops = exchanged(first)
    own = own_part(first, flipped)
    second, sent = pl.pallas_call(
        functools.partial(filter_kernel, bonds),
        grid=(STEPS,),
        out_shape=[
            jax.ShapeDtypeStruct((vec_count, row_count), F32),
            jax.ShapeDtypeStruct((vec_count, row_count // 2), F32),
        ],
        in_specs=[SMEM, SMEM] + [rows] * (bonds + 2),
        out_specs=[rows, half],
        compiler_params=params,
        name="filter",
    )(place, live_rows, own, *hops, start)
    flipped = exchange(second, 1)
    hops = [hop(sent, bond) for bond in reversed(range(bonds))][::-1]
    grams = own_gram(second, flipped)
    sums = pl.pallas_call(
        functools.partial(crossed_kernel, bonds, dev_count * row_count),
        out_shape=jax.ShapeDtypeStruct((vec_count, 2 * vec_count), F32),
        in_specs=[SMEM] + [pl.BlockSpec(memory_space=pltpu.VMEM)] * (bonds + 2),
        out_specs=pl.BlockSpec(memory_space=pltpu.VMEM),
        compiler_params=params,
        name="crossed",
    )(place, grams, second, *hops)
    for digit in range(bonds + 1):
        sums = sums + exchange(sums, 1 << digit)
    return (second, sums[:, :vec_count], sums[:, vec_count:])


def solution(mesh):
    in_specs = (
        P(None, ("groups", "hi", "lo")),
        P(("groups", "hi", "lo"), None, None),
        P(("hi", "lo")),
        P(("hi", "lo")),
        P(("hi", "lo")),
        P("groups"),
    )
    out_specs = (P(None, ("groups", "hi", "lo")), P("groups", None), P("groups", None))
    return jax.shard_map(local, mesh=mesh, in_specs=in_specs, out_specs=out_specs, check_vma=False)
```

```python
import functools

import jax
import jax.numpy as jnp
from jax import lax
from jax.experimental import pallas as pl
from jax.experimental.pallas import tpu as pltpu
from jax.sharding import PartitionSpec as P

HOP_SCALE = 0.5
ANISOTROPY = 1.0
FIELD_STEP = 0.25
HALF_WIDTH = 4.0
AXES = ("hi", "lo")
STEPS = 4
F32, BF16 = jnp.float32, jnp.bfloat16
SMEM = pl.BlockSpec(memory_space=pltpu.SMEM)
LIMIT = 32 * 1024 * 1024


def bit(number, place):
    return (number >> place) & 1


def halves(value):
    head = value.astype(BF16)
    return head, (value - head.astype(F32)).astype(BF16)


def stacked(value):
    return jnp.concatenate(halves(value), axis=0)


def product(left, right):
    rows, columns = left.shape[0] // 2, right.shape[0] // 2
    whole = lax.dot_general(left, right, (((1,), (1,)), ((), ())), preferred_element_type=F32)
    tails = whole[:rows, columns:] + whole[rows:, :columns] + whole[rows:, columns:]
    return whole[:rows, :columns] + tails


def coupling(config, bond):
    differ = bit(config, bond) ^ bit(config, bond + 1)
    return jnp.where(differ == 1, HOP_SCALE, 0.0)


def onsite_of(config, fields_ref):
    count = fields_ref.shape[0]
    spins = [bit(config, place).astype(F32) - 0.5 for place in range(count)]
    total = jnp.float32(0.0)
    for place in range(count):
        total += fields_ref[place].astype(F32) * FIELD_STEP * spins[place]
    for place in range(count - 1):
        total += ANISOTROPY * spins[place] * spins[place + 1]
    return total


def alive_of(live_ref, first, count):
    rows = lax.broadcasted_iota(jnp.int32, (1, count), 1) + first
    return (rows < live_ref[0]).astype(F32)


def own_block(block, row, config, cols_ref, fields_ref, field_ref, split_ref, flipped_ref, tiles_ref, map_ref):
    per_block, tile = tiles_ref.shape[1], tiles_ref.shape[2]
    span = pl.ds(pl.multiple_of(block * tile, tile), tile)
    picked = []
    for which in range(per_block):
        column = cols_ref[block * per_block + which]
        picked.append(split_ref[:, pl.ds(pl.multiple_of(column * tile, tile), tile)])
    weights = jnp.concatenate([tiles_ref[row, which] for which in range(per_block)], axis=1)
    total = product(jnp.concatenate(picked, axis=1), stacked(weights))
    total += onsite_of(config, fields_ref) * field_ref[:, span]
    targets = jnp.broadcast_to(map_ref[:, span], (8, tile))
    inside, outside = targets & (tile - 1), targets // tile
    outside = jnp.where(targets < 0, -1, outside)
    groups = []
    for group in range(field_ref.shape[0] // 8):
        found = jnp.zeros((8, tile), F32)
        for source in range(field_ref.shape[1] // tile):
            values = flipped_ref[group * 8 : group * 8 + 8, source * tile : (source + 1) * tile]
            moved = jnp.take_along_axis(values, inside, axis=1)
            found = jnp.where(outside == source, moved, found)
        groups.append(found)
    return span, total + HOP_SCALE * jnp.concatenate(groups, axis=0)


def own_kernel(place_ref, cols_ref, fields_ref, field_ref, flipped_ref, tiles_ref, map_ref, out_ref, split_ref):
    step, blocks = pl.program_id(0), tiles_ref.shape[0]

    @pl.when(step == 0)
    def _():
        split_ref[...] = stacked(field_ref[...])

    for row in range(blocks):
        span, total = own_block(
            step * blocks + row, row, place_ref[0], cols_ref, fields_ref, field_ref, split_ref, flipped_ref, tiles_ref, map_ref
        )
        out_ref[:, span] = total


def own_gram_kernel(
    place_ref, cols_ref, fields_ref, live_ref, field_ref, flipped_ref, tiles_ref, map_ref, out_ref, split_ref
):
    step, blocks, tile = pl.program_id(0), tiles_ref.shape[0], tiles_ref.shape[2]
    count = field_ref.shape[0]

    @pl.when(step == 0)
    def _():
        split_ref[...] = stacked(field_ref[...])
        out_ref[:, :count] = product(split_ref[...], split_ref[...])
        out_ref[:, count:] = jnp.zeros((count, count), F32)

    parts = []
    for row in range(blocks):
        span, total = own_block(
            step * blocks + row, row, place_ref[0], cols_ref, fields_ref, field_ref, split_ref, flipped_ref, tiles_ref, map_ref
        )
        parts.append(alive_of(live_ref, (step * blocks + row) * tile, tile) * total)
    image = stacked(jnp.concatenate(parts, axis=1))
    width = blocks * tile
    out_ref[:, count:] += product(split_ref[:, pl.ds(pl.multiple_of(step * width, width), width)], image)


def combine_kernel(bonds, place_ref, which_ref, live_ref, own_ref, *refs):
    hops, out_ref = refs[:bonds], refs[-1]
    total = own_ref[...]
    for bond in range(bonds):
        total += coupling(place_ref[0], bond) * hops[bond][...]
    out_ref[...] = alive_of(live_ref, 0, total.shape[1]) * total * (1.0 / HALF_WIDTH)


def filter_kernel(bonds, place_ref, which_ref, live_ref, own_ref, *refs):
    hops, start_ref, out_ref, sent_ref = refs[:bonds], refs[bonds], refs[-2], refs[-1]
    total = own_ref[...]
    for bond in range(bonds):
        total += coupling(place_ref[0], bond) * hops[bond][...]
    image = alive_of(live_ref, 0, total.shape[1]) * total * (1.0 / HALF_WIDTH)
    second = 2.0 * image - start_ref[...]
    out_ref[...] = second
    width = sent_ref.shape[1]
    sent_ref[...] = jnp.where(place_ref[1] == 0, second[:, :width], second[:, width:])


def crossed_kernel(bonds, states, place_ref, which_ref, own_ref, field_ref, *refs):
    hops, out_ref = refs[:bonds], refs[-1]
    width, count = hops[0].shape[1], own_ref.shape[0]
    theirs = jnp.zeros((count, width), F32)
    for bond in range(bonds):
        theirs += coupling(place_ref[0], bond) * hops[bond][...]
    mine = jnp.where(place_ref[1] == 0, field_ref[:, width:], field_ref[:, :width])
    crossed = product(stacked(mine), stacked(theirs))
    out_ref[:, :count] = own_ref[:, :count] * (1.0 / states)
    projected = own_ref[:, count:] + crossed + crossed.T
    out_ref[:, count:] = projected * (1.0 / (HALF_WIDTH * states))


def local(vectors, tile_values, tile_cols, live_rows, boundary_map, field_levels):
    dev_count = lax.axis_size(AXES)
    bonds = dev_count.bit_length() - 2
    flip = (dev_count - 1) // 3
    position = lax.axis_index(AXES)
    parity = sum(bit(position, place) for place in range(0, bonds + 1, 2)) & 1
    place = jnp.stack([position ^ flip, parity]).astype(jnp.int32)
    which = jnp.stack([1 - bit(position, bond + 1) for bond in range(bonds)]).astype(jnp.int32)
    vec_count, row_count = vectors.shape
    tile_size = tile_values.shape[1]
    block_count = row_count // tile_size
    per_block = tile_values.shape[0] // block_count
    tiles = tile_values.reshape(block_count, per_block, tile_size, tile_size)
    targets = boundary_map.reshape(1, row_count)
    params = pltpu.CompilerParams(vmem_limit_bytes=LIMIT)

    def coupled(source, bond):
        return bit(source ^ flip, bond) != bit(source ^ flip, bond + 1)

    def hop(value, bond):
        if bond == 0:
            pairs = [(here, here ^ 3 if coupled(here, 0) else here) for here in range(dev_count)]
            return lax.ppermute(value, AXES, pairs)
        masks = [3 << bond if coupled(here, bond) else 1 for here in range(dev_count)]
        groups = [[here, here ^ mask] for here, mask in enumerate(masks) if here < here ^ mask]
        return lax.all_gather(value, AXES, axis_index_groups=groups, tiled=True)

    def exchange(value, mask):
        return lax.ppermute(value, AXES, [(source, source ^ mask) for source in range(dev_count)])

    def whole(shape):
        return pl.BlockSpec(shape, lambda *refs: (0,) * len(shape))

    full = whole((vec_count, row_count))
    tile_spec = pl.BlockSpec(
        (block_count // STEPS, per_block, tile_size, tile_size), lambda step: (step, 0, 0, 0)
    )
    own_cost = pl.CostEstimate(
        flops=8 * vec_count * row_count * per_block * tile_size,
        bytes_accessed=4 * tile_values.size + 12 * vec_count * row_count,
        transcendentals=0,
    )
    split = pltpu.VMEM((2 * vec_count, row_count), BF16)

    def own_part(field, flipped):
        return pl.pallas_call(
            own_kernel,
            grid=(STEPS,),
            out_shape=jax.ShapeDtypeStruct((vec_count, row_count), F32),
            in_specs=[SMEM, SMEM, SMEM, full, full, tile_spec, whole((1, row_count))],
            out_specs=full,
            scratch_shapes=[split],
            compiler_params=params,
            cost_estimate=own_cost,
            name="own",
        )(place, tile_cols, field_levels, field, flipped, tiles, targets)

    def own_gram(field, flipped):
        return pl.pallas_call(
            own_gram_kernel,
            grid=(STEPS,),
            out_shape=jax.ShapeDtypeStruct((vec_count, 2 * vec_count), F32),
            in_specs=[SMEM, SMEM, SMEM, SMEM, full, full, tile_spec, whole((1, row_count))],
            out_specs=whole((vec_count, 2 * vec_count)),
            scratch_shapes=[split],
            compiler_params=params,
            cost_estimate=own_cost,
            name="own_gram",
        )(place, tile_cols, field_levels, live_rows, field, flipped, tiles, targets)

    rows = pl.BlockSpec((vec_count // STEPS, row_count), lambda step, *refs: (step, 0))
    half = pl.BlockSpec((vec_count // STEPS, row_count // 2), lambda step, *refs: (step, 0))

    def hop_specs(steps, width):
        shape = (vec_count // steps, width)
        far = [
            pl.BlockSpec(shape, lambda step, place, which, bond=bond: (which[bond] * steps + step, 0))
            for bond in range(1, bonds)
        ]
        return [pl.BlockSpec(shape, lambda step, *refs: (step, 0))] + far

    def exchanged(field):
        flipped = exchange(field, 1)
        hops = [hop(field, bond) for bond in reversed(range(bonds))][::-1]
        return flipped, hops

    start = vectors * alive_of(live_rows, 0, row_count)
    flipped, hops = exchanged(start)
    own = own_part(start, flipped)
    first = pl.pallas_call(
        functools.partial(combine_kernel, bonds),
        out_shape=jax.ShapeDtypeStruct((vec_count, row_count), F32),
        grid_spec=pltpu.PrefetchScalarGridSpec(
            num_scalar_prefetch=2,
            grid=(STEPS,),
            in_specs=[SMEM, rows] + hop_specs(STEPS, row_count),
            out_specs=rows,
        ),
        compiler_params=params,
        name="combine",
    )(place, which, live_rows, own, *hops)
    flipped, hops = exchanged(first)
    own = own_part(first, flipped)
    second, sent = pl.pallas_call(
        functools.partial(filter_kernel, bonds),
        out_shape=[
            jax.ShapeDtypeStruct((vec_count, row_count), F32),
            jax.ShapeDtypeStruct((vec_count, row_count // 2), F32),
        ],
        grid_spec=pltpu.PrefetchScalarGridSpec(
            num_scalar_prefetch=2,
            grid=(STEPS,),
            in_specs=[SMEM, rows] + hop_specs(STEPS, row_count) + [rows],
            out_specs=[rows, half],
        ),
        compiler_params=params,
        name="filter",
    )(place, which, live_rows, own, *hops, start)
    flipped = exchange(second, 1)
    hops = [hop(sent, bond) for bond in reversed(range(bonds))][::-1]
    grams = own_gram(second, flipped)
    sums = pl.pallas_call(
        functools.partial(crossed_kernel, bonds, dev_count * row_count),
        out_shape=jax.ShapeDtypeStruct((vec_count, 2 * vec_count), F32),
        grid_spec=pltpu.PrefetchScalarGridSpec(
            num_scalar_prefetch=2,
            grid=(1,),
            in_specs=[whole((vec_count, 2 * vec_count)), full] + hop_specs(1, row_count // 2),
            out_specs=whole((vec_count, 2 * vec_count)),
        ),
        compiler_params=params,
        name="crossed",
    )(place, which, grams, second, *hops)
    for digit in range(bonds + 1):
        sums = sums + exchange(sums, 1 << digit)
    return (second, sums[:, :vec_count], sums[:, vec_count:])


def solution(mesh):
    in_specs = (
        P(None, ("groups", "hi", "lo")),
        P(("groups", "hi", "lo"), None, None),
        P(("hi", "lo")),
        P(("hi", "lo")),
        P(("hi", "lo")),
        P("groups"),
    )
    out_specs = (P(None, ("groups", "hi", "lo")), P("groups", None), P("groups", None))
    return jax.shard_map(local, mesh=mesh, in_specs=in_specs, out_specs=out_specs, check_vma=False)
```

```python
import functools

import jax
import jax.numpy as jnp
from jax import lax
from jax.experimental import pallas as pl
from jax.experimental.pallas import tpu as pltpu
from jax.sharding import PartitionSpec as P

HOP_SCALE = 0.5
ANISOTROPY = 1.0
FIELD_STEP = 0.25
HALF_WIDTH = 4.0
AXES = ("hi", "lo")
STEPS = 4
F32, BF16 = jnp.float32, jnp.bfloat16
SMEM = pl.BlockSpec(memory_space=pltpu.SMEM)
LIMIT = 32 * 1024 * 1024


def bit(number, place):
    return (number >> place) & 1


def halves(value):
    head = value.astype(BF16)
    return head, (value - head.astype(F32)).astype(BF16)


def stacked(value):
    return jnp.concatenate(halves(value), axis=0)


def product(left, right):
    rows, columns = left.shape[0] // 2, right.shape[0] // 2
    whole = lax.dot_general(left, right, (((1,), (1,)), ((), ())), preferred_element_type=F32)
    tails = whole[:rows, columns:] + whole[rows:, :columns] + whole[rows:, columns:]
    return whole[:rows, :columns] + tails


def coupling(config, bond):
    differ = bit(config, bond) ^ bit(config, bond + 1)
    return jnp.where(differ == 1, HOP_SCALE, 0.0)


def onsite_of(config, fields_ref):
    count = fields_ref.shape[0]
    spins = [bit(config, place).astype(F32) - 0.5 for place in range(count)]
    total = jnp.float32(0.0)
    for place in range(count):
        total += fields_ref[place].astype(F32) * FIELD_STEP * spins[place]
    for place in range(count - 1):
        total += ANISOTROPY * spins[place] * spins[place + 1]
    return total


def alive_of(live_ref, first, count):
    rows = lax.broadcasted_iota(jnp.int32, (1, count), 1) + first
    return (rows < live_ref[0]).astype(F32)


def own_block(block, row, config, cols_ref, fields_ref, field_ref, split_ref, flipped_ref, tiles_ref, map_ref):
    per_block, tile = tiles_ref.shape[1], tiles_ref.shape[2]
    span = pl.ds(pl.multiple_of(block * tile, tile), tile)
    picked = []
    for which in range(per_block):
        column = cols_ref[block * per_block + which]
        picked.append(split_ref[:, pl.ds(pl.multiple_of(column * tile, tile), tile)])
    weights = jnp.concatenate([tiles_ref[row, which] for which in range(per_block)], axis=1)
    total = product(jnp.concatenate(picked, axis=1), stacked(weights))
    total += onsite_of(config, fields_ref) * field_ref[:, span]
    targets = jnp.broadcast_to(map_ref[:, span], (8, tile))
    inside, outside = targets & (tile - 1), targets // tile
    outside = jnp.where(targets < 0, -1, outside)
    groups = []
    for group in range(field_ref.shape[0] // 8):
        found = jnp.zeros((8, tile), F32)
        for source in range(field_ref.shape[1] // tile):
            values = flipped_ref[group * 8 : group * 8 + 8, source * tile : (source + 1) * tile]
            moved = jnp.take_along_axis(values, inside, axis=1)
            found = jnp.where(outside == source, moved, found)
        groups.append(found)
    return span, total + HOP_SCALE * jnp.concatenate(groups, axis=0)


def own_kernel(place_ref, cols_ref, fields_ref, field_ref, flipped_ref, tiles_ref, map_ref, out_ref, split_ref):
    step, blocks = pl.program_id(0), tiles_ref.shape[0]

    @pl.when(step == 0)
    def _():
        split_ref[...] = stacked(field_ref[...])

    for row in range(blocks):
        span, total = own_block(
            step * blocks + row, row, place_ref[0], cols_ref, fields_ref, field_ref, split_ref, flipped_ref, tiles_ref, map_ref
        )
        out_ref[:, span] = total


def own_gram_kernel(
    place_ref, cols_ref, fields_ref, live_ref, field_ref, flipped_ref, tiles_ref, map_ref, out_ref, split_ref
):
    step, blocks, tile = pl.program_id(0), tiles_ref.shape[0], tiles_ref.shape[2]
    count = field_ref.shape[0]

    @pl.when(step == 0)
    def _():
        split_ref[...] = stacked(field_ref[...])
        out_ref[:, :count] = product(split_ref[...], split_ref[...])
        out_ref[:, count:] = jnp.zeros((count, count), F32)

    parts = []
    for row in range(blocks):
        span, total = own_block(
            step * blocks + row, row, place_ref[0], cols_ref, fields_ref, field_ref, split_ref, flipped_ref, tiles_ref, map_ref
        )
        parts.append(alive_of(live_ref, (step * blocks + row) * tile, tile) * total)
    image = stacked(jnp.concatenate(parts, axis=1))
    width = blocks * tile
    out_ref[:, count:] += product(split_ref[:, pl.ds(pl.multiple_of(step * width, width), width)], image)


def combine_kernel(bonds, place_ref, live_ref, own_ref, *refs):
    hops, out_ref = refs[:bonds], refs[-1]
    total = own_ref[...]
    for bond, hop in zip(reversed(range(bonds)), hops):
        total += coupling(place_ref[0], bond) * hop[...]
    out_ref[...] = alive_of(live_ref, 0, total.shape[1]) * total * (1.0 / HALF_WIDTH)


def filter_kernel(bonds, place_ref, live_ref, own_ref, *refs):
    hops, start_ref, out_ref, sent_ref = refs[:bonds], refs[bonds], refs[-2], refs[-1]
    total = own_ref[...]
    for bond, hop in zip(reversed(range(bonds)), hops):
        total += coupling(place_ref[0], bond) * hop[...]
    image = alive_of(live_ref, 0, total.shape[1]) * total * (1.0 / HALF_WIDTH)
    second = 2.0 * image - start_ref[...]
    out_ref[...] = second
    width = sent_ref.shape[1]
    sent_ref[...] = jnp.where(place_ref[1] == 0, second[:, :width], second[:, width:])


def crossed_kernel(bonds, states, place_ref, own_ref, field_ref, *refs):
    hops, out_ref = refs[:bonds], refs[-1]
    width, count = hops[0].shape[1], own_ref.shape[0]
    theirs = jnp.zeros((count, width), F32)
    for bond, hop in zip((0, *reversed(range(1, bonds))), hops):
        theirs += coupling(place_ref[0], bond) * hop[...]
    mine = jnp.where(place_ref[1] == 0, field_ref[:, width:], field_ref[:, :width])
    crossed = product(stacked(mine), stacked(theirs))
    out_ref[:, :count] = own_ref[:, :count] * (1.0 / states)
    projected = own_ref[:, count:] + crossed + crossed.T
    out_ref[:, count:] = projected * (1.0 / (HALF_WIDTH * states))


def local(vectors, tile_values, tile_cols, live_rows, boundary_map, field_levels):
    dev_count = lax.axis_size(AXES)
    bonds = dev_count.bit_length() - 2
    flip = (dev_count - 1) // 3
    position = lax.axis_index(AXES)
    parity = sum(bit(position, place) for place in range(0, bonds + 1, 2)) & 1
    place = jnp.stack([position ^ flip, parity]).astype(jnp.int32)
    vec_count, row_count = vectors.shape
    tile_size = tile_values.shape[1]
    block_count = row_count // tile_size
    per_block = tile_values.shape[0] // block_count
    tiles = tile_values.reshape(block_count, per_block, tile_size, tile_size)
    targets = boundary_map.reshape(1, row_count)
    params = pltpu.CompilerParams(vmem_limit_bytes=LIMIT)

    def hop(value, bond):
        pairs = [
            (source, source ^ (3 << bond))
            if bit(source ^ flip, bond) != bit(source ^ flip, bond + 1)
            else (source, source)
            for source in range(dev_count)
        ]
        return lax.ppermute(value, AXES, pairs)

    def exchange(value, mask):
        return lax.ppermute(value, AXES, [(source, source ^ mask) for source in range(dev_count)])

    def whole(shape):
        return pl.BlockSpec(shape, lambda step: (0,) * len(shape))

    full = whole((vec_count, row_count))
    tile_spec = pl.BlockSpec(
        (block_count // STEPS, per_block, tile_size, tile_size), lambda step: (step, 0, 0, 0)
    )
    own_cost = pl.CostEstimate(
        flops=8 * vec_count * row_count * per_block * tile_size,
        bytes_accessed=4 * tile_values.size + 12 * vec_count * row_count,
        transcendentals=0,
    )
    split = pltpu.VMEM((2 * vec_count, row_count), BF16)

    def own_part(field, flipped):
        return pl.pallas_call(
            own_kernel,
            grid=(STEPS,),
            out_shape=jax.ShapeDtypeStruct((vec_count, row_count), F32),
            in_specs=[SMEM, SMEM, SMEM, full, full, tile_spec, whole((1, row_count))],
            out_specs=full,
            scratch_shapes=[split],
            compiler_params=params,
            cost_estimate=own_cost,
            name="own",
        )(place, tile_cols, field_levels, field, flipped, tiles, targets)

    def own_gram(field, flipped):
        return pl.pallas_call(
            own_gram_kernel,
            grid=(STEPS,),
            out_shape=jax.ShapeDtypeStruct((vec_count, 2 * vec_count), F32),
            in_specs=[SMEM, SMEM, SMEM, SMEM, full, full, tile_spec, whole((1, row_count))],
            out_specs=whole((vec_count, 2 * vec_count)),
            scratch_shapes=[split],
            compiler_params=params,
            cost_estimate=own_cost,
            name="own_gram",
        )(place, tile_cols, field_levels, live_rows, field, flipped, tiles, targets)

    rows = pl.BlockSpec((vec_count // STEPS, row_count), lambda step: (step, 0))
    half = pl.BlockSpec((vec_count // STEPS, row_count // 2), lambda step: (step, 0))

    def exchanged(field):
        flipped = exchange(field, 1)
        hops = [hop(field, bond) for bond in reversed(range(bonds))]
        return flipped, hops

    start = vectors * alive_of(live_rows, 0, row_count)
    flipped, hops = exchanged(start)
    own = own_part(start, flipped)
    first = pl.pallas_call(
        functools.partial(combine_kernel, bonds),
        grid=(STEPS,),
        out_shape=jax.ShapeDtypeStruct((vec_count, row_count), F32),
        in_specs=[SMEM, SMEM] + [rows] * (bonds + 1),
        out_specs=rows,
        compiler_params=params,
        name="combine",
    )(place, live_rows, own, *hops)
    flipped, hops = exchanged(first)
    own = own_part(first, flipped)
    second, sent = pl.pallas_call(
        functools.partial(filter_kernel, bonds),
        grid=(STEPS,),
        out_shape=[
            jax.ShapeDtypeStruct((vec_count, row_count), F32),
            jax.ShapeDtypeStruct((vec_count, row_count // 2), F32),
        ],
        in_specs=[SMEM, SMEM] + [rows] * (bonds + 2),
        out_specs=[rows, half],
        compiler_params=params,
        name="filter",
    )(place, live_rows, own, *hops, start)
    flipped = exchange(second, 1)
    hops = [hop(sent, bond) for bond in (0, *reversed(range(1, bonds)))]
    grams = own_gram(second, flipped)
    sums = pl.pallas_call(
        functools.partial(crossed_kernel, bonds, dev_count * row_count),
        out_shape=jax.ShapeDtypeStruct((vec_count, 2 * vec_count), F32),
        in_specs=[SMEM] + [pl.BlockSpec(memory_space=pltpu.VMEM)] * (bonds + 2),
        out_specs=pl.BlockSpec(memory_space=pltpu.VMEM),
        compiler_params=params,
        name="crossed",
    )(place, grams, second, *hops)
    for digit in range(bonds + 1):
        sums = sums + exchange(sums, 1 << digit)
    return (second, sums[:, :vec_count], sums[:, vec_count:])


def solution(mesh):
    in_specs = (
        P(None, ("groups", "hi", "lo")),
        P(("groups", "hi", "lo"), None, None),
        P(("hi", "lo")),
        P(("hi", "lo")),
        P(("hi", "lo")),
        P("groups"),
    )
    out_specs = (P(None, ("groups", "hi", "lo")), P("groups", None), P("groups", None))
    return jax.shard_map(local, mesh=mesh, in_specs=in_specs, out_specs=out_specs, check_vma=False)
```

```python
import functools

import jax
import jax.numpy as jnp
from jax import lax
from jax.experimental import pallas as pl
from jax.experimental.pallas import tpu as pltpu
from jax.sharding import PartitionSpec as P

HOP_SCALE = 0.5
ANISOTROPY = 1.0
FIELD_STEP = 0.25
HALF_WIDTH = 4.0
AXES = ("hi", "lo")
STEPS = 4
F32, BF16 = jnp.float32, jnp.bfloat16
SMEM = pl.BlockSpec(memory_space=pltpu.SMEM)
LIMIT = 32 * 1024 * 1024


def bit(number, place):
    return (number >> place) & 1


def halves(value):
    head = value.astype(BF16)
    return head, (value - head.astype(F32)).astype(BF16)


def stacked(value):
    return jnp.concatenate(halves(value), axis=0)


def product(left, right):
    rows, columns = left.shape[0] // 2, right.shape[0] // 2
    whole = lax.dot_general(left, right, (((1,), (1,)), ((), ())), preferred_element_type=F32)
    tails = whole[:rows, columns:] + whole[rows:, :columns] + whole[rows:, columns:]
    return whole[:rows, :columns] + tails


def coupling(config, bond):
    differ = bit(config, bond) ^ bit(config, bond + 1)
    return jnp.where(differ == 1, HOP_SCALE, 0.0)


def onsite_of(config, fields_ref):
    count = fields_ref.shape[0]
    spins = [bit(config, place).astype(F32) - 0.5 for place in range(count)]
    total = jnp.float32(0.0)
    for place in range(count):
        total += fields_ref[place].astype(F32) * FIELD_STEP * spins[place]
    for place in range(count - 1):
        total += ANISOTROPY * spins[place] * spins[place + 1]
    return total


def alive_of(live_ref, first, count):
    rows = lax.broadcasted_iota(jnp.int32, (1, count), 1) + first
    return (rows < live_ref[0]).astype(F32)


def own_block(block, row, config, cols_ref, fields_ref, field_ref, split_ref, flipped_ref, tiles_ref, map_ref):
    per_block, tile = tiles_ref.shape[1], tiles_ref.shape[2]
    span = pl.ds(pl.multiple_of(block * tile, tile), tile)
    picked = []
    for which in range(per_block):
        column = cols_ref[block * per_block + which]
        picked.append(split_ref[:, pl.ds(pl.multiple_of(column * tile, tile), tile)])
    weights = jnp.concatenate([tiles_ref[row, which] for which in range(per_block)], axis=1)
    total = product(jnp.concatenate(picked, axis=1), stacked(weights))
    total += onsite_of(config, fields_ref) * field_ref[:, span]
    targets = jnp.broadcast_to(map_ref[:, span], (8, tile))
    inside, outside = targets & (tile - 1), targets // tile
    outside = jnp.where(targets < 0, -1, outside)
    groups = []
    for group in range(field_ref.shape[0] // 8):
        found = jnp.zeros((8, tile), F32)
        for source in range(field_ref.shape[1] // tile):
            values = flipped_ref[group * 8 : group * 8 + 8, source * tile : (source + 1) * tile]
            moved = jnp.take_along_axis(values, inside, axis=1)
            found = jnp.where(outside == source, moved, found)
        groups.append(found)
    return span, total + HOP_SCALE * jnp.concatenate(groups, axis=0)


def own_kernel(place_ref, cols_ref, fields_ref, field_ref, flipped_ref, tiles_ref, map_ref, out_ref, split_ref):
    step, blocks = pl.program_id(0), tiles_ref.shape[0]

    @pl.when(step == 0)
    def _():
        split_ref[...] = stacked(field_ref[...])

    for row in range(blocks):
        span, total = own_block(
            step * blocks + row, row, place_ref[0], cols_ref, fields_ref, field_ref, split_ref, flipped_ref, tiles_ref, map_ref
        )
        out_ref[:, span] = total


def own_gram_kernel(
    place_ref, cols_ref, fields_ref, live_ref, field_ref, flipped_ref, tiles_ref, map_ref, out_ref, split_ref
):
    step, blocks, tile = pl.program_id(0), tiles_ref.shape[0], tiles_ref.shape[2]
    count = field_ref.shape[0]

    @pl.when(step == 0)
    def _():
        split_ref[...] = stacked(field_ref[...])
        out_ref[:, :count] = product(split_ref[...], split_ref[...])
        out_ref[:, count:] = jnp.zeros((count, count), F32)

    parts = []
    for row in range(blocks):
        span, total = own_block(
            step * blocks + row, row, place_ref[0], cols_ref, fields_ref, field_ref, split_ref, flipped_ref, tiles_ref, map_ref
        )
        parts.append(alive_of(live_ref, (step * blocks + row) * tile, tile) * total)
    image = stacked(jnp.concatenate(parts, axis=1))
    width = blocks * tile
    out_ref[:, count:] += product(split_ref[:, pl.ds(pl.multiple_of(step * width, width), width)], image)


def hop_sum(bonds, config, refs, upper):
    total = coupling(config, 0) * refs[-1][...]
    if bonds > 1:
        total += coupling(config, 1) * upper(refs[-3][...], refs[-2][...])
    for bond, ref in zip(reversed(range(2, bonds)), refs):
        total += coupling(config, bond) * ref[...]
    return total


def step_half(first, second):
    return jnp.where(pl.program_id(0) < pl.num_programs(0) // 2, first, second)


def start_kernel(live_ref, vectors_ref, out_ref, first_ref, second_ref):
    start = vectors_ref[...] * alive_of(live_ref, 0, vectors_ref.shape[1])
    out_ref[...] = start
    store_halves(start, first_ref, second_ref)


def store_halves(value, first_ref, second_ref):
    in_first = pl.program_id(0) < pl.num_programs(0) // 2

    @pl.when(in_first)
    def _():
        first_ref[...] = value

    @pl.when(jnp.logical_not(in_first))
    def _():
        second_ref[...] = value


def combine_kernel(bonds, place_ref, live_ref, own_ref, *refs):
    hops, (out_ref, first_ref, second_ref) = refs[:-3], refs[-3:]
    total = own_ref[...] + hop_sum(bonds, place_ref[0], hops, step_half)
    result = alive_of(live_ref, 0, total.shape[1]) * total * (1.0 / HALF_WIDTH)
    out_ref[...] = result
    store_halves(result, first_ref, second_ref)


def filter_kernel(bonds, place_ref, live_ref, own_ref, start_ref, *refs):
    hops, (out_ref, sent_ref, first_ref, second_ref) = refs[:-4], refs[-4:]
    total = own_ref[...] + hop_sum(bonds, place_ref[0], hops, step_half)
    image = alive_of(live_ref, 0, total.shape[1]) * total * (1.0 / HALF_WIDTH)
    second = 2.0 * image - start_ref[...]
    out_ref[...] = second
    width = sent_ref.shape[1]
    sent = jnp.where(place_ref[1] == 0, second[:, :width], second[:, width:])
    sent_ref[...] = sent
    store_halves(sent, first_ref, second_ref)


def crossed_kernel(bonds, states, place_ref, own_ref, field_ref, *refs):
    hops, out_ref = refs[:-1], refs[-1]
    width, count = hops[-1].shape[1], own_ref.shape[0]
    theirs = hop_sum(bonds, place_ref[0], hops, lambda first, second: jnp.concatenate([first, second], axis=0))
    mine = jnp.where(place_ref[1] == 0, field_ref[:, width:], field_ref[:, :width])
    crossed = product(stacked(mine), stacked(theirs))
    out_ref[:, :count] = own_ref[:, :count] * (1.0 / states)
    projected = own_ref[:, count:] + crossed + crossed.T
    out_ref[:, count:] = projected * (1.0 / (HALF_WIDTH * states))


def local(vectors, tile_values, tile_cols, live_rows, boundary_map, field_levels):
    dev_count = lax.axis_size(AXES)
    bonds = dev_count.bit_length() - 2
    flip = (dev_count - 1) // 3
    position = lax.axis_index(AXES)
    parity = sum(bit(position, place) for place in range(0, bonds + 1, 2)) & 1
    place = jnp.stack([position ^ flip, parity]).astype(jnp.int32)
    vec_count, row_count = vectors.shape
    tile_size = tile_values.shape[1]
    block_count = row_count // tile_size
    per_block = tile_values.shape[0] // block_count
    tiles = tile_values.reshape(block_count, per_block, tile_size, tile_size)
    targets = boundary_map.reshape(1, row_count)
    params = pltpu.CompilerParams(vmem_limit_bytes=LIMIT)

    def coupled(here, bond):
        return bit(here ^ flip, bond) != bit(here ^ flip, bond + 1)

    def hop(value, bond):
        pairs = [(here, here ^ (3 << bond) if coupled(here, bond) else here) for here in range(dev_count)]
        return lax.ppermute(value, AXES, pairs)

    def near(flipped):
        pairs = [(here, here ^ (1 if coupled(here, 0) else 2)) for here in range(dev_count)]
        return lax.ppermute(flipped, AXES, pairs)

    def around(value):
        pairs = [(here, here ^ (4 if coupled(here, 1) else 2)) for here in range(dev_count)]
        return exchange(lax.ppermute(value, AXES, pairs), 2)

    def exchange(value, mask):
        return lax.ppermute(value, AXES, [(source, source ^ mask) for source in range(dev_count)])

    def whole(shape):
        return pl.BlockSpec(shape, lambda step: (0,) * len(shape))

    full = whole((vec_count, row_count))
    tile_spec = pl.BlockSpec(
        (block_count // STEPS, per_block, tile_size, tile_size), lambda step: (step, 0, 0, 0)
    )
    own_cost = pl.CostEstimate(
        flops=8 * vec_count * row_count * per_block * tile_size,
        bytes_accessed=4 * tile_values.size + 12 * vec_count * row_count,
        transcendentals=0,
    )
    split = pltpu.VMEM((2 * vec_count, row_count), BF16)

    def own_part(field, flipped):
        return pl.pallas_call(
            own_kernel,
            grid=(STEPS,),
            out_shape=jax.ShapeDtypeStruct((vec_count, row_count), F32),
            in_specs=[SMEM, SMEM, SMEM, full, full, tile_spec, whole((1, row_count))],
            out_specs=full,
            scratch_shapes=[split],
            compiler_params=params,
            cost_estimate=own_cost,
            name="own",
        )(place, tile_cols, field_levels, field, flipped, tiles, targets)

    def own_gram(field, flipped):
        return pl.pallas_call(
            own_gram_kernel,
            grid=(STEPS,),
            out_shape=jax.ShapeDtypeStruct((vec_count, 2 * vec_count), F32),
            in_specs=[SMEM, SMEM, SMEM, SMEM, full, full, tile_spec, whole((1, row_count))],
            out_specs=whole((vec_count, 2 * vec_count)),
            scratch_shapes=[split],
            compiler_params=params,
            cost_estimate=own_cost,
            name="own_gram",
        )(place, tile_cols, field_levels, live_rows, field, flipped, tiles, targets)

    def row_specs(width):
        shape, middle = (vec_count // STEPS, width), STEPS // 2
        return (
            pl.BlockSpec(shape, lambda step: (step, 0)),
            pl.BlockSpec(shape, lambda step: (jnp.minimum(step, middle - 1), 0)),
            pl.BlockSpec(shape, lambda step: (jnp.maximum(step - middle, 0), 0)),
        )

    def row_shapes(width):
        whole_shape = jax.ShapeDtypeStruct((vec_count, width), F32)
        half_shape = jax.ShapeDtypeStruct((vec_count // 2, width), F32)
        return [whole_shape, half_shape, half_shape]

    rows, first_rows, second_rows = row_specs(row_count)
    hop_specs = [rows] * (bonds - 2) + [first_rows, second_rows] + [rows]

    def exchanged(field, first_half, second_half, closest):
        far = [hop(field, bond) for bond in reversed(range(2, bonds))]
        return far + [hop(first_half, 1), around(second_half), closest]

    start, *halves_of = pl.pallas_call(
        start_kernel,
        grid=(STEPS,),
        out_shape=row_shapes(row_count),
        in_specs=[SMEM, rows],
        out_specs=[rows, first_rows, second_rows],
        compiler_params=params,
        name="start",
    )(live_rows, vectors)
    flipped = exchange(start, 1)
    hops = exchanged(start, *halves_of, near(flipped))
    own = own_part(start, flipped)
    first, *halves_of = pl.pallas_call(
        functools.partial(combine_kernel, bonds),
        grid=(STEPS,),
        out_shape=row_shapes(row_count),
        in_specs=[SMEM, SMEM, rows] + hop_specs,
        out_specs=[rows, first_rows, second_rows],
        compiler_params=params,
        name="combine",
    )(place, live_rows, own, *hops)
    flipped = exchange(first, 1)
    hops = exchanged(first, *halves_of, near(flipped))
    own = own_part(first, flipped)
    second, sent, *halves_of = pl.pallas_call(
        functools.partial(filter_kernel, bonds),
        grid=(STEPS,),
        out_shape=row_shapes(row_count)[:1] + row_shapes(row_count // 2),
        in_specs=[SMEM, SMEM, rows, rows] + hop_specs,
        out_specs=[rows, *row_specs(row_count // 2)],
        compiler_params=params,
        name="filter",
    )(place, live_rows, own, start, *hops)
    flipped = exchange(second, 1)
    hops = exchanged(sent, *halves_of, hop(sent, 0))
    grams = own_gram(second, flipped)
    sums = pl.pallas_call(
        functools.partial(crossed_kernel, bonds, dev_count * row_count),
        out_shape=jax.ShapeDtypeStruct((vec_count, 2 * vec_count), F32),
        in_specs=[SMEM] + [pl.BlockSpec(memory_space=pltpu.VMEM)] * (bonds + 3),
        out_specs=pl.BlockSpec(memory_space=pltpu.VMEM),
        compiler_params=params,
        name="crossed",
    )(place, grams, second, *hops)
    for digit in range(bonds + 1):
        sums = sums + exchange(sums, 1 << digit)
    return (second, sums[:, :vec_count], sums[:, vec_count:])


def solution(mesh):
    in_specs = (
        P(None, ("groups", "hi", "lo")),
        P(("groups", "hi", "lo"), None, None),
        P(("hi", "lo")),
        P(("hi", "lo")),
        P(("hi", "lo")),
        P("groups"),
    )
    out_specs = (P(None, ("groups", "hi", "lo")), P("groups", None), P("groups", None))
    return jax.shard_map(local, mesh=mesh, in_specs=in_specs, out_specs=out_specs, check_vma=False)
```

```python
import functools

import jax
import jax.numpy as jnp
from jax import lax
from jax.experimental import pallas as pl
from jax.experimental.pallas import tpu as pltpu
from jax.sharding import PartitionSpec as P

HOP_SCALE = 0.5
ANISOTROPY = 1.0
FIELD_STEP = 0.25
HALF_WIDTH = 4.0
AXES = ("hi", "lo")
STEPS = 4
F32, BF16 = jnp.float32, jnp.bfloat16
SMEM = pl.BlockSpec(memory_space=pltpu.SMEM)
LIMIT = 32 * 1024 * 1024


def bit(number, place):
    return (number >> place) & 1


def halves(value):
    head = value.astype(BF16)
    return head, (value - head.astype(F32)).astype(BF16)


def stacked(value):
    return jnp.concatenate(halves(value), axis=0)


def product(left, right):
    rows, columns = left.shape[0] // 2, right.shape[0] // 2
    whole = lax.dot_general(left, right, (((1,), (1,)), ((), ())), preferred_element_type=F32)
    tails = whole[:rows, columns:] + whole[rows:, :columns] + whole[rows:, columns:]
    return whole[:rows, :columns] + tails


def coupling(config, bond):
    differ = bit(config, bond) ^ bit(config, bond + 1)
    return jnp.where(differ == 1, HOP_SCALE, 0.0)


def onsite_of(config, fields_ref):
    count = fields_ref.shape[0]
    spins = [bit(config, place).astype(F32) - 0.5 for place in range(count)]
    total = jnp.float32(0.0)
    for place in range(count):
        total += fields_ref[place].astype(F32) * FIELD_STEP * spins[place]
    for place in range(count - 1):
        total += ANISOTROPY * spins[place] * spins[place + 1]
    return total


def alive_of(live_ref, first, count):
    rows = lax.broadcasted_iota(jnp.int32, (1, count), 1) + first
    return (rows < live_ref[0]).astype(F32)


def own_block(block, row, config, cols_ref, fields_ref, field_ref, split_ref, flipped_ref, tiles_ref, map_ref):
    per_block, tile = tiles_ref.shape[1], tiles_ref.shape[2]
    span = pl.ds(pl.multiple_of(block * tile, tile), tile)
    picked = []
    for which in range(per_block):
        column = cols_ref[block * per_block + which]
        picked.append(split_ref[:, pl.ds(pl.multiple_of(column * tile, tile), tile)])
    weights = jnp.concatenate([tiles_ref[row, which] for which in range(per_block)], axis=1)
    total = product(jnp.concatenate(picked, axis=1), stacked(weights))
    total += onsite_of(config, fields_ref) * field_ref[:, span]
    targets = jnp.broadcast_to(map_ref[:, span], (8, tile))
    inside, outside = targets & (tile - 1), targets // tile
    outside = jnp.where(targets < 0, -1, outside)
    groups = []
    for group in range(field_ref.shape[0] // 8):
        found = jnp.zeros((8, tile), F32)
        for source in range(field_ref.shape[1] // tile):
            values = flipped_ref[group * 8 : group * 8 + 8, source * tile : (source + 1) * tile]
            moved = jnp.take_along_axis(values, inside, axis=1)
            found = jnp.where(outside == source, moved, found)
        groups.append(found)
    return span, total + HOP_SCALE * jnp.concatenate(groups, axis=0)


def own_kernel(place_ref, cols_ref, fields_ref, field_ref, flipped_ref, tiles_ref, map_ref, out_ref, split_ref):
    step, blocks = pl.program_id(0), tiles_ref.shape[0]

    @pl.when(step == 0)
    def _():
        split_ref[...] = stacked(field_ref[...])

    for row in range(blocks):
        span, total = own_block(
            step * blocks + row, row, place_ref[0], cols_ref, fields_ref, field_ref, split_ref, flipped_ref, tiles_ref, map_ref
        )
        out_ref[:, span] = total


def own_gram_kernel(
    place_ref, cols_ref, fields_ref, live_ref, field_ref, flipped_ref, tiles_ref, map_ref, out_ref, split_ref
):
    step, blocks, tile = pl.program_id(0), tiles_ref.shape[0], tiles_ref.shape[2]
    count = field_ref.shape[0]

    @pl.when(step == 0)
    def _():
        split_ref[...] = stacked(field_ref[...])
        out_ref[:, :count] = product(split_ref[...], split_ref[...])
        out_ref[:, count:] = jnp.zeros((count, count), F32)

    parts = []
    for row in range(blocks):
        span, total = own_block(
            step * blocks + row, row, place_ref[0], cols_ref, fields_ref, field_ref, split_ref, flipped_ref, tiles_ref, map_ref
        )
        parts.append(alive_of(live_ref, (step * blocks + row) * tile, tile) * total)
    image = stacked(jnp.concatenate(parts, axis=1))
    width = blocks * tile
    out_ref[:, count:] += product(split_ref[:, pl.ds(pl.multiple_of(step * width, width), width)], image)


def hop_sum(bonds, config, refs, upper):
    total = coupling(config, 0) * refs[-1][...]
    if bonds > 1:
        total += coupling(config, 1) * upper(refs[-3][...], refs[-2][...])
    for bond, ref in zip(reversed(range(2, bonds)), refs):
        total += coupling(config, bond) * ref[...]
    return total


def step_half(first, second):
    return jnp.where(pl.program_id(0) < pl.num_programs(0) // 2, first, second)


def start_kernel(live_ref, vectors_ref, out_ref, first_ref, second_ref):
    start = vectors_ref[...] * alive_of(live_ref, 0, vectors_ref.shape[1])
    out_ref[...] = start
    store_halves(start, first_ref, second_ref)


def store_halves(value, first_ref, second_ref):
    in_first = pl.program_id(0) < pl.num_programs(0) // 2

    @pl.when(in_first)
    def _():
        first_ref[...] = value

    @pl.when(jnp.logical_not(in_first))
    def _():
        second_ref[...] = value


def combine_kernel(bonds, place_ref, live_ref, own_ref, *refs):
    hops, (out_ref, first_ref, second_ref) = refs[:-3], refs[-3:]
    total = own_ref[...] + hop_sum(bonds, place_ref[0], hops, step_half)
    result = alive_of(live_ref, 0, total.shape[1]) * total * (1.0 / HALF_WIDTH)
    out_ref[...] = result
    store_halves(result, first_ref, second_ref)


def filter_kernel(bonds, place_ref, live_ref, own_ref, start_ref, *refs):
    hops, (out_ref, sent_ref, first_ref, second_ref) = refs[:-4], refs[-4:]
    total = own_ref[...] + hop_sum(bonds, place_ref[0], hops, step_half)
    image = alive_of(live_ref, 0, total.shape[1]) * total * (1.0 / HALF_WIDTH)
    second = 2.0 * image - start_ref[...]
    out_ref[...] = second
    width = sent_ref.shape[1]
    sent = jnp.where(place_ref[1] == 0, second[:, :width], second[:, width:])
    sent_ref[...] = sent
    store_halves(sent, first_ref, second_ref)


def crossed_kernel(bonds, states, place_ref, own_ref, field_ref, *refs):
    hops, out_ref = refs[:-1], refs[-1]
    width, count = hops[-1].shape[1], own_ref.shape[0]
    theirs = hop_sum(bonds, place_ref[0], hops, lambda first, second: jnp.concatenate([first, second], axis=0))
    mine = jnp.where(place_ref[1] == 0, field_ref[:, width:], field_ref[:, :width])
    crossed = product(stacked(mine), stacked(theirs))
    out_ref[:, :count] = own_ref[:, :count] * (1.0 / states)
    projected = own_ref[:, count:] + crossed + crossed.T
    out_ref[:, count:] = projected * (1.0 / (HALF_WIDTH * states))


def local(vectors, tile_values, tile_cols, live_rows, boundary_map, field_levels):
    dev_count = lax.axis_size(AXES)
    bonds = dev_count.bit_length() - 2
    flip = (dev_count - 1) // 3
    position = lax.axis_index(AXES)
    parity = sum(bit(position, place) for place in range(0, bonds + 1, 2)) & 1
    place = jnp.stack([position ^ flip, parity]).astype(jnp.int32)
    vec_count, row_count = vectors.shape
    tile_size = tile_values.shape[1]
    block_count = row_count // tile_size
    per_block = tile_values.shape[0] // block_count
    tiles = tile_values.reshape(block_count, per_block, tile_size, tile_size)
    targets = boundary_map.reshape(1, row_count)
    params = pltpu.CompilerParams(vmem_limit_bytes=LIMIT)

    def coupled(here, bond):
        return bit(here ^ flip, bond) != bit(here ^ flip, bond + 1)

    def hop(value, bond):
        pairs = [(here, here ^ (3 << bond) if coupled(here, bond) else here) for here in range(dev_count)]
        return lax.ppermute(value, AXES, pairs)

    def near(flipped):
        pairs = [(here, here ^ (1 if coupled(here, 0) else 2)) for here in range(dev_count)]
        return lax.ppermute(flipped, AXES, pairs)

    def around(value):
        pairs = [(here, here ^ (2 if coupled(here, 1) else 4)) for here in range(dev_count)]
        return lax.ppermute(exchange(value, 2), AXES, pairs)

    def exchange(value, mask):
        return lax.ppermute(value, AXES, [(source, source ^ mask) for source in range(dev_count)])

    def whole(shape):
        return pl.BlockSpec(shape, lambda step: (0,) * len(shape))

    full = whole((vec_count, row_count))
    tile_spec = pl.BlockSpec(
        (block_count // STEPS, per_block, tile_size, tile_size), lambda step: (step, 0, 0, 0)
    )
    own_cost = pl.CostEstimate(
        flops=8 * vec_count * row_count * per_block * tile_size,
        bytes_accessed=4 * tile_values.size + 12 * vec_count * row_count,
        transcendentals=0,
    )
    split = pltpu.VMEM((2 * vec_count, row_count), BF16)

    def own_part(field, flipped):
        return pl.pallas_call(
            own_kernel,
            grid=(STEPS,),
            out_shape=jax.ShapeDtypeStruct((vec_count, row_count), F32),
            in_specs=[SMEM, SMEM, SMEM, full, full, tile_spec, whole((1, row_count))],
            out_specs=full,
            scratch_shapes=[split],
            compiler_params=params,
            cost_estimate=own_cost,
            name="own",
        )(place, tile_cols, field_levels, field, flipped, tiles, targets)

    def own_gram(field, flipped):
        return pl.pallas_call(
            own_gram_kernel,
            grid=(STEPS,),
            out_shape=jax.ShapeDtypeStruct((vec_count, 2 * vec_count), F32),
            in_specs=[SMEM, SMEM, SMEM, SMEM, full, full, tile_spec, whole((1, row_count))],
            out_specs=whole((vec_count, 2 * vec_count)),
            scratch_shapes=[split],
            compiler_params=params,
            cost_estimate=own_cost,
            name="own_gram",
        )(place, tile_cols, field_levels, live_rows, field, flipped, tiles, targets)

    def row_specs(width):
        shape, middle = (vec_count // STEPS, width), STEPS // 2
        return (
            pl.BlockSpec(shape, lambda step: (step, 0)),
            pl.BlockSpec(shape, lambda step: (jnp.minimum(step, middle - 1), 0)),
            pl.BlockSpec(shape, lambda step: (jnp.maximum(step - middle, 0), 0)),
        )

    def row_shapes(width):
        whole_shape = jax.ShapeDtypeStruct((vec_count, width), F32)
        half_shape = jax.ShapeDtypeStruct((vec_count // 2, width), F32)
        return [whole_shape, half_shape, half_shape]

    rows, first_rows, second_rows = row_specs(row_count)
    hop_specs = [rows] * (bonds - 2) + [first_rows, second_rows] + [rows]

    def exchanged(field, first_half, second_half, closest):
        far = [hop(field, bond) for bond in reversed(range(2, bonds))]
        return far + [hop(first_half, 1), around(second_half), closest]

    start, *halves_of = pl.pallas_call(
        start_kernel,
        grid=(STEPS,),
        out_shape=row_shapes(row_count),
        in_specs=[SMEM, rows],
        out_specs=[rows, first_rows, second_rows],
        compiler_params=params,
        name="start",
    )(live_rows, vectors)
    flipped = exchange(start, 1)
    hops = exchanged(start, *halves_of, near(flipped))
    own = own_part(start, flipped)
    first, *halves_of = pl.pallas_call(
        functools.partial(combine_kernel, bonds),
        grid=(STEPS,),
        out_shape=row_shapes(row_count),
        in_specs=[SMEM, SMEM, rows] + hop_specs,
        out_specs=[rows, first_rows, second_rows],
        compiler_params=params,
        name="combine",
    )(place, live_rows, own, *hops)
    flipped = exchange(first, 1)
    hops = exchanged(first, *halves_of, near(flipped))
    own = own_part(first, flipped)
    second, sent, *halves_of = pl.pallas_call(
        functools.partial(filter_kernel, bonds),
        grid=(STEPS,),
        out_shape=row_shapes(row_count)[:1] + row_shapes(row_count // 2),
        in_specs=[SMEM, SMEM, rows, rows] + hop_specs,
        out_specs=[rows, *row_specs(row_count // 2)],
        compiler_params=params,
        name="filter",
    )(place, live_rows, own, start, *hops)
    flipped = exchange(second, 1)
    hops = exchanged(sent, *halves_of, hop(sent, 0))
    grams = own_gram(second, flipped)
    sums = pl.pallas_call(
        functools.partial(crossed_kernel, bonds, dev_count * row_count),
        out_shape=jax.ShapeDtypeStruct((vec_count, 2 * vec_count), F32),
        in_specs=[SMEM] + [pl.BlockSpec(memory_space=pltpu.VMEM)] * (bonds + 3),
        out_specs=pl.BlockSpec(memory_space=pltpu.VMEM),
        compiler_params=params,
        name="crossed",
    )(place, grams, second, *hops)
    for digit in range(bonds + 1):
        sums = sums + exchange(sums, 1 << digit)
    return (second, sums[:, :vec_count], sums[:, vec_count:])


def solution(mesh):
    in_specs = (
        P(None, ("groups", "hi", "lo")),
        P(("groups", "hi", "lo"), None, None),
        P(("hi", "lo")),
        P(("hi", "lo")),
        P(("hi", "lo")),
        P("groups"),
    )
    out_specs = (P(None, ("groups", "hi", "lo")), P("groups", None), P("groups", None))
    return jax.shard_map(local, mesh=mesh, in_specs=in_specs, out_specs=out_specs, check_vma=False)
```

```python
import functools

import jax
import jax.numpy as jnp
from jax import lax
from jax.experimental import pallas as pl
from jax.experimental.pallas import tpu as pltpu
from jax.sharding import PartitionSpec as P

HOP_SCALE = 0.5
ANISOTROPY = 1.0
FIELD_STEP = 0.25
HALF_WIDTH = 4.0
AXES = ("hi", "lo")
STEPS = 4
F32, BF16 = jnp.float32, jnp.bfloat16
SMEM = pl.BlockSpec(memory_space=pltpu.SMEM)
LIMIT = 32 * 1024 * 1024


def bit(number, place):
    return (number >> place) & 1


def halves(value):
    head = value.astype(BF16)
    return head, (value - head.astype(F32)).astype(BF16)


def stacked(value):
    return jnp.concatenate(halves(value), axis=0)


def product(left, right):
    rows, columns = left.shape[0] // 2, right.shape[0] // 2
    whole = lax.dot_general(left, right, (((1,), (1,)), ((), ())), preferred_element_type=F32)
    tails = whole[:rows, columns:] + whole[rows:, :columns] + whole[rows:, columns:]
    return whole[:rows, :columns] + tails


def coupling(config, bond):
    differ = bit(config, bond) ^ bit(config, bond + 1)
    return jnp.where(differ == 1, HOP_SCALE, 0.0)


def onsite_of(config, fields_ref):
    count = fields_ref.shape[0]
    spins = [bit(config, place).astype(F32) - 0.5 for place in range(count)]
    total = jnp.float32(0.0)
    for place in range(count):
        total += fields_ref[place].astype(F32) * FIELD_STEP * spins[place]
    for place in range(count - 1):
        total += ANISOTROPY * spins[place] * spins[place + 1]
    return total


def alive_of(live_ref, first, count):
    rows = lax.broadcasted_iota(jnp.int32, (1, count), 1) + first
    return (rows < live_ref[0]).astype(F32)


def own_block(block, row, config, cols_ref, fields_ref, field_ref, split_ref, flipped_ref, tiles_ref, map_ref):
    per_block, tile = tiles_ref.shape[1], tiles_ref.shape[2]
    span = pl.ds(pl.multiple_of(block * tile, tile), tile)
    picked = []
    for which in range(per_block):
        column = cols_ref[block * per_block + which]
        picked.append(split_ref[:, pl.ds(pl.multiple_of(column * tile, tile), tile)])
    weights = jnp.concatenate([tiles_ref[row, which] for which in range(per_block)], axis=1)
    total = product(jnp.concatenate(picked, axis=1), stacked(weights))
    total += onsite_of(config, fields_ref) * field_ref[:, span]
    targets = jnp.broadcast_to(map_ref[:, span], (8, tile))
    inside, outside = targets & (tile - 1), targets // tile
    outside = jnp.where(targets < 0, -1, outside)
    groups = []
    for group in range(field_ref.shape[0] // 8):
        found = jnp.zeros((8, tile), F32)
        for source in range(field_ref.shape[1] // tile):
            values = flipped_ref[group * 8 : group * 8 + 8, source * tile : (source + 1) * tile]
            moved = jnp.take_along_axis(values, inside, axis=1)
            found = jnp.where(outside == source, moved, found)
        groups.append(found)
    return span, total + HOP_SCALE * jnp.concatenate(groups, axis=0)


def own_kernel(place_ref, cols_ref, fields_ref, field_ref, flipped_ref, tiles_ref, map_ref, out_ref, split_ref):
    step, blocks = pl.program_id(0), tiles_ref.shape[0]

    @pl.when(step == 0)
    def _():
        split_ref[...] = stacked(field_ref[...])

    for row in range(blocks):
        span, total = own_block(
            step * blocks + row, row, place_ref[0], cols_ref, fields_ref, field_ref, split_ref, flipped_ref, tiles_ref, map_ref
        )
        out_ref[:, span] = total


def own_gram_kernel(
    place_ref, cols_ref, fields_ref, live_ref, field_ref, flipped_ref, tiles_ref, map_ref, out_ref, split_ref
):
    step, blocks, tile = pl.program_id(0), tiles_ref.shape[0], tiles_ref.shape[2]
    count = field_ref.shape[0]

    @pl.when(step == 0)
    def _():
        split_ref[...] = stacked(field_ref[...])
        out_ref[:, :count] = product(split_ref[...], split_ref[...])
        out_ref[:, count:] = jnp.zeros((count, count), F32)

    parts = []
    for row in range(blocks):
        span, total = own_block(
            step * blocks + row, row, place_ref[0], cols_ref, fields_ref, field_ref, split_ref, flipped_ref, tiles_ref, map_ref
        )
        parts.append(alive_of(live_ref, (step * blocks + row) * tile, tile) * total)
    image = stacked(jnp.concatenate(parts, axis=1))
    width = blocks * tile
    out_ref[:, count:] += product(split_ref[:, pl.ds(pl.multiple_of(step * width, width), width)], image)


def hop_sum(bonds, config, refs, upper):
    total = coupling(config, 0) * refs[-1][...]
    if bonds > 1:
        total += coupling(config, 1) * upper(refs[-3][...], refs[-2][...])
    for bond, ref in zip(reversed(range(2, bonds)), refs):
        total += coupling(config, bond) * ref[...]
    return total


def step_half(first, second):
    return jnp.where(pl.program_id(0) < pl.num_programs(0) // 2, first, second)


def start_kernel(live_ref, vectors_ref, out_ref, first_ref, second_ref):
    start = vectors_ref[...] * alive_of(live_ref, 0, vectors_ref.shape[1])
    out_ref[...] = start
    store_halves(start, first_ref, second_ref)


def store_halves(value, first_ref, second_ref):
    in_first = pl.program_id(0) < pl.num_programs(0) // 2

    @pl.when(in_first)
    def _():
        first_ref[...] = value

    @pl.when(jnp.logical_not(in_first))
    def _():
        second_ref[...] = value


def combine_kernel(bonds, place_ref, live_ref, own_ref, *refs):
    hops, (out_ref, first_ref, second_ref) = refs[:-3], refs[-3:]
    total = own_ref[...] + hop_sum(bonds, place_ref[0], hops, step_half)
    result = alive_of(live_ref, 0, total.shape[1]) * total * (1.0 / HALF_WIDTH)
    out_ref[...] = result
    store_halves(result, first_ref, second_ref)


def filter_kernel(bonds, place_ref, live_ref, own_ref, start_ref, *refs):
    hops, (out_ref, kept_ref, sent_ref) = refs[:-3], refs[-3:]
    total = own_ref[...] + hop_sum(bonds, place_ref[0], hops, step_half)
    image = alive_of(live_ref, 0, total.shape[1]) * total * (1.0 / HALF_WIDTH)
    second = 2.0 * image - start_ref[...]
    out_ref[...] = second
    kept_ref[...] = second
    width = sent_ref.shape[1]
    sent_ref[...] = jnp.where(place_ref[1] == 0, second[:, :width], second[:, width:])


def crossed_kernel(bonds, states, place_ref, own_ref, field_ref, *refs):
    hops, out_ref = refs[:-1], refs[-1]
    width, count = hops[0].shape[1], own_ref.shape[0]
    theirs = jnp.zeros((count, width), F32)
    for bond, hop in zip(reversed(range(bonds)), hops):
        theirs += coupling(place_ref[0], bond) * hop[...]
    mine = jnp.where(place_ref[1] == 0, field_ref[:, width:], field_ref[:, :width])
    crossed = product(stacked(mine), stacked(theirs))
    out_ref[:, :count] = own_ref[:, :count] * (1.0 / states)
    projected = own_ref[:, count:] + crossed + crossed.T
    out_ref[:, count:] = projected * (1.0 / (HALF_WIDTH * states))


def local(vectors, tile_values, tile_cols, live_rows, boundary_map, field_levels):
    dev_count = lax.axis_size(AXES)
    bonds = dev_count.bit_length() - 2
    flip = (dev_count - 1) // 3
    position = lax.axis_index(AXES)
    parity = sum(bit(position, place) for place in range(0, bonds + 1, 2)) & 1
    place = jnp.stack([position ^ flip, parity]).astype(jnp.int32)
    vec_count, row_count = vectors.shape
    tile_size = tile_values.shape[1]
    block_count = row_count // tile_size
    per_block = tile_values.shape[0] // block_count
    tiles = tile_values.reshape(block_count, per_block, tile_size, tile_size)
    targets = boundary_map.reshape(1, row_count)
    params = pltpu.CompilerParams(vmem_limit_bytes=LIMIT)

    def coupled(here, bond):
        return bit(here ^ flip, bond) != bit(here ^ flip, bond + 1)

    def hop(value, bond):
        pairs = [(here, here ^ (3 << bond) if coupled(here, bond) else here) for here in range(dev_count)]
        return lax.ppermute(value, AXES, pairs)

    def near(flipped):
        pairs = [(here, here ^ (1 if coupled(here, 0) else 2)) for here in range(dev_count)]
        return lax.ppermute(flipped, AXES, pairs)

    def exchange(value, mask):
        return lax.ppermute(value, AXES, [(source, source ^ mask) for source in range(dev_count)])

    def whole(shape):
        return pl.BlockSpec(shape, lambda step: (0,) * len(shape))

    full = whole((vec_count, row_count))
    tile_spec = pl.BlockSpec(
        (block_count // STEPS, per_block, tile_size, tile_size), lambda step: (step, 0, 0, 0)
    )
    own_cost = pl.CostEstimate(
        flops=8 * vec_count * row_count * per_block * tile_size,
        bytes_accessed=4 * tile_values.size + 12 * vec_count * row_count,
        transcendentals=0,
    )
    split = pltpu.VMEM((2 * vec_count, row_count), BF16)

    def own_part(field, flipped):
        return pl.pallas_call(
            own_kernel,
            grid=(STEPS,),
            out_shape=jax.ShapeDtypeStruct((vec_count, row_count), F32),
            in_specs=[SMEM, SMEM, SMEM, full, full, tile_spec, whole((1, row_count))],
            out_specs=full,
            scratch_shapes=[split],
            compiler_params=params,
            cost_estimate=own_cost,
            name="own",
        )(place, tile_cols, field_levels, field, flipped, tiles, targets)

    def own_gram(field, flipped):
        return pl.pallas_call(
            own_gram_kernel,
            grid=(STEPS,),
            out_shape=jax.ShapeDtypeStruct((vec_count, 2 * vec_count), F32),
            in_specs=[SMEM, SMEM, SMEM, SMEM, full, full, tile_spec, whole((1, row_count))],
            out_specs=whole((vec_count, 2 * vec_count)),
            scratch_shapes=[split],
            compiler_params=params,
            cost_estimate=own_cost,
            name="own_gram",
        )(place, tile_cols, field_levels, live_rows, field, flipped, tiles, targets)

    def row_specs(width):
        shape, middle = (vec_count // STEPS, width), STEPS // 2
        return (
            pl.BlockSpec(shape, lambda step: (step, 0)),
            pl.BlockSpec(shape, lambda step: (jnp.minimum(step, middle - 1), 0)),
            pl.BlockSpec(shape, lambda step: (jnp.maximum(step - middle, 0), 0)),
        )

    def row_shapes(width):
        whole_shape = jax.ShapeDtypeStruct((vec_count, width), F32)
        half_shape = jax.ShapeDtypeStruct((vec_count // 2, width), F32)
        return [whole_shape, half_shape, half_shape]

    rows, first_rows, second_rows = row_specs(row_count)
    hop_specs = [rows] * (bonds - 2) + [first_rows, second_rows] + [rows]

    def apply(field, first_half, second_half):
        flipped = exchange(field, 1)
        far = [hop(field, bond) for bond in reversed(range(2, bonds))]
        aside = lax.ppermute(second_half, AXES, [(here, here ^ 2) for here in range(dev_count) if coupled(here, 1)])
        flipped, first_half = lax.optimization_barrier((flipped, first_half))
        direct = hop(first_half, 1)
        closest = near(flipped)
        own, aside = lax.optimization_barrier((own_part(field, flipped), aside))
        round_way = [(here, here ^ 4) for here in range(dev_count) if not coupled(here, 1)]
        return own, far + [direct, lax.ppermute(aside, AXES, round_way), closest]

    start, *halves_of = pl.pallas_call(
        start_kernel,
        grid=(STEPS,),
        out_shape=row_shapes(row_count),
        in_specs=[SMEM, rows],
        out_specs=[rows, first_rows, second_rows],
        compiler_params=params,
        name="start",
    )(live_rows, vectors)
    own, hops = apply(start, *halves_of)
    first, *halves_of = pl.pallas_call(
        functools.partial(combine_kernel, bonds),
        grid=(STEPS,),
        out_shape=row_shapes(row_count),
        in_specs=[SMEM, SMEM, rows] + hop_specs,
        out_specs=[rows, first_rows, second_rows],
        compiler_params=params,
        name="combine",
    )(place, live_rows, own, *hops)
    own, hops = apply(first, *halves_of)
    second, kept, sent = pl.pallas_call(
        functools.partial(filter_kernel, bonds),
        grid=(STEPS,),
        out_shape=[row_shapes(row_count)[0], row_shapes(row_count)[0], row_shapes(row_count // 2)[0]],
        in_specs=[SMEM, SMEM, rows, rows] + hop_specs,
        out_specs=[rows, rows, row_specs(row_count // 2)[0]],
        compiler_params=params,
        name="filter",
    )(place, live_rows, own, start, *hops)
    flipped = exchange(kept, 1)
    hops = [hop(sent, bond) for bond in reversed(range(2, bonds))]
    flipped, sent = lax.optimization_barrier((flipped, sent))
    hops += [hop(sent, 1), hop(sent, 0)]
    grams = own_gram(kept, flipped)
    sums = pl.pallas_call(
        functools.partial(crossed_kernel, bonds, dev_count * row_count),
        out_shape=jax.ShapeDtypeStruct((vec_count, 2 * vec_count), F32),
        in_specs=[SMEM] + [pl.BlockSpec(memory_space=pltpu.VMEM)] * (bonds + 2),
        out_specs=pl.BlockSpec(memory_space=pltpu.VMEM),
        compiler_params=params,
        name="crossed",
    )(place, grams, kept, *hops)
    for digit in range(bonds + 1):
        sums = sums + exchange(sums, 1 << digit)
    return (second, sums[:, :vec_count], sums[:, vec_count:])


def solution(mesh):
    in_specs = (
        P(None, ("groups", "hi", "lo")),
        P(("groups", "hi", "lo"), None, None),
        P(("hi", "lo")),
        P(("hi", "lo")),
        P(("hi", "lo")),
        P("groups"),
    )
    out_specs = (P(None, ("groups", "hi", "lo")), P("groups", None), P("groups", None))
    return jax.shard_map(local, mesh=mesh, in_specs=in_specs, out_specs=out_specs, check_vma=False)
```

```python
import functools

import jax
import jax.numpy as jnp
from jax import lax
from jax.experimental import pallas as pl
from jax.experimental.pallas import tpu as pltpu
from jax.sharding import PartitionSpec as P

HOP_SCALE = 0.5
ANISOTROPY = 1.0
FIELD_STEP = 0.25
HALF_WIDTH = 4.0
AXES = ("hi", "lo")
STEPS = 4
F32, BF16 = jnp.float32, jnp.bfloat16
SMEM = pl.BlockSpec(memory_space=pltpu.SMEM)
LIMIT = 32 * 1024 * 1024


def bit(number, place):
    return (number >> place) & 1


def halves(value):
    head = value.astype(BF16)
    return head, (value - head.astype(F32)).astype(BF16)


def stacked(value):
    return jnp.concatenate(halves(value), axis=0)


def product(left, right):
    rows, columns = left.shape[0] // 2, right.shape[0] // 2
    whole = lax.dot_general(left, right, (((1,), (1,)), ((), ())), preferred_element_type=F32)
    tails = whole[:rows, columns:] + whole[rows:, :columns] + whole[rows:, columns:]
    return whole[:rows, :columns] + tails


def coupling(config, bond):
    differ = bit(config, bond) ^ bit(config, bond + 1)
    return jnp.where(differ == 1, HOP_SCALE, 0.0)


def onsite_of(config, fields_ref):
    count = fields_ref.shape[0]
    spins = [bit(config, place).astype(F32) - 0.5 for place in range(count)]
    total = jnp.float32(0.0)
    for place in range(count):
        total += fields_ref[place].astype(F32) * FIELD_STEP * spins[place]
    for place in range(count - 1):
        total += ANISOTROPY * spins[place] * spins[place + 1]
    return total


def alive_of(live_ref, first, count):
    rows = lax.broadcasted_iota(jnp.int32, (1, count), 1) + first
    return (rows < live_ref[0]).astype(F32)


def own_block(block, row, config, cols_ref, fields_ref, field_ref, split_ref, flipped_ref, tiles_ref, map_ref):
    per_block, tile = tiles_ref.shape[1], tiles_ref.shape[2]
    span = pl.ds(pl.multiple_of(block * tile, tile), tile)
    picked = []
    for which in range(per_block):
        column = cols_ref[block * per_block + which]
        picked.append(split_ref[:, pl.ds(pl.multiple_of(column * tile, tile), tile)])
    weights = jnp.concatenate([tiles_ref[row, which] for which in range(per_block)], axis=1)
    total = product(jnp.concatenate(picked, axis=1), stacked(weights))
    total += onsite_of(config, fields_ref) * field_ref[:, span]
    targets = jnp.broadcast_to(map_ref[:, span], (8, tile))
    inside, outside = targets & (tile - 1), targets // tile
    outside = jnp.where(targets < 0, -1, outside)
    groups = []
    for group in range(field_ref.shape[0] // 8):
        found = jnp.zeros((8, tile), F32)
        for source in range(field_ref.shape[1] // tile):
            values = flipped_ref[group * 8 : group * 8 + 8, source * tile : (source + 1) * tile]
            moved = jnp.take_along_axis(values, inside, axis=1)
            found = jnp.where(outside == source, moved, found)
        groups.append(found)
    return span, total + HOP_SCALE * jnp.concatenate(groups, axis=0)


def own_kernel(place_ref, cols_ref, fields_ref, field_ref, flipped_ref, tiles_ref, map_ref, out_ref, split_ref):
    step, blocks = pl.program_id(0), tiles_ref.shape[0]

    @pl.when(step == 0)
    def _():
        split_ref[...] = stacked(field_ref[...])

    for row in range(blocks):
        span, total = own_block(
            step * blocks + row, row, place_ref[0], cols_ref, fields_ref, field_ref, split_ref, flipped_ref, tiles_ref, map_ref
        )
        out_ref[:, span] = total


def own_gram_kernel(
    place_ref, cols_ref, fields_ref, live_ref, field_ref, flipped_ref, tiles_ref, map_ref, out_ref, split_ref
):
    step, blocks, tile = pl.program_id(0), tiles_ref.shape[0], tiles_ref.shape[2]
    count = field_ref.shape[0]

    @pl.when(step == 0)
    def _():
        split_ref[...] = stacked(field_ref[...])
        out_ref[:, :count] = product(split_ref[...], split_ref[...])
        out_ref[:, count:] = jnp.zeros((count, count), F32)

    parts = []
    for row in range(blocks):
        span, total = own_block(
            step * blocks + row, row, place_ref[0], cols_ref, fields_ref, field_ref, split_ref, flipped_ref, tiles_ref, map_ref
        )
        parts.append(alive_of(live_ref, (step * blocks + row) * tile, tile) * total)
    image = stacked(jnp.concatenate(parts, axis=1))
    width = blocks * tile
    out_ref[:, count:] += product(split_ref[:, pl.ds(pl.multiple_of(step * width, width), width)], image)


def hop_sum(bonds, config, refs, upper):
    total = coupling(config, 0) * refs[-1][...]
    if bonds > 1:
        total += coupling(config, 1) * upper(refs[-3][...], refs[-2][...])
    for bond, ref in zip(reversed(range(2, bonds)), refs):
        total += coupling(config, bond) * ref[...]
    return total


def step_half(first, second):
    return jnp.where(pl.program_id(0) < pl.num_programs(0) // 2, first, second)


def start_kernel(live_ref, vectors_ref, out_ref, first_ref, second_ref):
    start = vectors_ref[...] * alive_of(live_ref, 0, vectors_ref.shape[1])
    out_ref[...] = start
    store_halves(start, first_ref, second_ref)


def store_halves(value, first_ref, second_ref):
    in_first = pl.program_id(0) < pl.num_programs(0) // 2

    @pl.when(in_first)
    def _():
        first_ref[...] = value

    @pl.when(jnp.logical_not(in_first))
    def _():
        second_ref[...] = value


def combine_kernel(bonds, place_ref, live_ref, own_ref, *refs):
    hops, (out_ref, first_ref, second_ref) = refs[:-3], refs[-3:]
    total = own_ref[...] + hop_sum(bonds, place_ref[0], hops, step_half)
    result = alive_of(live_ref, 0, total.shape[1]) * total * (1.0 / HALF_WIDTH)
    out_ref[...] = result
    store_halves(result, first_ref, second_ref)


def filter_kernel(bonds, place_ref, live_ref, own_ref, start_ref, *refs):
    hops, (out_ref, kept_ref, sent_ref) = refs[:-3], refs[-3:]
    total = own_ref[...] + hop_sum(bonds, place_ref[0], hops, step_half)
    image = alive_of(live_ref, 0, total.shape[1]) * total * (1.0 / HALF_WIDTH)
    second = 2.0 * image - start_ref[...]
    out_ref[...] = second
    kept_ref[...] = second
    width = sent_ref.shape[1]
    sent_ref[...] = jnp.where(place_ref[1] == 0, second[:, :width], second[:, width:])


def crossed_kernel(bonds, states, place_ref, own_ref, field_ref, *refs):
    hops, out_ref = refs[:-1], refs[-1]
    width, count = hops[0].shape[1], own_ref.shape[0]
    theirs = jnp.zeros((count, width), F32)
    for bond, hop in zip(reversed(range(bonds)), hops):
        theirs += coupling(place_ref[0], bond) * hop[...]
    mine = jnp.where(place_ref[1] == 0, field_ref[:, width:], field_ref[:, :width])
    crossed = product(stacked(mine), stacked(theirs))
    out_ref[:, :count] = own_ref[:, :count] * (1.0 / states)
    projected = own_ref[:, count:] + crossed + crossed.T
    out_ref[:, count:] = projected * (1.0 / (HALF_WIDTH * states))


def local(vectors, tile_values, tile_cols, live_rows, boundary_map, field_levels):
    dev_count = lax.axis_size(AXES)
    bonds = dev_count.bit_length() - 2
    flip = (dev_count - 1) // 3
    position = lax.axis_index(AXES)
    parity = sum(bit(position, place) for place in range(0, bonds + 1, 2)) & 1
    place = jnp.stack([position ^ flip, parity]).astype(jnp.int32)
    vec_count, row_count = vectors.shape
    tile_size = tile_values.shape[1]
    block_count = row_count // tile_size
    per_block = tile_values.shape[0] // block_count
    tiles = tile_values.reshape(block_count, per_block, tile_size, tile_size)
    targets = boundary_map.reshape(1, row_count)
    params = pltpu.CompilerParams(vmem_limit_bytes=LIMIT)

    def coupled(here, bond):
        return bit(here ^ flip, bond) != bit(here ^ flip, bond + 1)

    def hop(value, bond):
        pairs = [(here, here ^ (3 << bond) if coupled(here, bond) else here) for here in range(dev_count)]
        return lax.ppermute(value, AXES, pairs)

    def near(flipped):
        pairs = [(here, here ^ (1 if coupled(here, 0) else 2)) for here in range(dev_count)]
        return lax.ppermute(flipped, AXES, pairs)

    def exchange(value, mask):
        return lax.ppermute(value, AXES, [(source, source ^ mask) for source in range(dev_count)])

    def whole(shape):
        return pl.BlockSpec(shape, lambda step: (0,) * len(shape))

    full = whole((vec_count, row_count))
    tile_spec = pl.BlockSpec(
        (block_count // STEPS, per_block, tile_size, tile_size), lambda step: (step, 0, 0, 0)
    )
    own_cost = pl.CostEstimate(
        flops=8 * vec_count * row_count * per_block * tile_size,
        bytes_accessed=4 * tile_values.size + 12 * vec_count * row_count,
        transcendentals=0,
    )
    split = pltpu.VMEM((2 * vec_count, row_count), BF16)

    def own_part(field, flipped):
        return pl.pallas_call(
            own_kernel,
            grid=(STEPS,),
            out_shape=jax.ShapeDtypeStruct((vec_count, row_count), F32),
            in_specs=[SMEM, SMEM, SMEM, full, full, tile_spec, whole((1, row_count))],
            out_specs=full,
            scratch_shapes=[split],
            compiler_params=params,
            cost_estimate=own_cost,
            name="own",
        )(place, tile_cols, field_levels, field, flipped, tiles, targets)

    def own_gram(field, flipped):
        return pl.pallas_call(
            own_gram_kernel,
            grid=(STEPS,),
            out_shape=jax.ShapeDtypeStruct((vec_count, 2 * vec_count), F32),
            in_specs=[SMEM, SMEM, SMEM, SMEM, full, full, tile_spec, whole((1, row_count))],
            out_specs=whole((vec_count, 2 * vec_count)),
            scratch_shapes=[split],
            compiler_params=params,
            cost_estimate=own_cost,
            name="own_gram",
        )(place, tile_cols, field_levels, live_rows, field, flipped, tiles, targets)

    def row_specs(width):
        shape, middle = (vec_count // STEPS, width), STEPS // 2
        return (
            pl.BlockSpec(shape, lambda step: (step, 0)),
            pl.BlockSpec(shape, lambda step: (jnp.minimum(step, middle - 1), 0)),
            pl.BlockSpec(shape, lambda step: (jnp.maximum(step - middle, 0), 0)),
        )

    def row_shapes(width):
        whole_shape = jax.ShapeDtypeStruct((vec_count, width), F32)
        half_shape = jax.ShapeDtypeStruct((vec_count // 2, width), F32)
        return [whole_shape, half_shape, half_shape]

    rows, first_rows, second_rows = row_specs(row_count)
    hop_specs = [rows] * (bonds - 2) + [first_rows, second_rows] + [rows]

    def apply(field, first_half, second_half):
        legs = [(here, here ^ 2) for here in range(dev_count) if coupled(here, 1)]
        round_way = [(here, here ^ 4) for here in range(dev_count) if not coupled(here, 1)]
        flipped = exchange(field, 1)
        far = [hop(field, bond) for bond in reversed(range(2, bonds))]
        aside = lax.ppermute(lax.ppermute(second_half, AXES, legs), AXES, round_way)
        direct = hop(first_half, 1)
        closest = near(flipped)
        return own_part(field, flipped), far + [direct, aside, closest]

    start, *halves_of = pl.pallas_call(
        start_kernel,
        grid=(STEPS,),
        out_shape=row_shapes(row_count),
        in_specs=[SMEM, rows],
        out_specs=[rows, first_rows, second_rows],
        compiler_params=params,
        name="start",
    )(live_rows, vectors)
    own, hops = apply(start, *halves_of)
    first, *halves_of = pl.pallas_call(
        functools.partial(combine_kernel, bonds),
        grid=(STEPS,),
        out_shape=row_shapes(row_count),
        in_specs=[SMEM, SMEM, rows] + hop_specs,
        out_specs=[rows, first_rows, second_rows],
        compiler_params=params,
        name="combine",
    )(place, live_rows, own, *hops)
    own, hops = apply(first, *halves_of)
    second, kept, sent = pl.pallas_call(
        functools.partial(filter_kernel, bonds),
        grid=(STEPS,),
        out_shape=[row_shapes(row_count)[0], row_shapes(row_count)[0], row_shapes(row_count // 2)[0]],
        in_specs=[SMEM, SMEM, rows, rows] + hop_specs,
        out_specs=[rows, rows, row_specs(row_count // 2)[0]],
        compiler_params=params,
        name="filter",
    )(place, live_rows, own, start, *hops)
    flipped = exchange(kept, 1)
    hops = [hop(sent, bond) for bond in reversed(range(2, bonds))]
    flipped, sent = lax.optimization_barrier((flipped, sent))
    hops += [hop(sent, 1), hop(sent, 0)]
    grams = own_gram(kept, flipped)
    sums = pl.pallas_call(
        functools.partial(crossed_kernel, bonds, dev_count * row_count),
        out_shape=jax.ShapeDtypeStruct((vec_count, 2 * vec_count), F32),
        in_specs=[SMEM] + [pl.BlockSpec(memory_space=pltpu.VMEM)] * (bonds + 2),
        out_specs=pl.BlockSpec(memory_space=pltpu.VMEM),
        compiler_params=params,
        name="crossed",
    )(place, grams, kept, *hops)
    for digit in range(bonds + 1):
        sums = sums + exchange(sums, 1 << digit)
    return (second, sums[:, :vec_count], sums[:, vec_count:])


def solution(mesh):
    in_specs = (
        P(None, ("groups", "hi", "lo")),
        P(("groups", "hi", "lo"), None, None),
        P(("hi", "lo")),
        P(("hi", "lo")),
        P(("hi", "lo")),
        P("groups"),
    )
    out_specs = (P(None, ("groups", "hi", "lo")), P("groups", None), P("groups", None))
    return jax.shard_map(local, mesh=mesh, in_specs=in_specs, out_specs=out_specs, check_vma=False)
```

```python
import functools

import jax
import jax.numpy as jnp
from jax import lax
from jax.experimental import pallas as pl
from jax.experimental.pallas import tpu as pltpu
from jax.sharding import PartitionSpec as P

HOP_SCALE = 0.5
ANISOTROPY = 1.0
FIELD_STEP = 0.25
HALF_WIDTH = 4.0
AXES = ("hi", "lo")
STEPS = 4
F32, BF16 = jnp.float32, jnp.bfloat16
SMEM = pl.BlockSpec(memory_space=pltpu.SMEM)
LIMIT = 32 * 1024 * 1024


def bit(number, place):
    return (number >> place) & 1


def halves(value):
    head = value.astype(BF16)
    return head, (value - head.astype(F32)).astype(BF16)


def stacked(value):
    return jnp.concatenate(halves(value), axis=0)


def product(left, right):
    rows, columns = left.shape[0] // 2, right.shape[0] // 2
    whole = lax.dot_general(left, right, (((1,), (1,)), ((), ())), preferred_element_type=F32)
    tails = whole[:rows, columns:] + whole[rows:, :columns] + whole[rows:, columns:]
    return whole[:rows, :columns] + tails


def coupling(config, bond):
    differ = bit(config, bond) ^ bit(config, bond + 1)
    return jnp.where(differ == 1, HOP_SCALE, 0.0)


def onsite_of(config, fields_ref):
    count = fields_ref.shape[0]
    spins = [bit(config, place).astype(F32) - 0.5 for place in range(count)]
    total = jnp.float32(0.0)
    for place in range(count):
        total += fields_ref[place].astype(F32) * FIELD_STEP * spins[place]
    for place in range(count - 1):
        total += ANISOTROPY * spins[place] * spins[place + 1]
    return total


def alive_of(live_ref, first, count):
    rows = lax.broadcasted_iota(jnp.int32, (1, count), 1) + first
    return (rows < live_ref[0]).astype(F32)


def own_block(block, row, config, cols_ref, fields_ref, field_ref, split_ref, flipped_ref, tiles_ref, map_ref):
    per_block, tile = tiles_ref.shape[1], tiles_ref.shape[2]
    span = pl.ds(pl.multiple_of(block * tile, tile), tile)
    picked = []
    for which in range(per_block):
        column = cols_ref[block * per_block + which]
        picked.append(split_ref[:, pl.ds(pl.multiple_of(column * tile, tile), tile)])
    weights = jnp.concatenate([tiles_ref[row, which] for which in range(per_block)], axis=1)
    total = product(jnp.concatenate(picked, axis=1), stacked(weights))
    total += onsite_of(config, fields_ref) * field_ref[:, span]
    targets = jnp.broadcast_to(map_ref[:, span], (8, tile))
    inside, outside = targets & (tile - 1), targets // tile
    outside = jnp.where(targets < 0, -1, outside)
    groups = []
    for group in range(field_ref.shape[0] // 8):
        found = jnp.zeros((8, tile), F32)
        for source in range(field_ref.shape[1] // tile):
            values = flipped_ref[group * 8 : group * 8 + 8, source * tile : (source + 1) * tile]
            moved = jnp.take_along_axis(values, inside, axis=1)
            found = jnp.where(outside == source, moved, found)
        groups.append(found)
    return span, total + HOP_SCALE * jnp.concatenate(groups, axis=0)


def own_kernel(place_ref, cols_ref, fields_ref, field_ref, flipped_ref, tiles_ref, map_ref, out_ref, split_ref):
    step, blocks = pl.program_id(0), tiles_ref.shape[0]

    @pl.when(step == 0)
    def _():
        split_ref[...] = stacked(field_ref[...])

    for row in range(blocks):
        span, total = own_block(
            step * blocks + row, row, place_ref[0], cols_ref, fields_ref, field_ref, split_ref, flipped_ref, tiles_ref, map_ref
        )
        out_ref[:, span] = total


def own_gram_kernel(
    place_ref, cols_ref, fields_ref, live_ref, field_ref, flipped_ref, tiles_ref, map_ref, out_ref, copy_ref, split_ref
):
    step, blocks, tile = pl.program_id(0), tiles_ref.shape[0], tiles_ref.shape[2]
    count = field_ref.shape[0]

    @pl.when(step == 0)
    def _():
        split_ref[...] = stacked(field_ref[...])
        out_ref[:, :count] = product(split_ref[...], split_ref[...])
        out_ref[:, count:] = jnp.zeros((count, count), F32)

    parts = []
    for row in range(blocks):
        span, total = own_block(
            step * blocks + row, row, place_ref[0], cols_ref, fields_ref, field_ref, split_ref, flipped_ref, tiles_ref, map_ref
        )
        parts.append(alive_of(live_ref, (step * blocks + row) * tile, tile) * total)
    image = stacked(jnp.concatenate(parts, axis=1))
    width = blocks * tile
    span = pl.ds(pl.multiple_of(step * width, width), width)
    copy_ref[...] = field_ref[:, span]
    out_ref[:, count:] += product(split_ref[:, span], image)


def hop_sum(bonds, config, refs, upper):
    total = coupling(config, 0) * refs[-1][...]
    if bonds > 1:
        total += coupling(config, 1) * upper(refs[-3][...], refs[-2][...])
    for bond, ref in zip(reversed(range(2, bonds)), refs):
        total += coupling(config, bond) * ref[...]
    return total


def step_half(first, second):
    return jnp.where(pl.program_id(0) < pl.num_programs(0) // 2, first, second)


def start_kernel(live_ref, vectors_ref, out_ref, first_ref, second_ref):
    start = vectors_ref[...] * alive_of(live_ref, 0, vectors_ref.shape[1])
    out_ref[...] = start
    store_halves(start, first_ref, second_ref)


def store_halves(value, first_ref, second_ref):
    in_first = pl.program_id(0) < pl.num_programs(0) // 2

    @pl.when(in_first)
    def _():
        first_ref[...] = value

    @pl.when(jnp.logical_not(in_first))
    def _():
        second_ref[...] = value


def combine_kernel(bonds, place_ref, live_ref, own_ref, *refs):
    hops, (out_ref, first_ref, second_ref) = refs[:-3], refs[-3:]
    total = own_ref[...] + hop_sum(bonds, place_ref[0], hops, step_half)
    result = alive_of(live_ref, 0, total.shape[1]) * total * (1.0 / HALF_WIDTH)
    out_ref[...] = result
    store_halves(result, first_ref, second_ref)


def filter_kernel(bonds, place_ref, live_ref, own_ref, start_ref, *refs):
    hops, (kept_ref, sent_ref) = refs[:-2], refs[-2:]
    total = own_ref[...] + hop_sum(bonds, place_ref[0], hops, step_half)
    image = alive_of(live_ref, 0, total.shape[1]) * total * (1.0 / HALF_WIDTH)
    second = 2.0 * image - start_ref[...]
    kept_ref[...] = second
    width = sent_ref.shape[1]
    sent_ref[...] = jnp.where(place_ref[1] == 0, second[:, :width], second[:, width:])


def crossed_kernel(bonds, states, place_ref, own_ref, field_ref, *refs):
    hops, out_ref = refs[:-1], refs[-1]
    width, count = hops[0].shape[1], own_ref.shape[0]
    theirs = jnp.zeros((count, width), F32)
    for bond, hop in zip((*reversed(range(2, bonds)), 0, 1), hops):
        theirs += coupling(place_ref[0], bond) * hop[...]
    mine = jnp.where(place_ref[1] == 0, field_ref[:, width:], field_ref[:, :width])
    crossed = product(stacked(mine), stacked(theirs))
    out_ref[:, :count] = own_ref[:, :count] * (1.0 / states)
    projected = own_ref[:, count:] + crossed + crossed.T
    out_ref[:, count:] = projected * (1.0 / (HALF_WIDTH * states))


def local(vectors, tile_values, tile_cols, live_rows, boundary_map, field_levels):
    dev_count = lax.axis_size(AXES)
    bonds = dev_count.bit_length() - 2
    flip = (dev_count - 1) // 3
    position = lax.axis_index(AXES)
    parity = sum(bit(position, place) for place in range(0, bonds + 1, 2)) & 1
    place = jnp.stack([position ^ flip, parity]).astype(jnp.int32)
    vec_count, row_count = vectors.shape
    tile_size = tile_values.shape[1]
    block_count = row_count // tile_size
    per_block = tile_values.shape[0] // block_count
    tiles = tile_values.reshape(block_count, per_block, tile_size, tile_size)
    targets = boundary_map.reshape(1, row_count)
    params = pltpu.CompilerParams(vmem_limit_bytes=LIMIT)

    def coupled(here, bond):
        return bit(here ^ flip, bond) != bit(here ^ flip, bond + 1)

    def hop(value, bond):
        pairs = [(here, here ^ (3 << bond) if coupled(here, bond) else here) for here in range(dev_count)]
        return lax.ppermute(value, AXES, pairs)

    def near(flipped):
        pairs = [(here, here ^ (1 if coupled(here, 0) else 2)) for here in range(dev_count)]
        return lax.ppermute(flipped, AXES, pairs)

    def exchange(value, mask):
        return lax.ppermute(value, AXES, [(source, source ^ mask) for source in range(dev_count)])

    def whole(shape):
        return pl.BlockSpec(shape, lambda step: (0,) * len(shape))

    full = whole((vec_count, row_count))
    tile_spec = pl.BlockSpec(
        (block_count // STEPS, per_block, tile_size, tile_size), lambda step: (step, 0, 0, 0)
    )
    own_cost = pl.CostEstimate(
        flops=8 * vec_count * row_count * per_block * tile_size,
        bytes_accessed=4 * tile_values.size + 12 * vec_count * row_count,
        transcendentals=0,
    )
    split = pltpu.VMEM((2 * vec_count, row_count), BF16)

    def own_part(field, flipped):
        return pl.pallas_call(
            own_kernel,
            grid=(STEPS,),
            out_shape=jax.ShapeDtypeStruct((vec_count, row_count), F32),
            in_specs=[SMEM, SMEM, SMEM, full, full, tile_spec, whole((1, row_count))],
            out_specs=full,
            scratch_shapes=[split],
            compiler_params=params,
            cost_estimate=own_cost,
            name="own",
        )(place, tile_cols, field_levels, field, flipped, tiles, targets)

    def own_gram(field, flipped):
        return pl.pallas_call(
            own_gram_kernel,
            grid=(STEPS,),
            out_shape=[
                jax.ShapeDtypeStruct((vec_count, 2 * vec_count), F32),
                jax.ShapeDtypeStruct((vec_count, row_count), F32),
            ],
            in_specs=[SMEM, SMEM, SMEM, SMEM, full, full, tile_spec, whole((1, row_count))],
            out_specs=[
                whole((vec_count, 2 * vec_count)),
                pl.BlockSpec((vec_count, row_count // STEPS), lambda step: (0, step)),
            ],
            scratch_shapes=[split],
            compiler_params=params,
            cost_estimate=own_cost,
            name="own_gram",
        )(place, tile_cols, field_levels, live_rows, field, flipped, tiles, targets)

    def row_specs(width):
        shape, middle = (vec_count // STEPS, width), STEPS // 2
        return (
            pl.BlockSpec(shape, lambda step: (step, 0)),
            pl.BlockSpec(shape, lambda step: (jnp.minimum(step, middle - 1), 0)),
            pl.BlockSpec(shape, lambda step: (jnp.maximum(step - middle, 0), 0)),
        )

    def row_shapes(width):
        whole_shape = jax.ShapeDtypeStruct((vec_count, width), F32)
        half_shape = jax.ShapeDtypeStruct((vec_count // 2, width), F32)
        return [whole_shape, half_shape, half_shape]

    rows, first_rows, second_rows = row_specs(row_count)
    hop_specs = [rows] * (bonds - 2) + [first_rows, second_rows] + [rows]

    def apply(field, first_half, second_half):
        legs = [(here, here ^ 2) for here in range(dev_count) if coupled(here, 1)]
        round_way = [(here, here ^ 4) for here in range(dev_count) if not coupled(here, 1)]
        flipped = exchange(field, 1)
        far = [hop(field, bond) for bond in reversed(range(2, bonds))]
        aside = lax.ppermute(lax.ppermute(second_half, AXES, legs), AXES, round_way)
        direct = hop(first_half, 1)
        closest = near(flipped)
        return own_part(field, flipped), far + [direct, aside, closest]

    start, *halves_of = pl.pallas_call(
        start_kernel,
        grid=(STEPS,),
        out_shape=row_shapes(row_count),
        in_specs=[SMEM, rows],
        out_specs=[rows, first_rows, second_rows],
        compiler_params=params,
        name="start",
    )(live_rows, vectors)
    own, hops = apply(start, *halves_of)
    first, *halves_of = pl.pallas_call(
        functools.partial(combine_kernel, bonds),
        grid=(STEPS,),
        out_shape=row_shapes(row_count),
        in_specs=[SMEM, SMEM, rows] + hop_specs,
        out_specs=[rows, first_rows, second_rows],
        compiler_params=params,
        name="combine",
    )(place, live_rows, own, *hops)
    own, hops = apply(first, *halves_of)
    kept, sent = pl.pallas_call(
        functools.partial(filter_kernel, bonds),
        grid=(STEPS,),
        out_shape=[row_shapes(row_count)[0], row_shapes(row_count // 2)[0]],
        in_specs=[SMEM, SMEM, rows, rows] + hop_specs,
        out_specs=[rows, row_specs(row_count // 2)[0]],
        compiler_params=params,
        name="filter",
    )(place, live_rows, own, start, *hops)
    flipped = exchange(kept, 1)
    hops = [hop(sent, bond) for bond in reversed(range(2, bonds))]
    flipped, sent = lax.optimization_barrier((flipped, sent))
    hops += [hop(sent, 0), hop(sent, 1)]
    grams, second = own_gram(kept, flipped)
    sums = pl.pallas_call(
        functools.partial(crossed_kernel, bonds, dev_count * row_count),
        out_shape=jax.ShapeDtypeStruct((vec_count, 2 * vec_count), F32),
        in_specs=[SMEM] + [pl.BlockSpec(memory_space=pltpu.VMEM)] * (bonds + 2),
        out_specs=pl.BlockSpec(memory_space=pltpu.VMEM),
        compiler_params=params,
        name="crossed",
    )(place, grams, kept, *hops)
    for digit in range(bonds + 1):
        sums = sums + exchange(sums, 1 << digit)
    return (second, sums[:, :vec_count], sums[:, vec_count:])


def solution(mesh):
    in_specs = (
        P(None, ("groups", "hi", "lo")),
        P(("groups", "hi", "lo"), None, None),
        P(("hi", "lo")),
        P(("hi", "lo")),
        P(("hi", "lo")),
        P("groups"),
    )
    out_specs = (P(None, ("groups", "hi", "lo")), P("groups", None), P("groups", None))
    return jax.shard_map(local, mesh=mesh, in_specs=in_specs, out_specs=out_specs, check_vma=False)
```

```python
import functools

import jax
import jax.numpy as jnp
from jax import lax
from jax.experimental import pallas as pl
from jax.experimental.pallas import tpu as pltpu
from jax.sharding import PartitionSpec as P

HOP_SCALE = 0.5
ANISOTROPY = 1.0
FIELD_STEP = 0.25
HALF_WIDTH = 4.0
AXES = ("hi", "lo")
STEPS = 4
F32, BF16 = jnp.float32, jnp.bfloat16
SMEM = pl.BlockSpec(memory_space=pltpu.SMEM)
LIMIT = 32 * 1024 * 1024


def bit(number, place):
    return (number >> place) & 1


def halves(value):
    head = value.astype(BF16)
    return head, (value - head.astype(F32)).astype(BF16)


def stacked(value):
    return jnp.concatenate(halves(value), axis=0)


def product(left, right):
    rows, columns = left.shape[0] // 2, right.shape[0] // 2
    whole = lax.dot_general(left, right, (((1,), (1,)), ((), ())), preferred_element_type=F32)
    tails = whole[:rows, columns:] + whole[rows:, :columns] + whole[rows:, columns:]
    return whole[:rows, :columns] + tails


def coupling(config, bond):
    differ = bit(config, bond) ^ bit(config, bond + 1)
    return jnp.where(differ == 1, HOP_SCALE, 0.0)


def onsite_of(config, fields_ref):
    count = fields_ref.shape[0]
    spins = [bit(config, place).astype(F32) - 0.5 for place in range(count)]
    total = jnp.float32(0.0)
    for place in range(count):
        total += fields_ref[place].astype(F32) * FIELD_STEP * spins[place]
    for place in range(count - 1):
        total += ANISOTROPY * spins[place] * spins[place + 1]
    return total


def alive_of(live_ref, first, count):
    rows = lax.broadcasted_iota(jnp.int32, (1, count), 1) + first
    return (rows < live_ref[0]).astype(F32)


def own_block(block, row, config, cols_ref, fields_ref, field_ref, split_ref, flipped_ref, tiles_ref, map_ref):
    per_block, tile = tiles_ref.shape[1], tiles_ref.shape[2]
    span = pl.ds(pl.multiple_of(block * tile, tile), tile)
    picked = []
    for which in range(per_block):
        column = cols_ref[block * per_block + which]
        picked.append(split_ref[:, pl.ds(pl.multiple_of(column * tile, tile), tile)])
    weights = jnp.concatenate([tiles_ref[row, which] for which in range(per_block)], axis=1)
    total = product(jnp.concatenate(picked, axis=1), stacked(weights))
    total += onsite_of(config, fields_ref) * field_ref[:, span]
    targets = jnp.broadcast_to(map_ref[:, span], (8, tile))
    inside, outside = targets & (tile - 1), targets // tile
    outside = jnp.where(targets < 0, -1, outside)
    groups = []
    for group in range(field_ref.shape[0] // 8):
        found = jnp.zeros((8, tile), F32)
        for source in range(field_ref.shape[1] // tile):
            values = flipped_ref[group * 8 : group * 8 + 8, source * tile : (source + 1) * tile]
            moved = jnp.take_along_axis(values, inside, axis=1)
            found = jnp.where(outside == source, moved, found)
        groups.append(found)
    return span, total + HOP_SCALE * jnp.concatenate(groups, axis=0)


def own_kernel(place_ref, cols_ref, fields_ref, field_ref, flipped_ref, tiles_ref, map_ref, out_ref, split_ref):
    step, blocks = pl.program_id(0), tiles_ref.shape[0]

    @pl.when(step == 0)
    def _():
        split_ref[...] = stacked(field_ref[...])

    for row in range(blocks):
        span, total = own_block(
            step * blocks + row, row, place_ref[0], cols_ref, fields_ref, field_ref, split_ref, flipped_ref, tiles_ref, map_ref
        )
        out_ref[:, span] = total


def own_gram_kernel(
    place_ref, cols_ref, fields_ref, live_ref, field_ref, flipped_ref, tiles_ref, map_ref, out_ref, copy_ref, split_ref
):
    step, blocks, tile = pl.program_id(0), tiles_ref.shape[0], tiles_ref.shape[2]
    count = field_ref.shape[0]

    @pl.when(step == 0)
    def _():
        split_ref[...] = stacked(field_ref[...])
        out_ref[:, :count] = product(split_ref[...], split_ref[...])
        out_ref[:, count:] = jnp.zeros((count, count), F32)

    parts = []
    for row in range(blocks):
        span, total = own_block(
            step * blocks + row, row, place_ref[0], cols_ref, fields_ref, field_ref, split_ref, flipped_ref, tiles_ref, map_ref
        )
        parts.append(alive_of(live_ref, (step * blocks + row) * tile, tile) * total)
    image = stacked(jnp.concatenate(parts, axis=1))
    width = blocks * tile
    span = pl.ds(pl.multiple_of(step * width, width), width)
    copy_ref[...] = field_ref[:, span]
    out_ref[:, count:] += product(split_ref[:, span], image)


def hop_sum(bonds, config, refs, upper):
    total = coupling(config, 0) * refs[-1][...]
    if bonds > 1:
        total += coupling(config, 1) * upper(refs[-3][...], refs[-2][...])
    for bond, ref in zip(reversed(range(2, bonds)), refs):
        total += coupling(config, bond) * ref[...]
    return total


def step_half(first, second):
    return jnp.where(pl.program_id(0) < pl.num_programs(0) // 2, first, second)


def start_kernel(live_ref, vectors_ref, out_ref, first_ref, second_ref):
    start = vectors_ref[...] * alive_of(live_ref, 0, vectors_ref.shape[1])
    out_ref[...] = start
    store_halves(start, first_ref, second_ref)


def store_halves(value, first_ref, second_ref):
    in_first = pl.program_id(0) < pl.num_programs(0) // 2

    @pl.when(in_first)
    def _():
        first_ref[...] = value

    @pl.when(jnp.logical_not(in_first))
    def _():
        second_ref[...] = value


def combine_kernel(bonds, place_ref, live_ref, own_ref, *refs):
    hops, (out_ref, first_ref, second_ref) = refs[:-3], refs[-3:]
    total = own_ref[...] + hop_sum(bonds, place_ref[0], hops, step_half)
    result = alive_of(live_ref, 0, total.shape[1]) * total * (1.0 / HALF_WIDTH)
    out_ref[...] = result
    store_halves(result, first_ref, second_ref)


def filter_kernel(bonds, place_ref, live_ref, own_ref, start_ref, *refs):
    hops, (kept_ref, sent_ref) = refs[:-2], refs[-2:]
    total = own_ref[...] + hop_sum(bonds, place_ref[0], hops, step_half)
    image = alive_of(live_ref, 0, total.shape[1]) * total * (1.0 / HALF_WIDTH)
    second = 2.0 * image - start_ref[...]
    kept_ref[...] = second
    width = sent_ref.shape[1]
    sent_ref[...] = jnp.where(place_ref[1] == 0, second[:, :width], second[:, width:])


def crossed_kernel(bonds, states, place_ref, own_ref, field_ref, *refs):
    hops, out_ref = refs[:-1], refs[-1]
    width, count = hops[0].shape[1], own_ref.shape[0]
    theirs = jnp.zeros((count, width), F32)
    for bond, hop in zip((*reversed(range(2, bonds)), 0, 1), hops):
        theirs += coupling(place_ref[0], bond) * hop[...]
    mine = jnp.where(place_ref[1] == 0, field_ref[:, width:], field_ref[:, :width])
    crossed = product(stacked(mine), stacked(theirs))
    out_ref[:, :count] = own_ref[:, :count] * (1.0 / states)
    projected = own_ref[:, count:] + crossed + crossed.T
    out_ref[:, count:] = projected * (1.0 / (HALF_WIDTH * states))


def local(vectors, tile_values, tile_cols, live_rows, boundary_map, field_levels):
    dev_count = lax.axis_size(AXES)
    bonds = dev_count.bit_length() - 2
    flip = (dev_count - 1) // 3
    position = lax.axis_index(AXES)
    parity = sum(bit(position, place) for place in range(0, bonds + 1, 2)) & 1
    place = jnp.stack([position ^ flip, parity]).astype(jnp.int32)
    vec_count, row_count = vectors.shape
    tile_size = tile_values.shape[1]
    block_count = row_count // tile_size
    per_block = tile_values.shape[0] // block_count
    tiles = tile_values.reshape(block_count, per_block, tile_size, tile_size)
    targets = boundary_map.reshape(1, row_count)
    params = pltpu.CompilerParams(vmem_limit_bytes=LIMIT)

    def coupled(here, bond):
        return bit(here ^ flip, bond) != bit(here ^ flip, bond + 1)

    def hop(value, bond):
        pairs = [(here, here ^ (3 << bond) if coupled(here, bond) else here) for here in range(dev_count)]
        return lax.ppermute(value, AXES, pairs)

    def near(flipped):
        pairs = [(here, here ^ (1 if coupled(here, 0) else 2)) for here in range(dev_count)]
        return lax.ppermute(flipped, AXES, pairs)

    def exchange(value, mask):
        return lax.ppermute(value, AXES, [(source, source ^ mask) for source in range(dev_count)])

    def whole(shape):
        return pl.BlockSpec(shape, lambda step: (0,) * len(shape))

    full = whole((vec_count, row_count))
    tile_spec = pl.BlockSpec(
        (block_count // STEPS, per_block, tile_size, tile_size), lambda step: (step, 0, 0, 0)
    )
    own_cost = pl.CostEstimate(
        flops=8 * vec_count * row_count * per_block * tile_size,
        bytes_accessed=4 * tile_values.size + 12 * vec_count * row_count,
        transcendentals=0,
    )
    split = pltpu.VMEM((2 * vec_count, row_count), BF16)

    def own_part(field, flipped):
        return pl.pallas_call(
            own_kernel,
            grid=(STEPS,),
            out_shape=jax.ShapeDtypeStruct((vec_count, row_count), F32),
            in_specs=[SMEM, SMEM, SMEM, full, full, tile_spec, whole((1, row_count))],
            out_specs=full,
            scratch_shapes=[split],
            compiler_params=params,
            cost_estimate=own_cost,
            name="own",
        )(place, tile_cols, field_levels, field, flipped, tiles, targets)

    def own_gram(field, flipped):
        return pl.pallas_call(
            own_gram_kernel,
            grid=(STEPS,),
            out_shape=[
                jax.ShapeDtypeStruct((vec_count, 2 * vec_count), F32),
                jax.ShapeDtypeStruct((vec_count, row_count), F32),
            ],
            in_specs=[SMEM, SMEM, SMEM, SMEM, full, full, tile_spec, whole((1, row_count))],
            out_specs=[
                whole((vec_count, 2 * vec_count)),
                pl.BlockSpec((vec_count, row_count // STEPS), lambda step: (0, step)),
            ],
            scratch_shapes=[split],
            compiler_params=params,
            cost_estimate=own_cost,
            name="own_gram",
        )(place, tile_cols, field_levels, live_rows, field, flipped, tiles, targets)

    def row_specs(width):
        shape, middle = (vec_count // STEPS, width), STEPS // 2
        return (
            pl.BlockSpec(shape, lambda step: (step, 0)),
            pl.BlockSpec(shape, lambda step: (jnp.minimum(step, middle - 1), 0)),
            pl.BlockSpec(shape, lambda step: (jnp.maximum(step - middle, 0), 0)),
        )

    def row_shapes(width):
        whole_shape = jax.ShapeDtypeStruct((vec_count, width), F32)
        half_shape = jax.ShapeDtypeStruct((vec_count // 2, width), F32)
        return [whole_shape, half_shape, half_shape]

    rows, first_rows, second_rows = row_specs(row_count)
    hop_specs = [rows] * (bonds - 2) + [first_rows, second_rows] + [rows]

    def apply(field, first_half, second_half):
        legs = [(here, here ^ 2) for here in range(dev_count) if coupled(here, 1)]
        round_way = [(here, here ^ 4) for here in range(dev_count) if not coupled(here, 1)]
        flipped = exchange(field, 1)
        far = [hop(field, bond) for bond in reversed(range(2, bonds))]
        aside = lax.ppermute(lax.ppermute(second_half, AXES, legs), AXES, round_way)
        direct = hop(first_half, 1)
        closest = near(flipped)
        return own_part(field, flipped), far + [direct, aside, closest]

    start, *halves_of = pl.pallas_call(
        start_kernel,
        grid=(STEPS,),
        out_shape=row_shapes(row_count),
        in_specs=[SMEM, rows],
        out_specs=[rows, first_rows, second_rows],
        compiler_params=params,
        name="start",
    )(live_rows, vectors)
    own, hops = apply(start, *halves_of)
    first, *halves_of = pl.pallas_call(
        functools.partial(combine_kernel, bonds),
        grid=(STEPS,),
        out_shape=row_shapes(row_count),
        in_specs=[SMEM, SMEM, rows] + hop_specs,
        out_specs=[rows, first_rows, second_rows],
        compiler_params=params,
        name="combine",
    )(place, live_rows, own, *hops)
    own, hops = apply(first, *halves_of)
    kept, sent = pl.pallas_call(
        functools.partial(filter_kernel, bonds),
        grid=(STEPS,),
        out_shape=[row_shapes(row_count)[0], row_shapes(row_count // 2)[0]],
        in_specs=[SMEM, SMEM, rows, rows] + hop_specs,
        out_specs=[rows, row_specs(row_count // 2)[0]],
        compiler_params=params,
        name="filter",
    )(place, live_rows, own, start, *hops)
    flipped = exchange(kept, 1)
    hops = [hop(sent, bond) for bond in reversed(range(2, bonds))]
    flipped, sent = lax.optimization_barrier((flipped, sent))
    hops += [hop(sent, 0), hop(sent, 1)]
    grams, second = own_gram(kept, flipped)
    sums = pl.pallas_call(
        functools.partial(crossed_kernel, bonds, dev_count * row_count),
        out_shape=jax.ShapeDtypeStruct((vec_count, 2 * vec_count), F32),
        in_specs=[SMEM] + [pl.BlockSpec(memory_space=pltpu.VMEM)] * (bonds + 2),
        out_specs=pl.BlockSpec(memory_space=pltpu.VMEM),
        compiler_params=params,
        name="crossed",
    )(place, grams, kept, *hops)
    for digit in range(bonds - 1):
        sums = sums + exchange(sums, 1 << digit)
    apart = dev_count // 4
    groups = [[first + apart * part for part in range(4)] for first in range(apart)]
    parts = lax.all_gather(sums, AXES, axis_index_groups=groups)
    sums = (parts[0] + parts[1]) + (parts[2] + parts[3])
    return (second, sums[:, :vec_count], sums[:, vec_count:])


def solution(mesh):
    in_specs = (
        P(None, ("groups", "hi", "lo")),
        P(("groups", "hi", "lo"), None, None),
        P(("hi", "lo")),
        P(("hi", "lo")),
        P(("hi", "lo")),
        P("groups"),
    )
    out_specs = (P(None, ("groups", "hi", "lo")), P("groups", None), P("groups", None))
    return jax.shard_map(local, mesh=mesh, in_specs=in_specs, out_specs=out_specs, check_vma=False)
```

```python
import functools

import jax
import jax.numpy as jnp
from jax import lax
from jax.experimental import pallas as pl
from jax.experimental.pallas import tpu as pltpu
from jax.sharding import PartitionSpec as P

HOP_SCALE = 0.5
ANISOTROPY = 1.0
FIELD_STEP = 0.25
HALF_WIDTH = 4.0
AXES = ("hi", "lo")
STEPS = 4
F32, BF16 = jnp.float32, jnp.bfloat16
SMEM = pl.BlockSpec(memory_space=pltpu.SMEM)
LIMIT = 32 * 1024 * 1024


def bit(number, place):
    return (number >> place) & 1


def halves(value):
    head = value.astype(BF16)
    return head, (value - head.astype(F32)).astype(BF16)


def stacked(value):
    return jnp.concatenate(halves(value), axis=0)


def product(left, right):
    rows, columns = left.shape[0] // 2, right.shape[0] // 2
    whole = lax.dot_general(left, right, (((1,), (1,)), ((), ())), preferred_element_type=F32)
    tails = whole[:rows, columns:] + whole[rows:, :columns] + whole[rows:, columns:]
    return whole[:rows, :columns] + tails


def coupling(config, bond):
    differ = bit(config, bond) ^ bit(config, bond + 1)
    return jnp.where(differ == 1, HOP_SCALE, 0.0)


def onsite_of(config, fields_ref):
    count = fields_ref.shape[0]
    spins = [bit(config, place).astype(F32) - 0.5 for place in range(count)]
    total = jnp.float32(0.0)
    for place in range(count):
        total += fields_ref[place].astype(F32) * FIELD_STEP * spins[place]
    for place in range(count - 1):
        total += ANISOTROPY * spins[place] * spins[place + 1]
    return total


def alive_of(live_ref, first, count):
    rows = lax.broadcasted_iota(jnp.int32, (1, count), 1) + first
    return (rows < live_ref[0]).astype(F32)


def own_block(block, row, config, cols_ref, fields_ref, field_ref, split_ref, flipped_ref, tiles_ref, map_ref):
    per_block, tile = tiles_ref.shape[1], tiles_ref.shape[2]
    span = pl.ds(pl.multiple_of(block * tile, tile), tile)
    picked = []
    for which in range(per_block):
        column = cols_ref[block * per_block + which]
        picked.append(split_ref[:, pl.ds(pl.multiple_of(column * tile, tile), tile)])
    weights = jnp.concatenate([tiles_ref[row, which] for which in range(per_block)], axis=1)
    total = product(jnp.concatenate(picked, axis=1), stacked(weights))
    total += onsite_of(config, fields_ref) * field_ref[:, span]
    targets = jnp.broadcast_to(map_ref[:, span], (8, tile))
    inside, outside = targets & (tile - 1), targets // tile
    outside = jnp.where(targets < 0, -1, outside)
    groups = []
    for group in range(field_ref.shape[0] // 8):
        found = jnp.zeros((8, tile), F32)
        for source in range(field_ref.shape[1] // tile):
            values = flipped_ref[group * 8 : group * 8 + 8, source * tile : (source + 1) * tile]
            moved = jnp.take_along_axis(values, inside, axis=1)
            found = jnp.where(outside == source, moved, found)
        groups.append(found)
    return span, total + HOP_SCALE * jnp.concatenate(groups, axis=0)


def own_kernel(place_ref, cols_ref, fields_ref, field_ref, flipped_ref, tiles_ref, map_ref, out_ref, split_ref):
    step, blocks = pl.program_id(0), tiles_ref.shape[0]

    @pl.when(step == 0)
    def _():
        split_ref[...] = stacked(field_ref[...])

    for row in range(blocks):
        span, total = own_block(
            step * blocks + row, row, place_ref[0], cols_ref, fields_ref, field_ref, split_ref, flipped_ref, tiles_ref, map_ref
        )
        out_ref[:, span] = total


def own_gram_kernel(
    place_ref, cols_ref, fields_ref, live_ref, field_ref, flipped_ref, tiles_ref, map_ref, out_ref, copy_ref, split_ref
):
    step, blocks, tile = pl.program_id(0), tiles_ref.shape[0], tiles_ref.shape[2]
    count = field_ref.shape[0]

    @pl.when(step == 0)
    def _():
        split_ref[...] = stacked(field_ref[...])
        out_ref[:, :count] = product(split_ref[...], split_ref[...])
        out_ref[:, count:] = jnp.zeros((count, count), F32)

    parts = []
    for row in range(blocks):
        span, total = own_block(
            step * blocks + row, row, place_ref[0], cols_ref, fields_ref, field_ref, split_ref, flipped_ref, tiles_ref, map_ref
        )
        parts.append(alive_of(live_ref, (step * blocks + row) * tile, tile) * total)
    image = stacked(jnp.concatenate(parts, axis=1))
    width = blocks * tile
    span = pl.ds(pl.multiple_of(step * width, width), width)
    copy_ref[...] = field_ref[:, span]
    out_ref[:, count:] += product(split_ref[:, span], image)


def hop_sum(bonds, config, refs):
    total = coupling(config, bonds - 1) * refs[0][...]
    for bond, ref in zip(reversed(range(bonds - 1)), refs[1:]):
        total += coupling(config, bond) * ref[...]
    return total


def start_kernel(live_ref, vectors_ref, first_ref, second_ref):
    count = first_ref.shape[0]
    alive = alive_of(live_ref, 0, vectors_ref.shape[1])
    first_ref[...] = vectors_ref[:count] * alive
    second_ref[...] = vectors_ref[count:] * alive


def combine_kernel(bonds, place_ref, live_ref, own_ref, *refs):
    hops, out_ref = refs[:-1], refs[-1]
    total = own_ref[...] + hop_sum(bonds, place_ref[0], hops)
    out_ref[...] = alive_of(live_ref, 0, total.shape[1]) * total * (1.0 / HALF_WIDTH)


def filter_kernel(bonds, place_ref, live_ref, own_ref, start_ref, *refs):
    hops, (kept_ref, sent_ref) = refs[:bonds], refs[-2:]
    total = own_ref[...] + hop_sum(bonds, place_ref[0], hops)
    image = alive_of(live_ref, 0, total.shape[1]) * total * (1.0 / HALF_WIDTH)
    second = 2.0 * image - start_ref[...]
    kept_ref[...] = second
    width = sent_ref.shape[1]
    sent_ref[...] = jnp.where(place_ref[1] == 0, second[:, :width], second[:, width:])


def crossed_kernel(bonds, states, place_ref, own_ref, field_ref, *refs):
    hops, out_ref = refs[:-1], refs[-1]
    width, count = hops[0].shape[1], own_ref.shape[0]
    theirs = jnp.zeros((count, width), F32)
    for bond, hop in zip((*reversed(range(2, bonds)), 0, 1), hops):
        theirs += coupling(place_ref[0], bond) * hop[...]
    mine = jnp.where(place_ref[1] == 0, field_ref[:, width:], field_ref[:, :width])
    crossed = product(stacked(mine), stacked(theirs))
    out_ref[:, :count] = own_ref[:, :count] * (1.0 / states)
    projected = own_ref[:, count:] + crossed + crossed.T
    out_ref[:, count:] = projected * (1.0 / (HALF_WIDTH * states))


def local(vectors, tile_values, tile_cols, live_rows, boundary_map, field_levels):
    dev_count = lax.axis_size(AXES)
    bonds = dev_count.bit_length() - 2
    flip = (dev_count - 1) // 3
    position = lax.axis_index(AXES)
    parity = sum(bit(position, place) for place in range(0, bonds + 1, 2)) & 1
    place = jnp.stack([position ^ flip, parity]).astype(jnp.int32)
    vec_count, row_count = vectors.shape
    tile_size = tile_values.shape[1]
    block_count = row_count // tile_size
    per_block = tile_values.shape[0] // block_count
    tiles = tile_values.reshape(block_count, per_block, tile_size, tile_size)
    targets = boundary_map.reshape(1, row_count)
    params = pltpu.CompilerParams(vmem_limit_bytes=LIMIT)

    def coupled(here, bond):
        return bit(here ^ flip, bond) != bit(here ^ flip, bond + 1)

    def hop(value, bond):
        pairs = [(here, here ^ (3 << bond) if coupled(here, bond) else here) for here in range(dev_count)]
        return lax.ppermute(value, AXES, pairs)

    def near(flipped):
        pairs = [(here, here ^ (1 if coupled(here, 0) else 2)) for here in range(dev_count)]
        return lax.ppermute(flipped, AXES, pairs)

    def exchange(value, mask):
        return lax.ppermute(value, AXES, [(source, source ^ mask) for source in range(dev_count)])

    def whole(shape):
        return pl.BlockSpec(shape, lambda *refs: (0,) * len(shape))

    part_count = vec_count // 2
    full = whole((vec_count, row_count))
    tile_spec = pl.BlockSpec(
        (block_count // STEPS, per_block, tile_size, tile_size), lambda step: (step, 0, 0, 0)
    )

    def own_cost(count):
        return pl.CostEstimate(
            flops=8 * count * row_count * per_block * tile_size,
            bytes_accessed=4 * tile_values.size + 12 * count * row_count,
            transcendentals=0,
        )

    def own_part(field, flipped):
        part = whole((part_count, row_count))
        return pl.pallas_call(
            own_kernel,
            grid=(STEPS,),
            out_shape=jax.ShapeDtypeStruct((part_count, row_count), F32),
            in_specs=[SMEM, SMEM, SMEM, part, part, tile_spec, whole((1, row_count))],
            out_specs=part,
            scratch_shapes=[pltpu.VMEM((2 * part_count, row_count), BF16)],
            compiler_params=params,
            cost_estimate=own_cost(part_count),
            name="own",
        )(place, tile_cols, field_levels, field, flipped, tiles, targets)

    def own_gram(field, flipped):
        return pl.pallas_call(
            own_gram_kernel,
            grid=(STEPS,),
            out_shape=[
                jax.ShapeDtypeStruct((vec_count, 2 * vec_count), F32),
                jax.ShapeDtypeStruct((vec_count, row_count), F32),
            ],
            in_specs=[SMEM, SMEM, SMEM, SMEM, full, full, tile_spec, whole((1, row_count))],
            out_specs=[
                whole((vec_count, 2 * vec_count)),
                pl.BlockSpec((vec_count, row_count // STEPS), lambda step: (0, step)),
            ],
            scratch_shapes=[pltpu.VMEM((2 * vec_count, row_count), BF16)],
            compiler_params=params,
            cost_estimate=own_cost(vec_count),
            name="own_gram",
        )(place, tile_cols, field_levels, live_rows, field, flipped, tiles, targets)

    part_steps = 2
    part_shape = jax.ShapeDtypeStruct((part_count, row_count), F32)
    rows = pl.BlockSpec((part_count // part_steps, row_count), lambda step: (step, 0))

    def apply_first(field):
        flipped = exchange(field, 1)
        hops = [hop(field, bond) for bond in reversed(range(1, bonds))] + [near(flipped)]
        return own_part(field, flipped), hops

    def apply_second(field):
        flipped = exchange(field, 1)
        across = exchange(field, 2)
        hops = [hop(field, bond) for bond in reversed(range(2, bonds))]
        round_way = [(here, here ^ 4) for here in range(dev_count) if not coupled(here, 1)]
        hops += [lax.ppermute(across, AXES, round_way), exchange(across, 1)]
        return own_part(field, flipped), hops

    def combine(own, hops):
        return pl.pallas_call(
            functools.partial(combine_kernel, bonds),
            grid=(part_steps,),
            out_shape=part_shape,
            in_specs=[SMEM, SMEM] + [rows] * (bonds + 1),
            out_specs=rows,
            compiler_params=params,
            name="combine",
        )(place, live_rows, own, *hops)

    def filtered(begin, own, start, hops, taken):
        shapes = [
            jax.ShapeDtypeStruct((vec_count, row_count), F32),
            jax.ShapeDtypeStruct((vec_count, row_count // 2), F32),
        ]
        shift = begin // (part_count // part_steps)
        return pl.pallas_call(
            functools.partial(filter_kernel, bonds),
            grid=(part_steps,),
            out_shape=shapes,
            in_specs=[SMEM, SMEM] + [rows] * (bonds + 2) + [pl.BlockSpec(memory_space=pl.ANY)] * len(taken),
            out_specs=[
                pl.BlockSpec((part_count // part_steps, shape.shape[1]), lambda step: (step + shift, 0))
                for shape in shapes
            ],
            input_output_aliases={bonds + 4 + which: which for which in range(len(taken))},
            compiler_params=params,
            name="filter",
        )(place, live_rows, own, start, *hops, *taken)

    starts = pl.pallas_call(
        start_kernel,
        out_shape=[part_shape, part_shape],
        in_specs=[SMEM, pl.BlockSpec(memory_space=pltpu.VMEM)],
        out_specs=[pl.BlockSpec(memory_space=pltpu.VMEM)] * 2,
        compiler_params=params,
        name="start",
    )(live_rows, vectors)
    own_a, hops_a = apply_first(starts[0])
    own_b, hops_b = apply_second(starts[1])
    first_a = combine(own_a, hops_a)
    own_a, hops_a = apply_first(first_a)
    first_b = combine(own_b, hops_b)
    own_b, hops_b = apply_second(first_b)
    taken = filtered(0, own_a, starts[0], hops_a, ())
    kept, sent = filtered(part_count, own_b, starts[1], hops_b, taken)
    flipped = exchange(kept, 1)
    hops = [hop(sent, bond) for bond in reversed(range(2, bonds))]
    flipped, sent = lax.optimization_barrier((flipped, sent))
    hops += [hop(sent, 0), hop(sent, 1)]
    grams, second = own_gram(kept, flipped)
    sums = pl.pallas_call(
        functools.partial(crossed_kernel, bonds, dev_count * row_count),
        out_shape=jax.ShapeDtypeStruct((vec_count, 2 * vec_count), F32),
        in_specs=[SMEM] + [pl.BlockSpec(memory_space=pltpu.VMEM)] * (bonds + 2),
        out_specs=pl.BlockSpec(memory_space=pltpu.VMEM),
        compiler_params=params,
        name="crossed",
    )(place, grams, kept, *hops)
    for digit in range(bonds + 1):
        sums = sums + exchange(sums, 1 << digit)
    return (second, sums[:, :vec_count], sums[:, vec_count:])


def solution(mesh):
    in_specs = (
        P(None, ("groups", "hi", "lo")),
        P(("groups", "hi", "lo"), None, None),
        P(("hi", "lo")),
        P(("hi", "lo")),
        P(("hi", "lo")),
        P("groups"),
    )
    out_specs = (P(None, ("groups", "hi", "lo")), P("groups", None), P("groups", None))
    return jax.shard_map(local, mesh=mesh, in_specs=in_specs, out_specs=out_specs, check_vma=False)
```

```python
import functools

import jax
import jax.numpy as jnp
from jax import lax
from jax.experimental import pallas as pl
from jax.experimental.pallas import tpu as pltpu
from jax.sharding import PartitionSpec as P

HOP_SCALE = 0.5
ANISOTROPY = 1.0
FIELD_STEP = 0.25
HALF_WIDTH = 4.0
AXES = ("hi", "lo")
STEPS = 4
F32, BF16 = jnp.float32, jnp.bfloat16
SMEM = pl.BlockSpec(memory_space=pltpu.SMEM)
LIMIT = 32 * 1024 * 1024


def bit(number, place):
    return (number >> place) & 1


def halves(value):
    head = value.astype(BF16)
    return head, (value - head.astype(F32)).astype(BF16)


def stacked(value):
    return jnp.concatenate(halves(value), axis=0)


def product(left, right):
    rows, columns = left.shape[0] // 2, right.shape[0] // 2
    whole = lax.dot_general(left, right, (((1,), (1,)), ((), ())), preferred_element_type=F32)
    tails = whole[:rows, columns:] + whole[rows:, :columns] + whole[rows:, columns:]
    return whole[:rows, :columns] + tails


def coupling(config, bond):
    differ = bit(config, bond) ^ bit(config, bond + 1)
    return jnp.where(differ == 1, HOP_SCALE, 0.0)


def onsite_of(config, fields_ref):
    count = fields_ref.shape[0]
    spins = [bit(config, place).astype(F32) - 0.5 for place in range(count)]
    total = jnp.float32(0.0)
    for place in range(count):
        total += fields_ref[place].astype(F32) * FIELD_STEP * spins[place]
    for place in range(count - 1):
        total += ANISOTROPY * spins[place] * spins[place + 1]
    return total


def alive_of(live_ref, first, count):
    rows = lax.broadcasted_iota(jnp.int32, (1, count), 1) + first
    return (rows < live_ref[0]).astype(F32)


def own_block(block, config, cols_ref, fields_ref, field_ref, split_ref, flipped_ref, tiles_ref, map_ref):
    per_block, tile = tiles_ref.shape[1], tiles_ref.shape[2]
    span = pl.ds(pl.multiple_of(block * tile, tile), tile)
    picked = []
    for which in range(per_block):
        column = cols_ref[block * per_block + which]
        picked.append(split_ref[:, pl.ds(pl.multiple_of(column * tile, tile), tile)])
    weights = jnp.concatenate([tiles_ref[block, which] for which in range(per_block)], axis=1)
    total = product(jnp.concatenate(picked, axis=1), stacked(weights))
    total += onsite_of(config, fields_ref) * field_ref[:, span]
    targets = jnp.broadcast_to(map_ref[:, span], (8, tile))
    inside, outside = targets & (tile - 1), targets // tile
    outside = jnp.where(targets < 0, -1, outside)
    groups = []
    for group in range(field_ref.shape[0] // 8):
        found = jnp.zeros((8, tile), F32)
        for source in range(field_ref.shape[1] // tile):
            values = flipped_ref[group * 8 : group * 8 + 8, source * tile : (source + 1) * tile]
            moved = jnp.take_along_axis(values, inside, axis=1)
            found = jnp.where(outside == source, moved, found)
        groups.append(found)
    return span, total + HOP_SCALE * jnp.concatenate(groups, axis=0)


def own_kernel(place_ref, cols_ref, fields_ref, field_ref, flipped_ref, tiles_ref, map_ref, out_ref, split_ref):
    blocks = tiles_ref.shape[0] // STEPS
    split_ref[...] = stacked(field_ref[...])

    def body(step, carry):
        for row in range(blocks):
            span, total = own_block(
                step * blocks + row, place_ref[0], cols_ref, fields_ref, field_ref, split_ref, flipped_ref, tiles_ref, map_ref
            )
            out_ref[:, span] = total
        return carry

    lax.fori_loop(0, STEPS, body, 0)


def own_gram_kernel(
    place_ref, cols_ref, fields_ref, live_ref, field_ref, flipped_ref, tiles_ref, map_ref, out_ref, copy_ref, split_ref, sem
):
    blocks, tile = tiles_ref.shape[0] // STEPS, tiles_ref.shape[2]
    count, width = field_ref.shape[0], blocks * tile
    copy = pltpu.make_async_copy(field_ref, copy_ref, sem)
    copy.start()
    split_ref[...] = stacked(field_ref[...])
    out_ref[:, :count] = product(split_ref[...], split_ref[...])
    out_ref[:, count:] = jnp.zeros((count, count), F32)

    def body(step, carry):
        parts = []
        for row in range(blocks):
            block = step * blocks + row
            span, total = own_block(
                block, place_ref[0], cols_ref, fields_ref, field_ref, split_ref, flipped_ref, tiles_ref, map_ref
            )
            parts.append(alive_of(live_ref, block * tile, tile) * total)
        image = stacked(jnp.concatenate(parts, axis=1))
        span = pl.ds(pl.multiple_of(step * width, width), width)
        out_ref[:, count:] += product(split_ref[:, span], image)
        return carry

    lax.fori_loop(0, STEPS, body, 0)
    copy.wait()


def hop_sum(bonds, config, refs):
    total = coupling(config, 0) * refs[-1][...]
    total += coupling(config, 1) * jnp.concatenate([refs[-3][...], refs[-2][...]], axis=0)
    for bond, ref in zip(reversed(range(2, bonds)), refs):
        total += coupling(config, bond) * ref[...]
    return total


def store_halves(value, out_ref, first_ref, second_ref):
    middle = first_ref.shape[0]
    out_ref[...] = value
    first_ref[...] = value[:middle]
    second_ref[...] = value[middle:]


def start_kernel(live_ref, vectors_ref, out_ref, first_ref, second_ref):
    start = vectors_ref[...] * alive_of(live_ref, 0, vectors_ref.shape[1])
    store_halves(start, out_ref, first_ref, second_ref)


def combine_kernel(bonds, place_ref, live_ref, own_ref, *refs):
    hops, outs = refs[:-3], refs[-3:]
    total = own_ref[...] + hop_sum(bonds, place_ref[0], hops)
    store_halves(alive_of(live_ref, 0, total.shape[1]) * total * (1.0 / HALF_WIDTH), *outs)


def filter_kernel(bonds, place_ref, live_ref, own_ref, start_ref, *refs):
    hops, (kept_ref, sent_ref) = refs[:-2], refs[-2:]
    total = own_ref[...] + hop_sum(bonds, place_ref[0], hops)
    image = alive_of(live_ref, 0, total.shape[1]) * total * (1.0 / HALF_WIDTH)
    second = 2.0 * image - start_ref[...]
    kept_ref[...] = second
    width = sent_ref.shape[1]
    sent_ref[...] = jnp.where(place_ref[1] == 0, second[:, :width], second[:, width:])


def crossed_kernel(bonds, states, place_ref, own_ref, field_ref, *refs):
    hops, out_ref = refs[:-1], refs[-1]
    width, count = hops[0].shape[1], own_ref.shape[0]
    theirs = jnp.zeros((count, width), F32)
    for bond, hop in zip((*reversed(range(2, bonds)), 0, 1), hops):
        theirs += coupling(place_ref[0], bond) * hop[...]
    mine = jnp.where(place_ref[1] == 0, field_ref[:, width:], field_ref[:, :width])
    crossed = product(stacked(mine), stacked(theirs))
    out_ref[:, :count] = own_ref[:, :count] * (1.0 / states)
    projected = own_ref[:, count:] + crossed + crossed.T
    out_ref[:, count:] = projected * (1.0 / (HALF_WIDTH * states))


def local(vectors, tile_values, tile_cols, live_rows, boundary_map, field_levels):
    dev_count = lax.axis_size(AXES)
    bonds = dev_count.bit_length() - 2
    flip = (dev_count - 1) // 3
    position = lax.axis_index(AXES)
    parity = sum(bit(position, place) for place in range(0, bonds + 1, 2)) & 1
    place = jnp.stack([position ^ flip, parity]).astype(jnp.int32)
    vec_count, row_count = vectors.shape
    tile_size = tile_values.shape[1]
    block_count = row_count // tile_size
    per_block = tile_values.shape[0] // block_count
    tiles = tile_values.reshape(block_count, per_block, tile_size, tile_size)
    targets = boundary_map.reshape(1, row_count)
    params = pltpu.CompilerParams(vmem_limit_bytes=LIMIT)

    def coupled(here, bond):
        return bit(here ^ flip, bond) != bit(here ^ flip, bond + 1)

    def hop(value, bond):
        pairs = [(here, here ^ (3 << bond) if coupled(here, bond) else here) for here in range(dev_count)]
        return lax.ppermute(value, AXES, pairs)

    def near(flipped):
        pairs = [(here, here ^ (1 if coupled(here, 0) else 2)) for here in range(dev_count)]
        return lax.ppermute(flipped, AXES, pairs)

    def exchange(value, mask):
        return lax.ppermute(value, AXES, [(source, source ^ mask) for source in range(dev_count)])

    inside = pl.BlockSpec(memory_space=pltpu.VMEM)
    own_cost = pl.CostEstimate(
        flops=8 * vec_count * row_count * per_block * tile_size,
        bytes_accessed=4 * tile_values.size + 12 * vec_count * row_count,
        transcendentals=0,
    )
    split = pltpu.VMEM((2 * vec_count, row_count), BF16)
    gram_shape = jax.ShapeDtypeStruct((vec_count, 2 * vec_count), F32)

    def rows_by(count, width):
        return jax.ShapeDtypeStruct((count, width), F32)

    full = rows_by(vec_count, row_count)

    def own_part(field, flipped):
        return pl.pallas_call(
            own_kernel,
            out_shape=full,
            in_specs=[SMEM] * 3 + [inside] * 4,
            out_specs=inside,
            scratch_shapes=[split],
            compiler_params=params,
            cost_estimate=own_cost,
            name="own",
        )(place, tile_cols, field_levels, field, flipped, tiles, targets)

    def own_gram(field, flipped):
        return pl.pallas_call(
            own_gram_kernel,
            out_shape=[gram_shape, full],
            in_specs=[SMEM] * 4 + [inside] * 4,
            out_specs=[inside, pl.BlockSpec(memory_space=pl.ANY)],
            scratch_shapes=[split, pltpu.SemaphoreType.DMA(())],
            compiler_params=params,
            cost_estimate=own_cost,
            name="own_gram",
        )(place, tile_cols, field_levels, live_rows, field, flipped, tiles, targets)

    three = [full, rows_by(vec_count // 2, row_count), rows_by(vec_count // 2, row_count)]

    def apply(field, first_half, second_half):
        legs = [(here, here ^ 2) for here in range(dev_count) if coupled(here, 1)]
        round_way = [(here, here ^ 4) for here in range(dev_count) if not coupled(here, 1)]
        flipped = exchange(field, 1)
        far = [hop(field, bond) for bond in reversed(range(2, bonds))]
        aside = lax.ppermute(lax.ppermute(second_half, AXES, legs), AXES, round_way)
        direct = hop(first_half, 1)
        closest = near(flipped)
        return own_part(field, flipped), far + [direct, aside, closest]

    start, *halves_of = pl.pallas_call(
        start_kernel,
        out_shape=three,
        in_specs=[SMEM, inside],
        out_specs=[inside] * 3,
        compiler_params=params,
        name="start",
    )(live_rows, vectors)
    own, hops = apply(start, *halves_of)
    first, *halves_of = pl.pallas_call(
        functools.partial(combine_kernel, bonds),
        out_shape=three,
        in_specs=[SMEM] * 2 + [inside] * (bonds + 2),
        out_specs=[inside] * 3,
        compiler_params=params,
        name="combine",
    )(place, live_rows, own, *hops)
    own, hops = apply(first, *halves_of)
    kept, sent = pl.pallas_call(
        functools.partial(filter_kernel, bonds),
        out_shape=[full, rows_by(vec_count, row_count // 2)],
        in_specs=[SMEM] * 2 + [inside] * (bonds + 3),
        out_specs=[inside] * 2,
        compiler_params=params,
        name="filter",
    )(place, live_rows, own, start, *hops)
    flipped = exchange(kept, 1)
    hops = [hop(sent, bond) for bond in reversed(range(2, bonds))]
    flipped, sent = lax.optimization_barrier((flipped, sent))
    hops += [hop(sent, 0), hop(sent, 1)]
    grams, second = own_gram(kept, flipped)
    sums = pl.pallas_call(
        functools.partial(crossed_kernel, bonds, dev_count * row_count),
        out_shape=gram_shape,
        in_specs=[SMEM] + [inside] * (bonds + 2),
        out_specs=inside,
        compiler_params=params,
        name="crossed",
    )(place, grams, kept, *hops)
    for digit in range(bonds + 1):
        sums = sums + exchange(sums, 1 << digit)
    return (second, sums[:, :vec_count], sums[:, vec_count:])


def solution(mesh):
    in_specs = (
        P(None, ("groups", "hi", "lo")),
        P(("groups", "hi", "lo"), None, None),
        P(("hi", "lo")),
        P(("hi", "lo")),
        P(("hi", "lo")),
        P("groups"),
    )
    out_specs = (P(None, ("groups", "hi", "lo")), P("groups", None), P("groups", None))
    return jax.shard_map(local, mesh=mesh, in_specs=in_specs, out_specs=out_specs, check_vma=False)
```

```python
import functools

import jax
import jax.numpy as jnp
from jax import lax
from jax.experimental import pallas as pl
from jax.experimental.pallas import tpu as pltpu
from jax.sharding import PartitionSpec as P

HOP_SCALE = 0.5
ANISOTROPY = 1.0
FIELD_STEP = 0.25
HALF_WIDTH = 4.0
AXES = ("hi", "lo")
STEPS = 4
F32, BF16 = jnp.float32, jnp.bfloat16
SMEM = pl.BlockSpec(memory_space=pltpu.SMEM)
LIMIT = 32 * 1024 * 1024


def bit(number, place):
    return (number >> place) & 1


def halves(value):
    head = value.astype(BF16)
    return head, (value - head.astype(F32)).astype(BF16)


def stacked(value):
    return jnp.concatenate(halves(value), axis=0)


def product(left, right):
    rows, columns = left.shape[0] // 2, right.shape[0] // 2
    whole = lax.dot_general(left, right, (((1,), (1,)), ((), ())), preferred_element_type=F32)
    tails = whole[:rows, columns:] + whole[rows:, :columns] + whole[rows:, columns:]
    return whole[:rows, :columns] + tails


def coupling(config, bond):
    differ = bit(config, bond) ^ bit(config, bond + 1)
    return jnp.where(differ == 1, HOP_SCALE, 0.0)


def onsite_of(config, fields_ref):
    count = fields_ref.shape[0]
    spins = [bit(config, place).astype(F32) - 0.5 for place in range(count)]
    total = jnp.float32(0.0)
    for place in range(count):
        total += fields_ref[place].astype(F32) * FIELD_STEP * spins[place]
    for place in range(count - 1):
        total += ANISOTROPY * spins[place] * spins[place + 1]
    return total


def alive_of(live_ref, first, count):
    rows = lax.broadcasted_iota(jnp.int32, (1, count), 1) + first
    return (rows < live_ref[0]).astype(F32)


def own_block(block, config, cols_ref, fields_ref, field_ref, split_ref, flipped_ref, tiles_ref, map_ref):
    per_block, tile = tiles_ref.shape[1], tiles_ref.shape[2]
    span = pl.ds(pl.multiple_of(block * tile, tile), tile)
    picked = []
    for which in range(per_block):
        column = cols_ref[block * per_block + which]
        picked.append(split_ref[:, pl.ds(pl.multiple_of(column * tile, tile), tile)])
    weights = jnp.concatenate([tiles_ref[block, which] for which in range(per_block)], axis=1)
    total = product(jnp.concatenate(picked, axis=1), stacked(weights))
    total += onsite_of(config, fields_ref) * field_ref[:, span]
    targets = jnp.broadcast_to(map_ref[:, span], (8, tile))
    inside, outside = targets & (tile - 1), targets // tile
    outside = jnp.where(targets < 0, -1, outside)
    groups = []
    for group in range(field_ref.shape[0] // 8):
        found = jnp.zeros((8, tile), F32)
        for source in range(field_ref.shape[1] // tile):
            values = flipped_ref[group * 8 : group * 8 + 8, source * tile : (source + 1) * tile]
            moved = jnp.take_along_axis(values, inside, axis=1)
            found = jnp.where(outside == source, moved, found)
        groups.append(found)
    return span, total + HOP_SCALE * jnp.concatenate(groups, axis=0)


def own_kernel(place_ref, cols_ref, fields_ref, field_ref, flipped_ref, tiles_ref, map_ref, out_ref, split_ref):
    blocks = tiles_ref.shape[0] // STEPS
    split_ref[...] = stacked(field_ref[...])

    def body(step, carry):
        for row in range(blocks):
            span, total = own_block(
                step * blocks + row, place_ref[0], cols_ref, fields_ref, field_ref, split_ref, flipped_ref, tiles_ref, map_ref
            )
            out_ref[:, span] = total
        return carry

    lax.fori_loop(0, STEPS, body, 0)


def own_gram_kernel(
    place_ref, cols_ref, fields_ref, live_ref, field_ref, flipped_ref, tiles_ref, map_ref, out_ref, copy_ref, split_ref, sem
):
    blocks, tile = tiles_ref.shape[0] // STEPS, tiles_ref.shape[2]
    count, width = field_ref.shape[0], blocks * tile
    copy = pltpu.make_async_copy(field_ref, copy_ref, sem)
    copy.start()
    split_ref[...] = stacked(field_ref[...])
    out_ref[:, :count] = product(split_ref[...], split_ref[...])
    out_ref[:, count:] = jnp.zeros((count, count), F32)

    def body(step, carry):
        parts = []
        for row in range(blocks):
            block = step * blocks + row
            span, total = own_block(
                block, place_ref[0], cols_ref, fields_ref, field_ref, split_ref, flipped_ref, tiles_ref, map_ref
            )
            parts.append(alive_of(live_ref, block * tile, tile) * total)
        image = stacked(jnp.concatenate(parts, axis=1))
        span = pl.ds(pl.multiple_of(step * width, width), width)
        out_ref[:, count:] += product(split_ref[:, span], image)
        return carry

    lax.fori_loop(0, STEPS, body, 0)
    copy.wait()


def hop_sum(bonds, config, refs):
    total = coupling(config, 0) * refs[-1][...]
    total += coupling(config, 1) * jnp.concatenate([refs[-3][...], refs[-2][...]], axis=0)
    for bond, ref in zip(reversed(range(2, bonds)), refs):
        total += coupling(config, bond) * ref[...]
    return total


def store_halves(value, out_ref, first_ref, second_ref):
    middle = first_ref.shape[0]
    out_ref[...] = value
    first_ref[...] = value[:middle]
    second_ref[...] = value[middle:]


def start_kernel(live_ref, vectors_ref, out_ref, first_ref, second_ref):
    start = vectors_ref[...] * alive_of(live_ref, 0, vectors_ref.shape[1])
    store_halves(start, out_ref, first_ref, second_ref)


def combine_kernel(bonds, place_ref, live_ref, own_ref, *refs):
    hops, outs = refs[:-3], refs[-3:]
    total = own_ref[...] + hop_sum(bonds, place_ref[0], hops)
    store_halves(alive_of(live_ref, 0, total.shape[1]) * total * (1.0 / HALF_WIDTH), *outs)


def filter_kernel(bonds, place_ref, live_ref, own_ref, start_ref, *refs):
    hops, (kept_ref, sent_ref) = refs[:-2], refs[-2:]
    total = own_ref[...] + hop_sum(bonds, place_ref[0], hops)
    image = alive_of(live_ref, 0, total.shape[1]) * total * (1.0 / HALF_WIDTH)
    second = 2.0 * image - start_ref[...]
    kept_ref[...] = second
    width = sent_ref.shape[1]
    sent_ref[...] = jnp.where(place_ref[1] == 0, second[:, :width], second[:, width:])


def crossed_kernel(bonds, states, place_ref, own_ref, field_ref, *refs):
    hops, out_ref = refs[:-1], refs[-1]
    width, count = hops[-1].shape[1], own_ref.shape[0]
    near = coupling(place_ref[0], 0) * hops[-2][...] + coupling(place_ref[0], 1) * hops[-1][...]
    theirs = jnp.where(place_ref[1] == 0, 0.0, near), jnp.where(place_ref[1] == 0, near, 0.0)
    theirs = jnp.concatenate(theirs, axis=1)
    for bond, hop in zip(reversed(range(2, bonds)), hops):
        theirs += coupling(place_ref[0], bond) * hop[...]
    crossed = product(stacked(field_ref[...]), stacked(theirs))
    out_ref[:, :count] = own_ref[:, :count] * (1.0 / states)
    projected = own_ref[:, count:] + crossed + crossed.T
    out_ref[:, count:] = projected * (1.0 / (HALF_WIDTH * states))


def local(vectors, tile_values, tile_cols, live_rows, boundary_map, field_levels):
    dev_count = lax.axis_size(AXES)
    bonds = dev_count.bit_length() - 2
    flip = (dev_count - 1) // 3
    position = lax.axis_index(AXES)
    parity = sum(bit(position, place) for place in range(0, bonds + 1, 2)) & 1
    place = jnp.stack([position ^ flip, parity]).astype(jnp.int32)
    vec_count, row_count = vectors.shape
    tile_size = tile_values.shape[1]
    block_count = row_count // tile_size
    per_block = tile_values.shape[0] // block_count
    tiles = tile_values.reshape(block_count, per_block, tile_size, tile_size)
    targets = boundary_map.reshape(1, row_count)
    params = pltpu.CompilerParams(vmem_limit_bytes=LIMIT)

    def coupled(here, bond):
        return bit(here ^ flip, bond) != bit(here ^ flip, bond + 1)

    def hop(value, bond):
        pairs = [(here, here ^ (3 << bond) if coupled(here, bond) else here) for here in range(dev_count)]
        return lax.ppermute(value, AXES, pairs)

    def one_way(value, bond):
        pairs = [
            (here, here ^ (3 << bond))
            for here in range(dev_count)
            if coupled(here, bond) and bit(here, bond) != bit(here, bond - 1)
        ]
        return lax.ppermute(value, AXES, pairs)

    def near(flipped):
        pairs = [(here, here ^ (1 if coupled(here, 0) else 2)) for here in range(dev_count)]
        return lax.ppermute(flipped, AXES, pairs)

    def exchange(value, mask):
        return lax.ppermute(value, AXES, [(source, source ^ mask) for source in range(dev_count)])

    inside = pl.BlockSpec(memory_space=pltpu.VMEM)
    own_cost = pl.CostEstimate(
        flops=8 * vec_count * row_count * per_block * tile_size,
        bytes_accessed=4 * tile_values.size + 12 * vec_count * row_count,
        transcendentals=0,
    )
    split = pltpu.VMEM((2 * vec_count, row_count), BF16)
    gram_shape = jax.ShapeDtypeStruct((vec_count, 2 * vec_count), F32)

    def rows_by(count, width):
        return jax.ShapeDtypeStruct((count, width), F32)

    full = rows_by(vec_count, row_count)

    def own_part(field, flipped):
        return pl.pallas_call(
            own_kernel,
            out_shape=full,
            in_specs=[SMEM] * 3 + [inside] * 4,
            out_specs=inside,
            scratch_shapes=[split],
            compiler_params=params,
            cost_estimate=own_cost,
            name="own",
        )(place, tile_cols, field_levels, field, flipped, tiles, targets)

    def own_gram(field, flipped):
        return pl.pallas_call(
            own_gram_kernel,
            out_shape=[gram_shape, full],
            in_specs=[SMEM] * 4 + [inside] * 4,
            out_specs=[inside, pl.BlockSpec(memory_space=pl.ANY)],
            scratch_shapes=[split, pltpu.SemaphoreType.DMA(())],
            compiler_params=params,
            cost_estimate=own_cost,
            name="own_gram",
        )(place, tile_cols, field_levels, live_rows, field, flipped, tiles, targets)

    three = [full, rows_by(vec_count // 2, row_count), rows_by(vec_count // 2, row_count)]

    def apply(field, first_half, second_half):
        legs = [(here, here ^ 2) for here in range(dev_count) if coupled(here, 1)]
        round_way = [(here, here ^ 4) for here in range(dev_count) if not coupled(here, 1)]
        flipped = exchange(field, 1)
        far = [hop(field, bond) for bond in reversed(range(2, bonds))]
        aside = lax.ppermute(lax.ppermute(second_half, AXES, legs), AXES, round_way)
        direct = hop(first_half, 1)
        closest = near(flipped)
        return own_part(field, flipped), far + [direct, aside, closest]

    start, *halves_of = pl.pallas_call(
        start_kernel,
        out_shape=three,
        in_specs=[SMEM, inside],
        out_specs=[inside] * 3,
        compiler_params=params,
        name="start",
    )(live_rows, vectors)
    own, hops = apply(start, *halves_of)
    first, *halves_of = pl.pallas_call(
        functools.partial(combine_kernel, bonds),
        out_shape=three,
        in_specs=[SMEM] * 2 + [inside] * (bonds + 2),
        out_specs=[inside] * 3,
        compiler_params=params,
        name="combine",
    )(place, live_rows, own, *hops)
    own, hops = apply(first, *halves_of)
    kept, sent = pl.pallas_call(
        functools.partial(filter_kernel, bonds),
        out_shape=[full, rows_by(vec_count, row_count // 2)],
        in_specs=[SMEM] * 2 + [inside] * (bonds + 3),
        out_specs=[inside] * 2,
        compiler_params=params,
        name="filter",
    )(place, live_rows, own, start, *hops)
    flipped = exchange(kept, 1)
    hops = [one_way(kept, bond) for bond in reversed(range(2, bonds))]
    flipped, sent = lax.optimization_barrier((flipped, sent))
    hops += [hop(sent, 0), hop(sent, 1)]
    grams, second = own_gram(kept, flipped)
    sums = pl.pallas_call(
        functools.partial(crossed_kernel, bonds, dev_count * row_count),
        out_shape=gram_shape,
        in_specs=[SMEM] + [inside] * (bonds + 2),
        out_specs=inside,
        compiler_params=params,
        name="crossed",
    )(place, grams, kept, *hops)
    for digit in range(bonds + 1):
        sums = sums + exchange(sums, 1 << digit)
    return (second, sums[:, :vec_count], sums[:, vec_count:])


def solution(mesh):
    in_specs = (
        P(None, ("groups", "hi", "lo")),
        P(("groups", "hi", "lo"), None, None),
        P(("hi", "lo")),
        P(("hi", "lo")),
        P(("hi", "lo")),
        P("groups"),
    )
    out_specs = (P(None, ("groups", "hi", "lo")), P("groups", None), P("groups", None))
    return jax.shard_map(local, mesh=mesh, in_specs=in_specs, out_specs=out_specs, check_vma=False)
```

```python
import functools

import jax
import jax.numpy as jnp
from jax import lax
from jax.experimental import pallas as pl
from jax.experimental.pallas import tpu as pltpu
from jax.sharding import PartitionSpec as P

HOP_SCALE = 0.5
ANISOTROPY = 1.0
FIELD_STEP = 0.25
HALF_WIDTH = 4.0
AXES = ("hi", "lo")
STEPS = 4
F32, BF16 = jnp.float32, jnp.bfloat16
SMEM = pl.BlockSpec(memory_space=pltpu.SMEM)
LIMIT = 32 * 1024 * 1024


def bit(number, place):
    return (number >> place) & 1


def halves(value):
    head = value.astype(BF16)
    return head, (value - head.astype(F32)).astype(BF16)


def stacked(value):
    return jnp.concatenate(halves(value), axis=0)


def product(left, right):
    rows, columns = left.shape[0] // 2, right.shape[0] // 2
    whole = lax.dot_general(left, right, (((1,), (1,)), ((), ())), preferred_element_type=F32)
    tails = whole[:rows, columns:] + whole[rows:, :columns] + whole[rows:, columns:]
    return whole[:rows, :columns] + tails


def coupling(config, bond):
    differ = bit(config, bond) ^ bit(config, bond + 1)
    return jnp.where(differ == 1, HOP_SCALE, 0.0)


def onsite_of(config, fields_ref):
    count = fields_ref.shape[0]
    spins = [bit(config, place).astype(F32) - 0.5 for place in range(count)]
    total = jnp.float32(0.0)
    for place in range(count):
        total += fields_ref[place].astype(F32) * FIELD_STEP * spins[place]
    for place in range(count - 1):
        total += ANISOTROPY * spins[place] * spins[place + 1]
    return total


def alive_of(live_ref, first, count):
    rows = lax.broadcasted_iota(jnp.int32, (1, count), 1) + first
    return (rows < live_ref[0]).astype(F32)


def own_block(block, config, cols_ref, fields_ref, field_ref, split_ref, flipped_ref, tiles_ref, map_ref):
    per_block, tile = tiles_ref.shape[1], tiles_ref.shape[2]
    span = pl.ds(pl.multiple_of(block * tile, tile), tile)
    picked = []
    for which in range(per_block):
        column = cols_ref[block * per_block + which]
        picked.append(split_ref[:, pl.ds(pl.multiple_of(column * tile, tile), tile)])
    weights = jnp.concatenate([tiles_ref[block, which] for which in range(per_block)], axis=1)
    total = product(jnp.concatenate(picked, axis=1), stacked(weights))
    total += onsite_of(config, fields_ref) * field_ref[:, span]
    targets = jnp.broadcast_to(map_ref[:, span], (8, tile))
    inside, outside = targets & (tile - 1), targets // tile
    outside = jnp.where(targets < 0, -1, outside)
    groups = []
    for group in range(field_ref.shape[0] // 8):
        found = jnp.zeros((8, tile), F32)
        for source in range(field_ref.shape[1] // tile):
            values = flipped_ref[group * 8 : group * 8 + 8, source * tile : (source + 1) * tile]
            moved = jnp.take_along_axis(values, inside, axis=1)
            found = jnp.where(outside == source, moved, found)
        groups.append(found)
    return span, total + HOP_SCALE * jnp.concatenate(groups, axis=0)


def own_kernel(place_ref, cols_ref, fields_ref, field_ref, flipped_ref, tiles_ref, map_ref, out_ref, split_ref):
    blocks = tiles_ref.shape[0] // STEPS
    split_ref[...] = stacked(field_ref[...])

    def body(step, carry):
        for row in range(blocks):
            span, total = own_block(
                step * blocks + row, place_ref[0], cols_ref, fields_ref, field_ref, split_ref, flipped_ref, tiles_ref, map_ref
            )
            out_ref[:, span] = total
        return carry

    lax.fori_loop(0, STEPS, body, 0)


def own_gram_kernel(
    place_ref, cols_ref, fields_ref, live_ref, field_ref, flipped_ref, tiles_ref, map_ref, out_ref, copy_ref, split_ref, sem
):
    blocks, tile = tiles_ref.shape[0] // STEPS, tiles_ref.shape[2]
    count, width = field_ref.shape[0], blocks * tile
    copy = pltpu.make_async_copy(field_ref, copy_ref, sem)
    copy.start()
    split_ref[...] = stacked(field_ref[...])
    out_ref[:, :count] = product(split_ref[...], split_ref[...])
    out_ref[:, count:] = jnp.zeros((count, count), F32)

    def body(step, carry):
        parts = []
        for row in range(blocks):
            block = step * blocks + row
            span, total = own_block(
                block, place_ref[0], cols_ref, fields_ref, field_ref, split_ref, flipped_ref, tiles_ref, map_ref
            )
            parts.append(alive_of(live_ref, block * tile, tile) * total)
        image = stacked(jnp.concatenate(parts, axis=1))
        span = pl.ds(pl.multiple_of(step * width, width), width)
        out_ref[:, count:] += product(split_ref[:, span], image)
        return carry

    lax.fori_loop(0, STEPS, body, 0)
    copy.wait()


def hop_sum(bonds, config, refs):
    total = coupling(config, 0) * refs[-1][...]
    total += coupling(config, 1) * jnp.concatenate([refs[-3][...], refs[-2][...]], axis=0)
    for bond, ref in zip(reversed(range(2, bonds)), refs):
        total += coupling(config, bond) * ref[...]
    return total


def store_halves(value, out_ref, first_ref, second_ref):
    middle = first_ref.shape[0]
    out_ref[...] = value
    first_ref[...] = value[:middle]
    second_ref[...] = value[middle:]


def start_kernel(live_ref, vectors_ref, out_ref, first_ref, second_ref):
    start = vectors_ref[...] * alive_of(live_ref, 0, vectors_ref.shape[1])
    store_halves(start, out_ref, first_ref, second_ref)


def combine_kernel(bonds, place_ref, live_ref, own_ref, *refs):
    hops, outs = refs[:-3], refs[-3:]
    total = own_ref[...] + hop_sum(bonds, place_ref[0], hops)
    store_halves(alive_of(live_ref, 0, total.shape[1]) * total * (1.0 / HALF_WIDTH), *outs)


def filter_kernel(bonds, place_ref, live_ref, own_ref, start_ref, *refs):
    hops, (kept_ref, sent_ref, lead_ref, rest_ref) = refs[:-4], refs[-4:]
    total = own_ref[...] + hop_sum(bonds, place_ref[0], hops)
    image = alive_of(live_ref, 0, total.shape[1]) * total * (1.0 / HALF_WIDTH)
    second = 2.0 * image - start_ref[...]
    kept_ref[...] = second
    lead_ref[...] = second[:, : lead_ref.shape[1]]
    rest_ref[...] = second[:, lead_ref.shape[1] :]
    width = sent_ref.shape[1]
    sent_ref[...] = jnp.where(place_ref[1] == 0, second[:, :width], second[:, width:])


def crossed_kernel(bonds, states, place_ref, own_ref, field_ref, *refs):
    hops, out_ref = refs[:-1], refs[-1]
    width, count = hops[-1].shape[1], own_ref.shape[0]
    near = coupling(place_ref[0], 0) * hops[-2][...] + coupling(place_ref[0], 1) * hops[-1][...]
    theirs = jnp.where(place_ref[1] == 0, 0.0, near), jnp.where(place_ref[1] == 0, near, 0.0)
    theirs = jnp.concatenate(theirs, axis=1)
    for bond, lead, rest in zip(reversed(range(2, bonds)), hops, hops[bonds - 2 :]):
        theirs += coupling(place_ref[0], bond) * jnp.concatenate([lead[...], rest[...]], axis=1)
    crossed = product(stacked(field_ref[...]), stacked(theirs))
    out_ref[:, :count] = own_ref[:, :count] * (1.0 / states)
    projected = own_ref[:, count:] + crossed + crossed.T
    out_ref[:, count:] = projected * (1.0 / (HALF_WIDTH * states))


def local(vectors, tile_values, tile_cols, live_rows, boundary_map, field_levels):
    dev_count = lax.axis_size(AXES)
    bonds = dev_count.bit_length() - 2
    flip = (dev_count - 1) // 3
    position = lax.axis_index(AXES)
    parity = sum(bit(position, place) for place in range(0, bonds + 1, 2)) & 1
    place = jnp.stack([position ^ flip, parity]).astype(jnp.int32)
    vec_count, row_count = vectors.shape
    tile_size = tile_values.shape[1]
    block_count = row_count // tile_size
    per_block = tile_values.shape[0] // block_count
    tiles = tile_values.reshape(block_count, per_block, tile_size, tile_size)
    targets = boundary_map.reshape(1, row_count)
    params = pltpu.CompilerParams(vmem_limit_bytes=LIMIT)

    def coupled(here, bond):
        return bit(here ^ flip, bond) != bit(here ^ flip, bond + 1)

    def hop(value, bond):
        pairs = [(here, here ^ (3 << bond) if coupled(here, bond) else here) for here in range(dev_count)]
        return lax.ppermute(value, AXES, pairs)

    def one_way(value, bond, lead):
        pairs = [
            (here, here ^ (3 << bond))
            for here in range(dev_count)
            if coupled(here, bond) and bit(here, bond) ^ bit(here, bond - 1) == lead
        ]
        return lax.ppermute(value, AXES, pairs)

    def near(flipped):
        pairs = [(here, here ^ (1 if coupled(here, 0) else 2)) for here in range(dev_count)]
        return lax.ppermute(flipped, AXES, pairs)

    def exchange(value, mask):
        return lax.ppermute(value, AXES, [(source, source ^ mask) for source in range(dev_count)])

    inside = pl.BlockSpec(memory_space=pltpu.VMEM)
    own_cost = pl.CostEstimate(
        flops=8 * vec_count * row_count * per_block * tile_size,
        bytes_accessed=4 * tile_values.size + 12 * vec_count * row_count,
        transcendentals=0,
    )
    split = pltpu.VMEM((2 * vec_count, row_count), BF16)
    gram_shape = jax.ShapeDtypeStruct((vec_count, 2 * vec_count), F32)

    def rows_by(count, width):
        return jax.ShapeDtypeStruct((count, width), F32)

    full = rows_by(vec_count, row_count)

    def own_part(field, flipped):
        return pl.pallas_call(
            own_kernel,
            out_shape=full,
            in_specs=[SMEM] * 3 + [inside] * 4,
            out_specs=inside,
            scratch_shapes=[split],
            compiler_params=params,
            cost_estimate=own_cost,
            name="own",
        )(place, tile_cols, field_levels, field, flipped, tiles, targets)

    def own_gram(field, flipped):
        return pl.pallas_call(
            own_gram_kernel,
            out_shape=[gram_shape, full],
            in_specs=[SMEM] * 4 + [inside] * 4,
            out_specs=[inside, pl.BlockSpec(memory_space=pl.ANY)],
            scratch_shapes=[split, pltpu.SemaphoreType.DMA(())],
            compiler_params=params,
            cost_estimate=own_cost,
            name="own_gram",
        )(place, tile_cols, field_levels, live_rows, field, flipped, tiles, targets)

    three = [full, rows_by(vec_count // 2, row_count), rows_by(vec_count // 2, row_count)]

    def apply(field, first_half, second_half):
        legs = [(here, here ^ 2) for here in range(dev_count) if coupled(here, 1)]
        round_way = [(here, here ^ 4) for here in range(dev_count) if not coupled(here, 1)]
        flipped = exchange(field, 1)
        far = [hop(field, bond) for bond in reversed(range(2, bonds))]
        aside = lax.ppermute(lax.ppermute(second_half, AXES, legs), AXES, round_way)
        direct = hop(first_half, 1)
        closest = near(flipped)
        return own_part(field, flipped), far + [direct, aside, closest]

    start, *halves_of = pl.pallas_call(
        start_kernel,
        out_shape=three,
        in_specs=[SMEM, inside],
        out_specs=[inside] * 3,
        compiler_params=params,
        name="start",
    )(live_rows, vectors)
    own, hops = apply(start, *halves_of)
    first, *halves_of = pl.pallas_call(
        functools.partial(combine_kernel, bonds),
        out_shape=three,
        in_specs=[SMEM] * 2 + [inside] * (bonds + 2),
        out_specs=[inside] * 3,
        compiler_params=params,
        name="combine",
    )(place, live_rows, own, *hops)
    own, hops = apply(first, *halves_of)
    cut = row_count * 3 // 4
    kept, sent, lead, rest = pl.pallas_call(
        functools.partial(filter_kernel, bonds),
        out_shape=[full] + [rows_by(vec_count, width) for width in (row_count // 2, cut, row_count - cut)],
        in_specs=[SMEM] * 2 + [inside] * (bonds + 3),
        out_specs=[inside] * 4,
        compiler_params=params,
        name="filter",
    )(place, live_rows, own, start, *hops)
    flipped = exchange(kept, 1)
    hops = [one_way(lead, bond, 1) for bond in reversed(range(2, bonds))]
    flipped, sent, rest = lax.optimization_barrier((flipped, sent, rest))
    hops += [one_way(rest, bond, 0) for bond in reversed(range(2, bonds))]
    hops += [hop(sent, 0), hop(sent, 1)]
    grams, second = own_gram(kept, flipped)
    sums = pl.pallas_call(
        functools.partial(crossed_kernel, bonds, dev_count * row_count),
        out_shape=gram_shape,
        in_specs=[SMEM] + [inside] * (2 * bonds),
        out_specs=inside,
        compiler_params=params,
        name="crossed",
    )(place, grams, kept, *hops)
    for digit in range(bonds + 1):
        sums = sums + exchange(sums, 1 << digit)
    return (second, sums[:, :vec_count], sums[:, vec_count:])


def solution(mesh):
    in_specs = (
        P(None, ("groups", "hi", "lo")),
        P(("groups", "hi", "lo"), None, None),
        P(("hi", "lo")),
        P(("hi", "lo")),
        P(("hi", "lo")),
        P("groups"),
    )
    out_specs = (P(None, ("groups", "hi", "lo")), P("groups", None), P("groups", None))
    return jax.shard_map(local, mesh=mesh, in_specs=in_specs, out_specs=out_specs, check_vma=False)
```

```python
import functools

import jax
import jax.numpy as jnp
from jax import lax
from jax.experimental import pallas as pl
from jax.experimental.pallas import tpu as pltpu
from jax.sharding import PartitionSpec as P

HOP_SCALE = 0.5
ANISOTROPY = 1.0
FIELD_STEP = 0.25
HALF_WIDTH = 4.0
AXES = ("hi", "lo")
STEPS = 4
F32, BF16 = jnp.float32, jnp.bfloat16
SMEM = pl.BlockSpec(memory_space=pltpu.SMEM)
LIMIT = 32 * 1024 * 1024


def bit(number, place):
    return (number >> place) & 1


def halves(value):
    head = value.astype(BF16)
    return head, (value - head.astype(F32)).astype(BF16)


def stacked(value):
    return jnp.concatenate(halves(value), axis=0)


def product(left, right):
    rows, columns = left.shape[0] // 2, right.shape[0] // 2
    whole = lax.dot_general(left, right, (((1,), (1,)), ((), ())), preferred_element_type=F32)
    tails = whole[:rows, columns:] + whole[rows:, :columns] + whole[rows:, columns:]
    return whole[:rows, :columns] + tails


def coupling(config, bond):
    differ = bit(config, bond) ^ bit(config, bond + 1)
    return jnp.where(differ == 1, HOP_SCALE, 0.0)


def onsite_of(config, fields_ref):
    count = fields_ref.shape[0]
    spins = [bit(config, place).astype(F32) - 0.5 for place in range(count)]
    total = jnp.float32(0.0)
    for place in range(count):
        total += fields_ref[place].astype(F32) * FIELD_STEP * spins[place]
    for place in range(count - 1):
        total += ANISOTROPY * spins[place] * spins[place + 1]
    return total


def alive_of(live_ref, first, count):
    rows = lax.broadcasted_iota(jnp.int32, (1, count), 1) + first
    return (rows < live_ref[0]).astype(F32)


def own_block(block, config, cols_ref, fields_ref, field_ref, split_ref, flipped_ref, tiles_ref, map_ref):
    per_block, tile = tiles_ref.shape[1], tiles_ref.shape[2]
    span = pl.ds(pl.multiple_of(block * tile, tile), tile)
    picked = []
    for which in range(per_block):
        column = cols_ref[block * per_block + which]
        picked.append(split_ref[:, pl.ds(pl.multiple_of(column * tile, tile), tile)])
    weights = jnp.concatenate([tiles_ref[block, which] for which in range(per_block)], axis=1)
    total = product(jnp.concatenate(picked, axis=1), stacked(weights))
    total += onsite_of(config, fields_ref) * field_ref[:, span]
    targets = jnp.broadcast_to(map_ref[:, span], (8, tile))
    inside, outside = targets & (tile - 1), targets // tile
    outside = jnp.where(targets < 0, -1, outside)
    groups = []
    for group in range(field_ref.shape[0] // 8):
        found = jnp.zeros((8, tile), F32)
        for source in range(field_ref.shape[1] // tile):
            values = flipped_ref[group * 8 : group * 8 + 8, source * tile : (source + 1) * tile]
            moved = jnp.take_along_axis(values, inside, axis=1)
            found = jnp.where(outside == source, moved, found)
        groups.append(found)
    return span, total + HOP_SCALE * jnp.concatenate(groups, axis=0)


def own_kernel(place_ref, cols_ref, fields_ref, field_ref, flipped_ref, tiles_ref, map_ref, out_ref, split_ref):
    blocks = tiles_ref.shape[0] // STEPS
    split_ref[...] = stacked(field_ref[...])

    def body(step, carry):
        for row in range(blocks):
            span, total = own_block(
                step * blocks + row, place_ref[0], cols_ref, fields_ref, field_ref, split_ref, flipped_ref, tiles_ref, map_ref
            )
            out_ref[:, span] = total
        return carry

    lax.fori_loop(0, STEPS, body, 0)


def own_gram_kernel(
    place_ref, cols_ref, fields_ref, live_ref, field_ref, flipped_ref, tiles_ref, map_ref, out_ref, copy_ref, split_ref, sem
):
    blocks, tile = tiles_ref.shape[0] // STEPS, tiles_ref.shape[2]
    count, width = field_ref.shape[0], blocks * tile
    copy = pltpu.make_async_copy(field_ref, copy_ref, sem)
    copy.start()
    split_ref[...] = stacked(field_ref[...])
    out_ref[:, :count] = product(split_ref[...], split_ref[...])
    out_ref[:, count:] = jnp.zeros((count, count), F32)

    def body(step, carry):
        parts = []
        for row in range(blocks):
            block = step * blocks + row
            span, total = own_block(
                block, place_ref[0], cols_ref, fields_ref, field_ref, split_ref, flipped_ref, tiles_ref, map_ref
            )
            parts.append(alive_of(live_ref, block * tile, tile) * total)
        image = stacked(jnp.concatenate(parts, axis=1))
        span = pl.ds(pl.multiple_of(step * width, width), width)
        out_ref[:, count:] += product(split_ref[:, span], image)
        return carry

    lax.fori_loop(0, STEPS, body, 0)
    copy.wait()


def hop_sum(bonds, config, refs):
    total = coupling(config, 0) * refs[-1][...]
    total += coupling(config, 1) * jnp.concatenate([refs[-3][...], refs[-2][...]], axis=0)
    for bond, ref in zip(reversed(range(2, bonds)), refs):
        total += coupling(config, bond) * ref[...]
    return total


def store_halves(value, out_ref, first_ref, second_ref):
    middle = first_ref.shape[0]
    out_ref[...] = value
    first_ref[...] = value[:middle]
    second_ref[...] = value[middle:]


def start_kernel(live_ref, vectors_ref, out_ref, first_ref, second_ref):
    start = vectors_ref[...] * alive_of(live_ref, 0, vectors_ref.shape[1])
    store_halves(start, out_ref, first_ref, second_ref)


def combine_kernel(bonds, place_ref, live_ref, own_ref, *refs):
    hops, outs = refs[:-3], refs[-3:]
    total = own_ref[...] + hop_sum(bonds, place_ref[0], hops)
    store_halves(alive_of(live_ref, 0, total.shape[1]) * total * (1.0 / HALF_WIDTH), *outs)


def filter_kernel(bonds, place_ref, live_ref, own_ref, start_ref, *refs):
    hops, (kept_ref, sent_ref, lead_ref, rest_ref) = refs[:-4], refs[-4:]
    total = own_ref[...] + hop_sum(bonds, place_ref[0], hops)
    image = alive_of(live_ref, 0, total.shape[1]) * total * (1.0 / HALF_WIDTH)
    second = 2.0 * image - start_ref[...]
    kept_ref[...] = second
    lead_ref[...] = second[:, : lead_ref.shape[1]]
    rest_ref[...] = second[:, lead_ref.shape[1] :]
    width = sent_ref.shape[1]
    sent_ref[...] = jnp.where(place_ref[1] == 0, second[:, :width], second[:, width:])


def crossed_kernel(bonds, states, place_ref, own_ref, field_ref, *refs):
    hops, out_ref = refs[:-1], refs[-1]
    count = own_ref.shape[0]
    near = coupling(place_ref[0], 1) * hops[-1][...]
    theirs = jnp.where(place_ref[1] == 0, 0.0, near), jnp.where(place_ref[1] == 0, near, 0.0)
    theirs = jnp.concatenate(theirs, axis=1)
    for lead, rest in zip(hops, hops[bonds - 2 : -1]):
        theirs += HOP_SCALE * jnp.concatenate([lead[...], rest[...]], axis=1)
    crossed = product(stacked(field_ref[...]), stacked(theirs))
    out_ref[:, :count] = own_ref[:, :count] * (1.0 / states)
    projected = own_ref[:, count:] + crossed + crossed.T
    out_ref[:, count:] = projected * (1.0 / (HALF_WIDTH * states))


def local(vectors, tile_values, tile_cols, live_rows, boundary_map, field_levels):
    dev_count = lax.axis_size(AXES)
    bonds = dev_count.bit_length() - 2
    flip = (dev_count - 1) // 3
    position = lax.axis_index(AXES)
    parity = sum(bit(position, place) for place in range(0, bonds + 1, 2)) & 1
    place = jnp.stack([position ^ flip, parity]).astype(jnp.int32)
    vec_count, row_count = vectors.shape
    tile_size = tile_values.shape[1]
    block_count = row_count // tile_size
    per_block = tile_values.shape[0] // block_count
    tiles = tile_values.reshape(block_count, per_block, tile_size, tile_size)
    targets = boundary_map.reshape(1, row_count)
    params = pltpu.CompilerParams(vmem_limit_bytes=LIMIT)

    def coupled(here, bond):
        return bit(here ^ flip, bond) != bit(here ^ flip, bond + 1)

    def hop(value, bond):
        pairs = [(here, here ^ (3 << bond) if coupled(here, bond) else here) for here in range(dev_count)]
        return lax.ppermute(value, AXES, pairs)

    def one_way(value, bond, lead):
        pairs = []
        for here in range(dev_count):
            ahead = bit(here, bond) ^ bit(here, bond - 1) == lead
            if coupled(here, bond) and ahead:
                pairs.append((here, here ^ (3 << bond)))
            if bond == 2 and coupled(here, 0) and not ahead:
                pairs.append((here, here ^ 3))
        return lax.ppermute(value, AXES, pairs)

    def near(flipped):
        pairs = [(here, here ^ (1 if coupled(here, 0) else 2)) for here in range(dev_count)]
        return lax.ppermute(flipped, AXES, pairs)

    def exchange(value, mask):
        return lax.ppermute(value, AXES, [(source, source ^ mask) for source in range(dev_count)])

    inside = pl.BlockSpec(memory_space=pltpu.VMEM)
    own_cost = pl.CostEstimate(
        flops=8 * vec_count * row_count * per_block * tile_size,
        bytes_accessed=4 * tile_values.size + 12 * vec_count * row_count,
        transcendentals=0,
    )
    split = pltpu.VMEM((2 * vec_count, row_count), BF16)
    gram_shape = jax.ShapeDtypeStruct((vec_count, 2 * vec_count), F32)

    def rows_by(count, width):
        return jax.ShapeDtypeStruct((count, width), F32)

    full = rows_by(vec_count, row_count)

    def own_part(field, flipped):
        return pl.pallas_call(
            own_kernel,
            out_shape=full,
            in_specs=[SMEM] * 3 + [inside] * 4,
            out_specs=inside,
            scratch_shapes=[split],
            compiler_params=params,
            cost_estimate=own_cost,
            name="own",
        )(place, tile_cols, field_levels, field, flipped, tiles, targets)

    def own_gram(field, flipped):
        return pl.pallas_call(
            own_gram_kernel,
            out_shape=[gram_shape, full],
            in_specs=[SMEM] * 4 + [inside] * 4,
            out_specs=[inside, pl.BlockSpec(memory_space=pl.ANY)],
            scratch_shapes=[split, pltpu.SemaphoreType.DMA(())],
            compiler_params=params,
            cost_estimate=own_cost,
            name="own_gram",
        )(place, tile_cols, field_levels, live_rows, field, flipped, tiles, targets)

    three = [full, rows_by(vec_count // 2, row_count), rows_by(vec_count // 2, row_count)]

    def apply(field, first_half, second_half):
        legs = [(here, here ^ 2) for here in range(dev_count) if coupled(here, 1)]
        round_way = [(here, here ^ 4) for here in range(dev_count) if not coupled(here, 1)]
        flipped = exchange(field, 1)
        far = [hop(field, bond) for bond in reversed(range(2, bonds))]
        aside = lax.ppermute(lax.ppermute(second_half, AXES, legs), AXES, round_way)
        direct = hop(first_half, 1)
        closest = near(flipped)
        return own_part(field, flipped), far + [direct, aside, closest]

    start, *halves_of = pl.pallas_call(
        start_kernel,
        out_shape=three,
        in_specs=[SMEM, inside],
        out_specs=[inside] * 3,
        compiler_params=params,
        name="start",
    )(live_rows, vectors)
    own, hops = apply(start, *halves_of)
    first, *halves_of = pl.pallas_call(
        functools.partial(combine_kernel, bonds),
        out_shape=three,
        in_specs=[SMEM] * 2 + [inside] * (bonds + 2),
        out_specs=[inside] * 3,
        compiler_params=params,
        name="combine",
    )(place, live_rows, own, *hops)
    own, hops = apply(first, *halves_of)
    cut = row_count * 3 // 4
    kept, sent, lead, rest = pl.pallas_call(
        functools.partial(filter_kernel, bonds),
        out_shape=[full] + [rows_by(vec_count, width) for width in (row_count // 2, cut, row_count - cut)],
        in_specs=[SMEM] * 2 + [inside] * (bonds + 3),
        out_specs=[inside] * 4,
        compiler_params=params,
        name="filter",
    )(place, live_rows, own, start, *hops)
    flipped = exchange(kept, 1)
    hops = [one_way(lead, bond, 1) for bond in reversed(range(2, bonds))]
    flipped, sent, rest = lax.optimization_barrier((flipped, sent, rest))
    hops += [one_way(rest, bond, 0) for bond in reversed(range(2, bonds))]
    hops += [hop(sent, 1)]
    grams, second = own_gram(kept, flipped)
    sums = pl.pallas_call(
        functools.partial(crossed_kernel, bonds, dev_count * row_count),
        out_shape=gram_shape,
        in_specs=[SMEM] + [inside] * (2 * bonds - 1),
        out_specs=inside,
        compiler_params=params,
        name="crossed",
    )(place, grams, kept, *hops)
    for digit in range(bonds + 1):
        sums = sums + exchange(sums, 1 << digit)
    return (second, sums[:, :vec_count], sums[:, vec_count:])


def solution(mesh):
    in_specs = (
        P(None, ("groups", "hi", "lo")),
        P(("groups", "hi", "lo"), None, None),
        P(("hi", "lo")),
        P(("hi", "lo")),
        P(("hi", "lo")),
        P("groups"),
    )
    out_specs = (P(None, ("groups", "hi", "lo")), P("groups", None), P("groups", None))
    return jax.shard_map(local, mesh=mesh, in_specs=in_specs, out_specs=out_specs, check_vma=False)
```

```python
import functools

import jax
import jax.numpy as jnp
from jax import lax
from jax.experimental import pallas as pl
from jax.experimental.pallas import tpu as pltpu
from jax.sharding import PartitionSpec as P

HOP_SCALE = 0.5
ANISOTROPY = 1.0
FIELD_STEP = 0.25
HALF_WIDTH = 4.0
AXES = ("hi", "lo")
STEPS = 4
F32, BF16 = jnp.float32, jnp.bfloat16
SMEM = pl.BlockSpec(memory_space=pltpu.SMEM)
LIMIT = 32 * 1024 * 1024


def bit(number, place):
    return (number >> place) & 1


def halves(value):
    head = value.astype(BF16)
    return head, (value - head.astype(F32)).astype(BF16)


def stacked(value):
    return jnp.concatenate(halves(value), axis=0)


def product(left, right):
    rows, columns = left.shape[0] // 2, right.shape[0] // 2
    whole = lax.dot_general(left, right, (((1,), (1,)), ((), ())), preferred_element_type=F32)
    tails = whole[:rows, columns:] + whole[rows:, :columns] + whole[rows:, columns:]
    return whole[:rows, :columns] + tails


def coupling(config, bond):
    differ = bit(config, bond) ^ bit(config, bond + 1)
    return jnp.where(differ == 1, HOP_SCALE, 0.0)


def onsite_of(config, fields_ref):
    count = fields_ref.shape[0]
    spins = [bit(config, place).astype(F32) - 0.5 for place in range(count)]
    total = jnp.float32(0.0)
    for place in range(count):
        total += fields_ref[place].astype(F32) * FIELD_STEP * spins[place]
    for place in range(count - 1):
        total += ANISOTROPY * spins[place] * spins[place + 1]
    return total


def alive_of(live_ref, first, count):
    rows = lax.broadcasted_iota(jnp.int32, (1, count), 1) + first
    return (rows < live_ref[0]).astype(F32)


def own_block(block, config, cols_ref, fields_ref, field_ref, split_ref, flipped_ref, tiles_ref, map_ref):
    per_block, tile = tiles_ref.shape[1], tiles_ref.shape[2]
    span = pl.ds(pl.multiple_of(block * tile, tile), tile)
    picked = []
    for which in range(per_block):
        column = cols_ref[block * per_block + which]
        picked.append(split_ref[:, pl.ds(pl.multiple_of(column * tile, tile), tile)])
    weights = jnp.concatenate([tiles_ref[block, which] for which in range(per_block)], axis=1)
    total = product(jnp.concatenate(picked, axis=1), stacked(weights))
    total += onsite_of(config, fields_ref) * field_ref[:, span]
    targets = jnp.broadcast_to(map_ref[:, span], (8, tile))
    inside, outside = targets & (tile - 1), targets // tile
    outside = jnp.where(targets < 0, -1, outside)
    groups = []
    for group in range(field_ref.shape[0] // 8):
        found = jnp.zeros((8, tile), F32)
        for source in range(field_ref.shape[1] // tile):
            values = flipped_ref[group * 8 : group * 8 + 8, source * tile : (source + 1) * tile]
            moved = jnp.take_along_axis(values, inside, axis=1)
            found = jnp.where(outside == source, moved, found)
        groups.append(found)
    return span, total + HOP_SCALE * jnp.concatenate(groups, axis=0)


def own_kernel(place_ref, cols_ref, fields_ref, field_ref, flipped_ref, tiles_ref, map_ref, out_ref, split_ref):
    blocks = tiles_ref.shape[0] // STEPS
    split_ref[...] = stacked(field_ref[...])

    def body(step, carry):
        for row in range(blocks):
            span, total = own_block(
                step * blocks + row, place_ref[0], cols_ref, fields_ref, field_ref, split_ref, flipped_ref, tiles_ref, map_ref
            )
            out_ref[:, span] = total
        return carry

    lax.fori_loop(0, STEPS, body, 0)


def own_gram_kernel(
    place_ref, cols_ref, fields_ref, live_ref, field_ref, flipped_ref, tiles_ref, map_ref, out_ref, copy_ref, split_ref, sem
):
    blocks, tile = tiles_ref.shape[0] // STEPS, tiles_ref.shape[2]
    count, width = field_ref.shape[0], blocks * tile
    copy = pltpu.make_async_copy(field_ref, copy_ref, sem)
    copy.start()
    split_ref[...] = stacked(field_ref[...])
    out_ref[:, :count] = product(split_ref[...], split_ref[...])
    out_ref[:, count:] = jnp.zeros((count, count), F32)

    def body(step, carry):
        parts = []
        for row in range(blocks):
            block = step * blocks + row
            span, total = own_block(
                block, place_ref[0], cols_ref, fields_ref, field_ref, split_ref, flipped_ref, tiles_ref, map_ref
            )
            parts.append(alive_of(live_ref, block * tile, tile) * total)
        image = stacked(jnp.concatenate(parts, axis=1))
        span = pl.ds(pl.multiple_of(step * width, width), width)
        out_ref[:, count:] += product(split_ref[:, span], image)
        return carry

    lax.fori_loop(0, STEPS, body, 0)
    copy.wait()


def hop_sum(bonds, config, refs):
    total = coupling(config, 0) * refs[-1][...]
    total += coupling(config, 1) * jnp.concatenate([refs[-3][...], refs[-2][...]], axis=0)
    for bond, ref in zip(reversed(range(2, bonds)), refs):
        total += coupling(config, bond) * ref[...]
    return total


def store_halves(value, out_ref, first_ref, second_ref):
    middle = first_ref.shape[0]
    out_ref[...] = value
    first_ref[...] = value[:middle]
    second_ref[...] = value[middle:]


def start_kernel(live_ref, vectors_ref, out_ref, first_ref, second_ref):
    start = vectors_ref[...] * alive_of(live_ref, 0, vectors_ref.shape[1])
    store_halves(start, out_ref, first_ref, second_ref)


def combine_kernel(bonds, place_ref, live_ref, own_ref, *refs):
    hops, outs = refs[:-3], refs[-3:]
    total = own_ref[...] + hop_sum(bonds, place_ref[0], hops)
    store_halves(alive_of(live_ref, 0, total.shape[1]) * total * (1.0 / HALF_WIDTH), *outs)


def filter_kernel(bonds, place_ref, live_ref, own_ref, start_ref, *refs):
    hops, (kept_ref, sent_ref, lead_ref, rest_ref) = refs[:-4], refs[-4:]
    total = own_ref[...] + hop_sum(bonds, place_ref[0], hops)
    image = alive_of(live_ref, 0, total.shape[1]) * total * (1.0 / HALF_WIDTH)
    second = 2.0 * image - start_ref[...]
    kept_ref[...] = second
    lead_ref[...] = second[:, : lead_ref.shape[1]]
    rest_ref[...] = second[:, lead_ref.shape[1] :]
    width = sent_ref.shape[1]
    sent_ref[...] = jnp.where(place_ref[1] == 0, second[:, :width], second[:, width:])


def crossed_kernel(bonds, states, place_ref, own_ref, field_ref, *refs):
    hops, out_ref = refs[:-1], refs[-1]
    count = own_ref.shape[0]
    near = coupling(place_ref[0], 1) * hops[-1][...]
    theirs = jnp.where(place_ref[1] == 0, 0.0, near), jnp.where(place_ref[1] == 0, near, 0.0)
    theirs = jnp.concatenate(theirs, axis=1)
    for lead, rest in zip(hops, hops[bonds - 2 : -1]):
        theirs += HOP_SCALE * jnp.concatenate([lead[...], rest[...]], axis=1)
    crossed = product(stacked(field_ref[...]), stacked(theirs))
    out_ref[:, :count] = own_ref[:, :count] * (1.0 / states)
    projected = own_ref[:, count:] + crossed + crossed.T
    out_ref[:, count:] = projected * (1.0 / (HALF_WIDTH * states))


def local(vectors, tile_values, tile_cols, live_rows, boundary_map, field_levels):
    dev_count = lax.axis_size(AXES)
    bonds = dev_count.bit_length() - 2
    flip = (dev_count - 1) // 3
    position = lax.axis_index(AXES)
    parity = sum(bit(position, place) for place in range(0, bonds + 1, 2)) & 1
    place = jnp.stack([position ^ flip, parity]).astype(jnp.int32)
    vec_count, row_count = vectors.shape
    tile_size = tile_values.shape[1]
    block_count = row_count // tile_size
    per_block = tile_values.shape[0] // block_count
    tiles = tile_values.reshape(block_count, per_block, tile_size, tile_size)
    targets = boundary_map.reshape(1, row_count)
    params = pltpu.CompilerParams(vmem_limit_bytes=LIMIT)

    def coupled(here, bond):
        return bit(here ^ flip, bond) != bit(here ^ flip, bond + 1)

    def hop(value, bond):
        pairs = [(here, here ^ (3 << bond) if coupled(here, bond) else here) for here in range(dev_count)]
        return lax.ppermute(value, AXES, pairs)

    def one_way(value, bond, lead):
        pairs = []
        for here in range(dev_count):
            ahead = bit(here, bond) ^ bit(here, bond - 1) == lead
            if coupled(here, bond) and ahead:
                pairs.append((here, here ^ (3 << bond)))
            if bond == 2 and coupled(here, 0) and not ahead:
                pairs.append((here, here ^ 3))
        return lax.ppermute(value, AXES, pairs)

    def near(flipped):
        pairs = [(here, here ^ (1 if coupled(here, 0) else 2)) for here in range(dev_count)]
        return lax.ppermute(flipped, AXES, pairs)

    def exchange(value, mask):
        return lax.ppermute(value, AXES, [(source, source ^ mask) for source in range(dev_count)])

    inside = pl.BlockSpec(memory_space=pltpu.VMEM)
    own_cost = pl.CostEstimate(
        flops=8 * vec_count * row_count * per_block * tile_size,
        bytes_accessed=4 * tile_values.size + 12 * vec_count * row_count,
        transcendentals=0,
    )
    split = pltpu.VMEM((2 * vec_count, row_count), BF16)
    gram_shape = jax.ShapeDtypeStruct((vec_count, 2 * vec_count), F32)

    def rows_by(count, width):
        return jax.ShapeDtypeStruct((count, width), F32)

    full = rows_by(vec_count, row_count)

    def own_part(field, flipped):
        return pl.pallas_call(
            own_kernel,
            out_shape=full,
            in_specs=[SMEM] * 3 + [inside] * 4,
            out_specs=inside,
            scratch_shapes=[split],
            compiler_params=params,
            cost_estimate=own_cost,
            name="own",
        )(place, tile_cols, field_levels, field, flipped, tiles, targets)

    def own_gram(field, flipped):
        return pl.pallas_call(
            own_gram_kernel,
            out_shape=[gram_shape, full],
            in_specs=[SMEM] * 4 + [inside] * 4,
            out_specs=[inside, pl.BlockSpec(memory_space=pl.ANY)],
            scratch_shapes=[split, pltpu.SemaphoreType.DMA(())],
            compiler_params=params,
            cost_estimate=own_cost,
            name="own_gram",
        )(place, tile_cols, field_levels, live_rows, field, flipped, tiles, targets)

    three = [full, rows_by(vec_count // 2, row_count), rows_by(vec_count // 2, row_count)]

    def apply(field, first_half, second_half):
        legs = [(here, here ^ 2) for here in range(dev_count) if coupled(here, 1)]
        round_way = [(here, here ^ 4) for here in range(dev_count) if not coupled(here, 1)]
        flipped = exchange(field, 1)
        far = [hop(field, bond) for bond in reversed(range(2, bonds))]
        aside = lax.ppermute(lax.ppermute(second_half, AXES, legs), AXES, round_way)
        direct = hop(first_half, 1)
        closest = near(flipped)
        return own_part(field, flipped), far + [direct, aside, closest]

    start, *halves_of = pl.pallas_call(
        start_kernel,
        out_shape=three,
        in_specs=[SMEM, inside],
        out_specs=[inside] * 3,
        compiler_params=params,
        name="start",
    )(live_rows, vectors)
    own, hops = apply(start, *halves_of)
    first, *halves_of = pl.pallas_call(
        functools.partial(combine_kernel, bonds),
        out_shape=three,
        in_specs=[SMEM] * 2 + [inside] * (bonds + 2),
        out_specs=[inside] * 3,
        compiler_params=params,
        name="combine",
    )(place, live_rows, own, *hops)
    own, hops = apply(first, *halves_of)
    cut = row_count * 3 // 4
    kept, sent, lead, rest = pl.pallas_call(
        functools.partial(filter_kernel, bonds),
        out_shape=[full] + [rows_by(vec_count, width) for width in (row_count // 2, cut, row_count - cut)],
        in_specs=[SMEM] * 2 + [inside] * (bonds + 3),
        out_specs=[inside] * 4,
        compiler_params=params,
        name="filter",
    )(place, live_rows, own, start, *hops)
    flipped = exchange(kept, 1)
    hops = [one_way(lead, bond, 1) for bond in reversed(range(2, bonds))]
    flipped, sent, rest = lax.optimization_barrier((flipped, sent, rest))
    hops += [one_way(rest, bond, 0) for bond in reversed(range(2, bonds))]
    hops += [hop(sent, 1)]
    grams, second = own_gram(kept, flipped)
    sums = pl.pallas_call(
        functools.partial(crossed_kernel, bonds, dev_count * row_count),
        out_shape=gram_shape,
        in_specs=[SMEM] + [inside] * (2 * bonds - 1),
        out_specs=inside,
        compiler_params=params,
        name="crossed",
    )(place, grams, kept, *hops)
    sums = sums + exchange(sums, 1)
    for digit in range(1, bonds + 1, 2):
        near_mask, far_mask = 1 << digit, 2 << digit
        pair = sums + exchange(sums, near_mask)
        if far_mask < dev_count:
            pair = pair + (exchange(sums, far_mask) + exchange(sums, near_mask | far_mask))
        sums = pair
    return (second, sums[:, :vec_count], sums[:, vec_count:])


def solution(mesh):
    in_specs = (
        P(None, ("groups", "hi", "lo")),
        P(("groups", "hi", "lo"), None, None),
        P(("hi", "lo")),
        P(("hi", "lo")),
        P(("hi", "lo")),
        P("groups"),
    )
    out_specs = (P(None, ("groups", "hi", "lo")), P("groups", None), P("groups", None))
    return jax.shard_map(local, mesh=mesh, in_specs=in_specs, out_specs=out_specs, check_vma=False)
```

```python
import functools

import jax
import jax.numpy as jnp
from jax import lax
from jax.experimental import pallas as pl
from jax.experimental.pallas import tpu as pltpu
from jax.sharding import PartitionSpec as P

HOP_SCALE = 0.5
ANISOTROPY = 1.0
FIELD_STEP = 0.25
HALF_WIDTH = 4.0
AXES = ("hi", "lo")
STEPS = 4
F32, BF16 = jnp.float32, jnp.bfloat16
SMEM = pl.BlockSpec(memory_space=pltpu.SMEM)
LIMIT = 32 * 1024 * 1024


def bit(number, place):
    return (number >> place) & 1


def halves(value):
    head = value.astype(BF16)
    return head, (value - head.astype(F32)).astype(BF16)


def stacked(value):
    return jnp.concatenate(halves(value), axis=0)


def product(left, right):
    rows, columns = left.shape[0] // 2, right.shape[0] // 2
    whole = lax.dot_general(left, right, (((1,), (1,)), ((), ())), preferred_element_type=F32)
    tails = whole[:rows, columns:] + whole[rows:, :columns] + whole[rows:, columns:]
    return whole[:rows, :columns] + tails


def coupling(config, bond):
    differ = bit(config, bond) ^ bit(config, bond + 1)
    return jnp.where(differ == 1, HOP_SCALE, 0.0)


def onsite_of(config, fields_ref):
    count = fields_ref.shape[0]
    spins = [bit(config, place).astype(F32) - 0.5 for place in range(count)]
    total = jnp.float32(0.0)
    for place in range(count):
        total += fields_ref[place].astype(F32) * FIELD_STEP * spins[place]
    for place in range(count - 1):
        total += ANISOTROPY * spins[place] * spins[place + 1]
    return total


def alive_of(live_ref, first, count):
    rows = lax.broadcasted_iota(jnp.int32, (1, count), 1) + first
    return (rows < live_ref[0]).astype(F32)


def own_block(block, config, cols_ref, fields_ref, field_ref, split_ref, flipped_ref, tiles_ref, map_ref):
    per_block, tile = tiles_ref.shape[1], tiles_ref.shape[2]
    span = pl.ds(pl.multiple_of(block * tile, tile), tile)
    picked = []
    for which in range(per_block):
        column = cols_ref[block * per_block + which]
        picked.append(split_ref[:, pl.ds(pl.multiple_of(column * tile, tile), tile)])
    weights = jnp.concatenate([tiles_ref[block, which] for which in range(per_block)], axis=1)
    total = product(jnp.concatenate(picked, axis=1), stacked(weights))
    total += onsite_of(config, fields_ref) * field_ref[:, span]
    targets = jnp.broadcast_to(map_ref[:, span], (8, tile))
    inside, outside = targets & (tile - 1), targets // tile
    outside = jnp.where(targets < 0, -1, outside)
    groups = []
    for group in range(field_ref.shape[0] // 8):
        found = jnp.zeros((8, tile), F32)
        for source in range(field_ref.shape[1] // tile):
            values = flipped_ref[group * 8 : group * 8 + 8, source * tile : (source + 1) * tile]
            moved = jnp.take_along_axis(values, inside, axis=1)
            found = jnp.where(outside == source, moved, found)
        groups.append(found)
    return span, total + HOP_SCALE * jnp.concatenate(groups, axis=0)


def own_kernel(place_ref, cols_ref, fields_ref, field_ref, flipped_ref, tiles_ref, map_ref, out_ref, split_ref):
    blocks = tiles_ref.shape[0] // STEPS
    split_ref[...] = stacked(field_ref[...])

    def body(step, carry):
        for row in range(blocks):
            span, total = own_block(
                step * blocks + row, place_ref[0], cols_ref, fields_ref, field_ref, split_ref, flipped_ref, tiles_ref, map_ref
            )
            out_ref[:, span] = total
        return carry

    lax.fori_loop(0, STEPS, body, 0)


def own_gram_kernel(
    place_ref, cols_ref, fields_ref, live_ref, field_ref, flipped_ref, tiles_ref, map_ref, out_ref, copy_ref, split_ref, sem
):
    blocks, tile = tiles_ref.shape[0] // STEPS, tiles_ref.shape[2]
    count, width = field_ref.shape[0], blocks * tile
    copy = pltpu.make_async_copy(field_ref, copy_ref, sem)
    copy.start()
    split_ref[...] = stacked(field_ref[...])
    out_ref[:, :count] = product(split_ref[...], split_ref[...])
    out_ref[:, count:] = jnp.zeros((count, count), F32)

    def body(step, carry):
        parts = []
        for row in range(blocks):
            block = step * blocks + row
            span, total = own_block(
                block, place_ref[0], cols_ref, fields_ref, field_ref, split_ref, flipped_ref, tiles_ref, map_ref
            )
            parts.append(alive_of(live_ref, block * tile, tile) * total)
        image = stacked(jnp.concatenate(parts, axis=1))
        span = pl.ds(pl.multiple_of(step * width, width), width)
        out_ref[:, count:] += product(split_ref[:, span], image)
        return carry

    lax.fori_loop(0, STEPS, body, 0)
    copy.wait()


def far_kernel(bonds, place_ref, own_ref, *refs):
    total = own_ref[...]
    for bond, ref in zip(reversed(range(2, bonds)), refs):
        total += coupling(place_ref[0], bond) * ref[...]
    refs[-1][...] = total


def hop_sum(config, refs):
    total = coupling(config, 0) * refs[-1][...]
    return total + coupling(config, 1) * jnp.concatenate([refs[0][...], refs[1][...]], axis=0)


def store_halves(value, out_ref, first_ref, second_ref):
    middle = first_ref.shape[0]
    out_ref[...] = value
    first_ref[...] = value[:middle]
    second_ref[...] = value[middle:]


def start_kernel(live_ref, vectors_ref, out_ref, first_ref, second_ref):
    start = vectors_ref[...] * alive_of(live_ref, 0, vectors_ref.shape[1])
    store_halves(start, out_ref, first_ref, second_ref)


def combine_kernel(place_ref, live_ref, own_ref, *refs):
    hops, outs = refs[:-3], refs[-3:]
    total = own_ref[...] + hop_sum(place_ref[0], hops)
    store_halves(alive_of(live_ref, 0, total.shape[1]) * total * (1.0 / HALF_WIDTH), *outs)


def filter_kernel(place_ref, live_ref, own_ref, start_ref, *refs):
    hops, (kept_ref, sent_ref, lead_ref, rest_ref) = refs[:-4], refs[-4:]
    total = own_ref[...] + hop_sum(place_ref[0], hops)
    image = alive_of(live_ref, 0, total.shape[1]) * total * (1.0 / HALF_WIDTH)
    second = 2.0 * image - start_ref[...]
    kept_ref[...] = second
    lead_ref[...] = second[:, : lead_ref.shape[1]]
    rest_ref[...] = second[:, lead_ref.shape[1] :]
    width = sent_ref.shape[1]
    sent_ref[...] = jnp.where(place_ref[1] == 0, second[:, :width], second[:, width:])


def crossed_kernel(bonds, states, place_ref, own_ref, field_ref, *refs):
    hops, out_ref = refs[:-1], refs[-1]
    count = own_ref.shape[0]
    near = coupling(place_ref[0], 1) * hops[-1][...]
    theirs = jnp.where(place_ref[1] == 0, 0.0, near), jnp.where(place_ref[1] == 0, near, 0.0)
    theirs = jnp.concatenate(theirs, axis=1)
    for lead, rest in zip(hops, hops[bonds - 2 : -1]):
        theirs += HOP_SCALE * jnp.concatenate([lead[...], rest[...]], axis=1)
    crossed = product(stacked(field_ref[...]), stacked(theirs))
    out_ref[:, :count] = own_ref[:, :count] * (1.0 / states)
    projected = own_ref[:, count:] + crossed + crossed.T
    out_ref[:, count:] = projected * (1.0 / (HALF_WIDTH * states))


def local(vectors, tile_values, tile_cols, live_rows, boundary_map, field_levels):
    dev_count = lax.axis_size(AXES)
    bonds = dev_count.bit_length() - 2
    flip = (dev_count - 1) // 3
    position = lax.axis_index(AXES)
    parity = sum(bit(position, place) for place in range(0, bonds + 1, 2)) & 1
    place = jnp.stack([position ^ flip, parity]).astype(jnp.int32)
    vec_count, row_count = vectors.shape
    tile_size = tile_values.shape[1]
    block_count = row_count // tile_size
    per_block = tile_values.shape[0] // block_count
    tiles = tile_values.reshape(block_count, per_block, tile_size, tile_size)
    targets = boundary_map.reshape(1, row_count)
    params = pltpu.CompilerParams(vmem_limit_bytes=LIMIT)

    def coupled(here, bond):
        return bit(here ^ flip, bond) != bit(here ^ flip, bond + 1)

    def hop(value, bond):
        pairs = [(here, here ^ (3 << bond) if coupled(here, bond) else here) for here in range(dev_count)]
        return lax.ppermute(value, AXES, pairs)

    def one_way(value, bond, lead):
        pairs = []
        for here in range(dev_count):
            ahead = bit(here, bond) ^ bit(here, bond - 1) == lead
            if coupled(here, bond) and ahead:
                pairs.append((here, here ^ (3 << bond)))
            if bond == 2 and coupled(here, 0) and not ahead:
                pairs.append((here, here ^ 3))
        return lax.ppermute(value, AXES, pairs)

    def near(flipped):
        pairs = [(here, here ^ (1 if coupled(here, 0) else 2)) for here in range(dev_count)]
        return lax.ppermute(flipped, AXES, pairs)

    def exchange(value, mask):
        return lax.ppermute(value, AXES, [(source, source ^ mask) for source in range(dev_count)])

    inside = pl.BlockSpec(memory_space=pltpu.VMEM)
    own_cost = pl.CostEstimate(
        flops=8 * vec_count * row_count * per_block * tile_size,
        bytes_accessed=4 * tile_values.size + 12 * vec_count * row_count,
        transcendentals=0,
    )
    split = pltpu.VMEM((2 * vec_count, row_count), BF16)
    gram_shape = jax.ShapeDtypeStruct((vec_count, 2 * vec_count), F32)

    def rows_by(count, width):
        return jax.ShapeDtypeStruct((count, width), F32)

    full = rows_by(vec_count, row_count)

    def own_part(field, flipped):
        return pl.pallas_call(
            own_kernel,
            out_shape=full,
            in_specs=[SMEM] * 3 + [inside] * 4,
            out_specs=inside,
            scratch_shapes=[split],
            compiler_params=params,
            cost_estimate=own_cost,
            name="own",
        )(place, tile_cols, field_levels, field, flipped, tiles, targets)

    def own_gram(field, flipped):
        return pl.pallas_call(
            own_gram_kernel,
            out_shape=[gram_shape, full],
            in_specs=[SMEM] * 4 + [inside] * 4,
            out_specs=[inside, pl.BlockSpec(memory_space=pl.ANY)],
            scratch_shapes=[split, pltpu.SemaphoreType.DMA(())],
            compiler_params=params,
            cost_estimate=own_cost,
            name="own_gram",
        )(place, tile_cols, field_levels, live_rows, field, flipped, tiles, targets)

    three = [full, rows_by(vec_count // 2, row_count), rows_by(vec_count // 2, row_count)]

    def apply(field, first_half, second_half):
        legs = [(here, here ^ 2) for here in range(dev_count) if coupled(here, 1)]
        round_way = [(here, here ^ 4) for here in range(dev_count) if not coupled(here, 1)]
        flipped = exchange(field, 1)
        far = [hop(field, bond) for bond in reversed(range(2, bonds))]
        aside = lax.ppermute(lax.ppermute(second_half, AXES, legs), AXES, round_way)
        direct = hop(first_half, 1)
        closest = near(flipped)
        total = pl.pallas_call(
            functools.partial(far_kernel, bonds),
            out_shape=full,
            in_specs=[SMEM] + [inside] * (bonds - 1),
            out_specs=inside,
            input_output_aliases={1: 0},
            compiler_params=params,
            cost_estimate=pl.CostEstimate(flops=vec_count * row_count, bytes_accessed=12 * vec_count * row_count, transcendentals=0),
            name="far",
        )(place, own_part(field, flipped), *far)
        return total, [direct, aside, closest]

    start, *halves_of = pl.pallas_call(
        start_kernel,
        out_shape=three,
        in_specs=[SMEM, inside],
        out_specs=[inside] * 3,
        compiler_params=params,
        name="start",
    )(live_rows, vectors)
    own, hops = apply(start, *halves_of)
    first, *halves_of = pl.pallas_call(
        combine_kernel,
        out_shape=three,
        in_specs=[SMEM] * 2 + [inside] * 4,
        out_specs=[inside] * 3,
        compiler_params=params,
        name="combine",
    )(place, live_rows, own, *hops)
    own, hops = apply(first, *halves_of)
    cut = row_count * 3 // 4
    kept, sent, lead, rest = pl.pallas_call(
        filter_kernel,
        out_shape=[full] + [rows_by(vec_count, width) for width in (row_count // 2, cut, row_count - cut)],
        in_specs=[SMEM] * 2 + [inside] * 5,
        out_specs=[inside] * 4,
        compiler_params=params,
        name="filter",
    )(place, live_rows, own, start, *hops)
    flipped = exchange(kept, 1)
    hops = [one_way(lead, bond, 1) for bond in reversed(range(2, bonds))]
    flipped, sent, rest = lax.optimization_barrier((flipped, sent, rest))
    hops += [one_way(rest, bond, 0) for bond in reversed(range(2, bonds))]
    hops += [hop(sent, 1)]
    grams, second = own_gram(kept, flipped)
    sums = pl.pallas_call(
        functools.partial(crossed_kernel, bonds, dev_count * row_count),
        out_shape=gram_shape,
        in_specs=[SMEM] + [inside] * (2 * bonds - 1),
        out_specs=inside,
        compiler_params=params,
        name="crossed",
    )(place, grams, kept, *hops)
    sums = sums + exchange(sums, 1)
    for digit in range(1, bonds + 1, 2):
        near_mask, far_mask = 1 << digit, 2 << digit
        pair = sums + exchange(sums, near_mask)
        if far_mask < dev_count:
            pair = pair + (exchange(sums, far_mask) + exchange(sums, near_mask | far_mask))
        sums = pair
    return (second, sums[:, :vec_count], sums[:, vec_count:])


def solution(mesh):
    in_specs = (
        P(None, ("groups", "hi", "lo")),
        P(("groups", "hi", "lo"), None, None),
        P(("hi", "lo")),
        P(("hi", "lo")),
        P(("hi", "lo")),
        P("groups"),
    )
    out_specs = (P(None, ("groups", "hi", "lo")), P("groups", None), P("groups", None))
    return jax.shard_map(local, mesh=mesh, in_specs=in_specs, out_specs=out_specs, check_vma=False)
```

```python
import functools

import jax
import jax.numpy as jnp
from jax import lax
from jax.experimental import pallas as pl
from jax.experimental.pallas import tpu as pltpu
from jax.sharding import PartitionSpec as P

HOP_SCALE = 0.5
ANISOTROPY = 1.0
FIELD_STEP = 0.25
HALF_WIDTH = 4.0
AXES = ("hi", "lo")
STEPS = 4
F32, BF16 = jnp.float32, jnp.bfloat16
SMEM = pl.BlockSpec(memory_space=pltpu.SMEM)
LIMIT = 32 * 1024 * 1024
FIRST_LIMIT = 50 * 1024 * 1024


class Part:
    def __init__(self, ref, begin, count):
        self.ref, self.begin, self.shape = ref, begin, (count,)

    def __getitem__(self, index):
        return self.ref[self.begin + index]


def parts_of(table_ref, field_count):
    fields = Part(table_ref, 2, field_count)
    return table_ref, Part(table_ref, 2 + field_count, table_ref.shape[0] - 2 - field_count), fields


def bit(number, place):
    return (number >> place) & 1


def halves(value):
    head = value.astype(BF16)
    return head, (value - head.astype(F32)).astype(BF16)


def stacked(value):
    return jnp.concatenate(halves(value), axis=0)


def product(left, right):
    rows, columns = left.shape[0] // 2, right.shape[0] // 2
    whole = lax.dot_general(left, right, (((1,), (1,)), ((), ())), preferred_element_type=F32)
    tails = whole[:rows, columns:] + whole[rows:, :columns] + whole[rows:, columns:]
    return whole[:rows, :columns] + tails


def coupling(config, bond):
    differ = bit(config, bond) ^ bit(config, bond + 1)
    return jnp.where(differ == 1, HOP_SCALE, 0.0)


def onsite_of(config, fields_ref):
    count = fields_ref.shape[0]
    spins = [bit(config, place).astype(F32) - 0.5 for place in range(count)]
    total = jnp.float32(0.0)
    for place in range(count):
        total += fields_ref[place].astype(F32) * FIELD_STEP * spins[place]
    for place in range(count - 1):
        total += ANISOTROPY * spins[place] * spins[place + 1]
    return total


def alive_of(live_ref, first, count):
    rows = lax.broadcasted_iota(jnp.int32, (1, count), 1) + first
    return (rows < live_ref[0]).astype(F32)


def own_block(block, config, cols_ref, fields_ref, field_ref, split_ref, flipped_ref, tiles_ref, map_ref):
    per_block, tile = tiles_ref.shape[1], tiles_ref.shape[2]
    span = pl.ds(pl.multiple_of(block * tile, tile), tile)
    picked = []
    for which in range(per_block):
        column = cols_ref[block * per_block + which]
        picked.append(split_ref[:, pl.ds(pl.multiple_of(column * tile, tile), tile)])
    weights = jnp.concatenate([tiles_ref[block, which] for which in range(per_block)], axis=1)
    total = product(jnp.concatenate(picked, axis=1), stacked(weights))
    total += onsite_of(config, fields_ref) * field_ref[:, span]
    targets = jnp.broadcast_to(map_ref[:, span], (8, tile))
    inside, outside = targets & (tile - 1), targets // tile
    outside = jnp.where(targets < 0, -1, outside)
    groups = []
    for group in range(field_ref.shape[0] // 8):
        found = jnp.zeros((8, tile), F32)
        for source in range(field_ref.shape[1] // tile):
            values = flipped_ref[group * 8 : group * 8 + 8, source * tile : (source + 1) * tile]
            moved = jnp.take_along_axis(values, inside, axis=1)
            found = jnp.where(outside == source, moved, found)
        groups.append(found)
    return span, total + HOP_SCALE * jnp.concatenate(groups, axis=0)


def first_own_kernel(
    field_count, table_ref, field_ref, flipped_ref, far_tiles, map_ref, out_ref, split_ref, tiles_ref, sems
):
    place_ref, cols_ref, fields_ref = parts_of(table_ref, field_count)
    blocks = tiles_ref.shape[0] // STEPS
    fetched = []
    for step in range(STEPS):
        span = pl.ds(step * blocks, blocks)
        fetched.append(pltpu.make_async_copy(far_tiles.at[span], tiles_ref.at[span], sems.at[step]))
    for copy in fetched:
        copy.start()
    split_ref[...] = stacked(field_ref[...])
    for step in range(STEPS):
        fetched[step].wait()
        for row in range(blocks):
            span, total = own_block(
                step * blocks + row, place_ref[0], cols_ref, fields_ref, field_ref, split_ref, flipped_ref, tiles_ref, map_ref
            )
            out_ref[:, span] = total


def own_kernel(field_count, table_ref, field_ref, flipped_ref, tiles_ref, map_ref, out_ref, split_ref):
    place_ref, cols_ref, fields_ref = parts_of(table_ref, field_count)
    blocks = tiles_ref.shape[0] // STEPS
    split_ref[...] = stacked(field_ref[...])

    def body(step, carry):
        for row in range(blocks):
            span, total = own_block(
                step * blocks + row, place_ref[0], cols_ref, fields_ref, field_ref, split_ref, flipped_ref, tiles_ref, map_ref
            )
            out_ref[:, span] = total
        return carry

    lax.fori_loop(0, STEPS, body, 0)


def own_gram_kernel(
    field_count, table_ref, live_ref, field_ref, flipped_ref, tiles_ref, map_ref, out_ref, copy_ref, split_ref, sem
):
    place_ref, cols_ref, fields_ref = parts_of(table_ref, field_count)
    blocks, tile = tiles_ref.shape[0] // STEPS, tiles_ref.shape[2]
    count, width = field_ref.shape[0], blocks * tile
    copy = pltpu.make_async_copy(field_ref, copy_ref, sem)
    copy.start()
    split_ref[...] = stacked(field_ref[...])
    out_ref[:, :count] = product(split_ref[...], split_ref[...])
    out_ref[:, count:] = jnp.zeros((count, count), F32)

    def body(step, carry):
        parts = []
        for row in range(blocks):
            block = step * blocks + row
            span, total = own_block(
                block, place_ref[0], cols_ref, fields_ref, field_ref, split_ref, flipped_ref, tiles_ref, map_ref
            )
            parts.append(alive_of(live_ref, block * tile, tile) * total)
        image = stacked(jnp.concatenate(parts, axis=1))
        span = pl.ds(pl.multiple_of(step * width, width), width)
        out_ref[:, count:] += product(split_ref[:, span], image)
        return carry

    lax.fori_loop(0, STEPS, body, 0)
    copy.wait()


def far_kernel(bonds, place_ref, own_ref, *refs):
    total = own_ref[...]
    for bond, ref in zip(reversed(range(2, bonds)), refs):
        total += coupling(place_ref[0], bond) * ref[...]
    refs[-1][...] = total


def hop_sum(config, refs):
    total = coupling(config, 0) * refs[-1][...]
    return total + coupling(config, 1) * jnp.concatenate([refs[0][...], refs[1][...]], axis=0)


def store_halves(value, out_ref, first_ref, second_ref):
    middle = first_ref.shape[0]
    out_ref[...] = value
    first_ref[...] = value[:middle]
    second_ref[...] = value[middle:]


def start_kernel(live_ref, vectors_ref, out_ref, first_ref, second_ref):
    start = vectors_ref[...] * alive_of(live_ref, 0, vectors_ref.shape[1])
    store_halves(start, out_ref, first_ref, second_ref)


def combine_kernel(place_ref, live_ref, own_ref, *refs):
    hops, outs = refs[:-3], refs[-3:]
    total = own_ref[...] + hop_sum(place_ref[0], hops)
    store_halves(alive_of(live_ref, 0, total.shape[1]) * total * (1.0 / HALF_WIDTH), *outs)


def filter_kernel(place_ref, live_ref, own_ref, start_ref, *refs):
    hops, (kept_ref, sent_ref, lead_ref, rest_ref) = refs[:-4], refs[-4:]
    total = own_ref[...] + hop_sum(place_ref[0], hops)
    image = alive_of(live_ref, 0, total.shape[1]) * total * (1.0 / HALF_WIDTH)
    second = 2.0 * image - start_ref[...]
    kept_ref[...] = second
    lead_ref[...] = second[:, : lead_ref.shape[1]]
    rest_ref[...] = second[:, lead_ref.shape[1] :]
    width = sent_ref.shape[1]
    sent_ref[...] = jnp.where(place_ref[1] == 0, second[:, :width], second[:, width:])


def crossed_kernel(bonds, states, place_ref, own_ref, field_ref, *refs):
    hops, out_ref = refs[:-1], refs[-1]
    count = own_ref.shape[0]
    near = coupling(place_ref[0], 1) * hops[-1][...]
    theirs = jnp.where(place_ref[1] == 0, 0.0, near), jnp.where(place_ref[1] == 0, near, 0.0)
    theirs = jnp.concatenate(theirs, axis=1)
    for lead, rest in zip(hops, hops[bonds - 2 : -1]):
        theirs += HOP_SCALE * jnp.concatenate([lead[...], rest[...]], axis=1)
    crossed = product(stacked(field_ref[...]), stacked(theirs))
    out_ref[:, :count] = own_ref[:, :count] * (1.0 / states)
    projected = own_ref[:, count:] + crossed + crossed.T
    out_ref[:, count:] = projected * (1.0 / (HALF_WIDTH * states))


def local(vectors, tile_values, tile_cols, live_rows, boundary_map, field_levels):
    dev_count = lax.axis_size(AXES)
    bonds = dev_count.bit_length() - 2
    flip = (dev_count - 1) // 3
    position = lax.axis_index(AXES)
    parity = sum(bit(position, place) for place in range(0, bonds + 1, 2)) & 1
    place = jnp.stack([position ^ flip, parity]).astype(jnp.int32)
    table = jnp.concatenate([place, field_levels, tile_cols])
    vec_count, row_count = vectors.shape
    tile_size = tile_values.shape[1]
    block_count = row_count // tile_size
    per_block = tile_values.shape[0] // block_count
    tiles = tile_values.reshape(block_count, per_block, tile_size, tile_size)
    targets = boundary_map.reshape(1, row_count)
    params = pltpu.CompilerParams(vmem_limit_bytes=LIMIT)

    def coupled(here, bond):
        return bit(here ^ flip, bond) != bit(here ^ flip, bond + 1)

    def hop(value, bond):
        pairs = [(here, here ^ (3 << bond) if coupled(here, bond) else here) for here in range(dev_count)]
        return lax.ppermute(value, AXES, pairs)

    def one_way(value, bond, lead):
        pairs = []
        for here in range(dev_count):
            ahead = bit(here, bond) ^ bit(here, bond - 1) == lead
            if coupled(here, bond) and ahead:
                pairs.append((here, here ^ (3 << bond)))
            if bond == 2 and coupled(here, 0) and not ahead:
                pairs.append((here, here ^ 3))
        return lax.ppermute(value, AXES, pairs)

    def near(flipped):
        pairs = [(here, here ^ (1 if coupled(here, 0) else 2)) for here in range(dev_count)]
        return lax.ppermute(flipped, AXES, pairs)

    def exchange(value, mask):
        return lax.ppermute(value, AXES, [(source, source ^ mask) for source in range(dev_count)])

    inside = pl.BlockSpec(memory_space=pltpu.VMEM)
    own_cost = pl.CostEstimate(
        flops=8 * vec_count * row_count * per_block * tile_size,
        bytes_accessed=4 * tile_values.size + 12 * vec_count * row_count,
        transcendentals=0,
    )
    split = pltpu.VMEM((2 * vec_count, row_count), BF16)
    gram_shape = jax.ShapeDtypeStruct((vec_count, 2 * vec_count), F32)

    def rows_by(count, width):
        return jax.ShapeDtypeStruct((count, width), F32)

    full = rows_by(vec_count, row_count)

    def first_own_part(field, flipped):
        return pl.pallas_call(
            functools.partial(first_own_kernel, bonds + 1),
            out_shape=full,
            in_specs=[SMEM] + [inside] * 2 + [pl.BlockSpec(memory_space=pl.ANY), inside],
            out_specs=inside,
            scratch_shapes=[
                split,
                pltpu.VMEM(tiles.shape, F32),
                pltpu.SemaphoreType.DMA((STEPS,)),
            ],
            compiler_params=pltpu.CompilerParams(vmem_limit_bytes=FIRST_LIMIT),
            cost_estimate=own_cost,
            name="first_own",
        )(table, field, flipped, tiles, targets)

    def own_part(field, flipped):
        return pl.pallas_call(
            functools.partial(own_kernel, bonds + 1),
            out_shape=full,
            in_specs=[SMEM] + [inside] * 4,
            out_specs=inside,
            scratch_shapes=[split],
            compiler_params=params,
            cost_estimate=own_cost,
            name="own",
        )(table, field, flipped, tiles, targets)

    def own_gram(field, flipped):
        return pl.pallas_call(
            functools.partial(own_gram_kernel, bonds + 1),
            out_shape=[gram_shape, full],
            in_specs=[SMEM] * 2 + [inside] * 4,
            out_specs=[inside, pl.BlockSpec(memory_space=pl.ANY)],
            scratch_shapes=[split, pltpu.SemaphoreType.DMA(())],
            compiler_params=params,
            cost_estimate=own_cost,
            name="own_gram",
        )(table, live_rows, field, flipped, tiles, targets)

    three = [full, rows_by(vec_count // 2, row_count), rows_by(vec_count // 2, row_count)]

    def apply(own, field, first_half, second_half):
        legs = [(here, here ^ 2) for here in range(dev_count) if coupled(here, 1)]
        round_way = [(here, here ^ 4) for here in range(dev_count) if not coupled(here, 1)]
        flipped = exchange(field, 1)
        far = [hop(field, bond) for bond in reversed(range(2, bonds))]
        aside = lax.ppermute(lax.ppermute(second_half, AXES, legs), AXES, round_way)
        direct = hop(first_half, 1)
        closest = near(flipped)
        total = pl.pallas_call(
            functools.partial(far_kernel, bonds),
            out_shape=full,
            in_specs=[SMEM] + [inside] * (bonds - 1),
            out_specs=inside,
            input_output_aliases={1: 0},
            compiler_params=params,
            cost_estimate=pl.CostEstimate(flops=vec_count * row_count, bytes_accessed=12 * vec_count * row_count, transcendentals=0),
            name="far",
        )(table, own(field, flipped), *far)
        return total, [direct, aside, closest]

    start, *halves_of = pl.pallas_call(
        start_kernel,
        out_shape=three,
        in_specs=[SMEM, inside],
        out_specs=[inside] * 3,
        compiler_params=params,
        name="start",
    )(live_rows, vectors)
    own, hops = apply(first_own_part, start, *halves_of)
    first, *halves_of = pl.pallas_call(
        combine_kernel,
        out_shape=three,
        in_specs=[SMEM] * 2 + [inside] * 4,
        out_specs=[inside] * 3,
        compiler_params=params,
        name="combine",
    )(table, live_rows, own, *hops)
    own, hops = apply(own_part, first, *halves_of)
    cut = row_count * 3 // 4
    kept, sent, lead, rest = pl.pallas_call(
        filter_kernel,
        out_shape=[full] + [rows_by(vec_count, width) for width in (row_count // 2, cut, row_count - cut)],
        in_specs=[SMEM] * 2 + [inside] * 5,
        out_specs=[inside] * 4,
        compiler_params=params,
        name="filter",
    )(table, live_rows, own, start, *hops)
    flipped = exchange(kept, 1)
    hops = [one_way(lead, bond, 1) for bond in reversed(range(2, bonds))]
    flipped, sent, rest = lax.optimization_barrier((flipped, sent, rest))
    hops += [one_way(rest, bond, 0) for bond in reversed(range(2, bonds))]
    hops += [hop(sent, 1)]
    grams, second = own_gram(kept, flipped)
    sums = pl.pallas_call(
        functools.partial(crossed_kernel, bonds, dev_count * row_count),
        out_shape=gram_shape,
        in_specs=[SMEM] + [inside] * (2 * bonds - 1),
        out_specs=inside,
        compiler_params=params,
        name="crossed",
    )(table, grams, kept, *hops)
    sums = sums + exchange(sums, 1)
    for digit in range(1, bonds + 1, 2):
        near_mask, far_mask = 1 << digit, 2 << digit
        pair = sums + exchange(sums, near_mask)
        if far_mask < dev_count:
            pair = pair + (exchange(sums, far_mask) + exchange(sums, near_mask | far_mask))
        sums = pair
    return (second, sums[:, :vec_count], sums[:, vec_count:])


def solution(mesh):
    in_specs = (
        P(None, ("groups", "hi", "lo")),
        P(("groups", "hi", "lo"), None, None),
        P(("hi", "lo")),
        P(("hi", "lo")),
        P(("hi", "lo")),
        P("groups"),
    )
    out_specs = (P(None, ("groups", "hi", "lo")), P("groups", None), P("groups", None))
    return jax.shard_map(local, mesh=mesh, in_specs=in_specs, out_specs=out_specs, check_vma=False)
```

```python
import functools

import jax
import jax.numpy as jnp
from jax import lax
from jax.experimental import pallas as pl
from jax.experimental.pallas import tpu as pltpu
from jax.sharding import PartitionSpec as P

HOP_SCALE = 0.5
ANISOTROPY = 1.0
FIELD_STEP = 0.25
HALF_WIDTH = 4.0
AXES = ("hi", "lo")
STEPS = 4
F32, BF16 = jnp.float32, jnp.bfloat16
SMEM = pl.BlockSpec(memory_space=pltpu.SMEM)
LIMIT = 32 * 1024 * 1024
FIRST_LIMIT = 50 * 1024 * 1024


class Part:
    def __init__(self, ref, begin, count):
        self.ref, self.begin, self.shape = ref, begin, (count,)

    def __getitem__(self, index):
        return self.ref[self.begin + index]


def parts_of(table_ref, field_count):
    fields = Part(table_ref, 2, field_count)
    return table_ref, Part(table_ref, 2 + field_count, table_ref.shape[0] - 2 - field_count), fields


def bit(number, place):
    return (number >> place) & 1


def halves(value):
    head = value.astype(BF16)
    return head, (value - head.astype(F32)).astype(BF16)


def stacked(value):
    return jnp.concatenate(halves(value), axis=0)


def product(left, right):
    rows, columns = left.shape[0] // 2, right.shape[0] // 2
    whole = lax.dot_general(left, right, (((1,), (1,)), ((), ())), preferred_element_type=F32)
    tails = whole[:rows, columns:] + whole[rows:, :columns] + whole[rows:, columns:]
    return whole[:rows, :columns] + tails


def coupling(config, bond):
    differ = bit(config, bond) ^ bit(config, bond + 1)
    return jnp.where(differ == 1, HOP_SCALE, 0.0)


def onsite_of(config, fields_ref):
    count = fields_ref.shape[0]
    spins = [bit(config, place).astype(F32) - 0.5 for place in range(count)]
    total = jnp.float32(0.0)
    for place in range(count):
        total += fields_ref[place].astype(F32) * FIELD_STEP * spins[place]
    for place in range(count - 1):
        total += ANISOTROPY * spins[place] * spins[place + 1]
    return total


def alive_of(live_ref, first, count):
    rows = lax.broadcasted_iota(jnp.int32, (1, count), 1) + first
    return (rows < live_ref[0]).astype(F32)


def own_block(block, config, cols_ref, fields_ref, field_ref, split_ref, flipped_ref, tiles_ref, map_ref):
    per_block, tile = tiles_ref.shape[1], tiles_ref.shape[2]
    span = pl.ds(pl.multiple_of(block * tile, tile), tile)
    picked = []
    for which in range(per_block):
        column = cols_ref[block * per_block + which]
        picked.append(split_ref[:, pl.ds(pl.multiple_of(column * tile, tile), tile)])
    weights = jnp.concatenate([tiles_ref[block, which] for which in range(per_block)], axis=1)
    total = product(jnp.concatenate(picked, axis=1), stacked(weights))
    total += onsite_of(config, fields_ref) * field_ref[:, span]
    targets = jnp.broadcast_to(map_ref[:, span], (8, tile))
    inside, outside = targets & (tile - 1), targets // tile
    outside = jnp.where(targets < 0, -1, outside)
    groups = []
    for group in range(field_ref.shape[0] // 8):
        found = jnp.zeros((8, tile), F32)
        for source in range(field_ref.shape[1] // tile):
            values = flipped_ref[group * 8 : group * 8 + 8, source * tile : (source + 1) * tile]
            moved = jnp.take_along_axis(values, inside, axis=1)
            found = jnp.where(outside == source, moved, found)
        groups.append(found)
    return span, total + HOP_SCALE * jnp.concatenate(groups, axis=0)


def first_own_kernel(
    field_count, table_ref, field_ref, flipped_ref, far_tiles, map_ref, out_ref, split_ref, tiles_ref, sems
):
    place_ref, cols_ref, fields_ref = parts_of(table_ref, field_count)
    blocks = tiles_ref.shape[0] // STEPS

    def fetch(step):
        span = pl.ds(step * blocks, blocks)
        return pltpu.make_async_copy(far_tiles.at[span], tiles_ref.at[span], sems.at[step])

    for step in range(STEPS):
        fetch(step).start()
    split_ref[...] = stacked(field_ref[...])

    def body(step, carry):
        fetch(step).wait()
        for row in range(blocks):
            span, total = own_block(
                step * blocks + row, place_ref[0], cols_ref, fields_ref, field_ref, split_ref, flipped_ref, tiles_ref, map_ref
            )
            out_ref[:, span] = total
        return carry

    lax.fori_loop(0, STEPS, body, 0)


def own_kernel(field_count, table_ref, field_ref, flipped_ref, tiles_ref, map_ref, out_ref, split_ref):
    place_ref, cols_ref, fields_ref = parts_of(table_ref, field_count)
    blocks = tiles_ref.shape[0] // STEPS
    split_ref[...] = stacked(field_ref[...])

    def body(step, carry):
        for row in range(blocks):
            span, total = own_block(
                step * blocks + row, place_ref[0], cols_ref, fields_ref, field_ref, split_ref, flipped_ref, tiles_ref, map_ref
            )
            out_ref[:, span] = total
        return carry

    lax.fori_loop(0, STEPS, body, 0)


def own_gram_kernel(
    field_count, table_ref, live_ref, field_ref, flipped_ref, tiles_ref, map_ref, out_ref, copy_ref, split_ref, sem
):
    place_ref, cols_ref, fields_ref = parts_of(table_ref, field_count)
    blocks, tile = tiles_ref.shape[0] // STEPS, tiles_ref.shape[2]
    count, width = field_ref.shape[0], blocks * tile
    copy = pltpu.make_async_copy(field_ref, copy_ref, sem)
    copy.start()
    split_ref[...] = stacked(field_ref[...])
    out_ref[:, :count] = product(split_ref[...], split_ref[...])
    out_ref[:, count:] = jnp.zeros((count, count), F32)

    def body(step, carry):
        parts = []
        for row in range(blocks):
            block = step * blocks + row
            span, total = own_block(
                block, place_ref[0], cols_ref, fields_ref, field_ref, split_ref, flipped_ref, tiles_ref, map_ref
            )
            parts.append(alive_of(live_ref, block * tile, tile) * total)
        image = stacked(jnp.concatenate(parts, axis=1))
        span = pl.ds(pl.multiple_of(step * width, width), width)
        out_ref[:, count:] += product(split_ref[:, span], image)
        return carry

    lax.fori_loop(0, STEPS, body, 0)
    copy.wait()


def far_kernel(bonds, place_ref, own_ref, *refs):
    total = own_ref[...]
    for bond, ref in zip(reversed(range(2, bonds)), refs):
        total += coupling(place_ref[0], bond) * ref[...]
    refs[-1][...] = total


def hop_sum(config, refs):
    total = coupling(config, 0) * refs[-1][...]
    return total + coupling(config, 1) * jnp.concatenate([refs[0][...], refs[1][...]], axis=0)


def store_halves(value, out_ref, first_ref, second_ref):
    middle = first_ref.shape[0]
    out_ref[...] = value
    first_ref[...] = value[:middle]
    second_ref[...] = value[middle:]


def start_kernel(live_ref, vectors_ref, out_ref, first_ref, second_ref):
    start = vectors_ref[...] * alive_of(live_ref, 0, vectors_ref.shape[1])
    store_halves(start, out_ref, first_ref, second_ref)


def combine_kernel(place_ref, live_ref, own_ref, *refs):
    hops, outs = refs[:-3], refs[-3:]
    total = own_ref[...] + hop_sum(place_ref[0], hops)
    store_halves(alive_of(live_ref, 0, total.shape[1]) * total * (1.0 / HALF_WIDTH), *outs)


def filter_kernel(place_ref, live_ref, own_ref, start_ref, *refs):
    hops, (kept_ref, sent_ref, lead_ref, rest_ref) = refs[:-4], refs[-4:]
    total = own_ref[...] + hop_sum(place_ref[0], hops)
    image = alive_of(live_ref, 0, total.shape[1]) * total * (1.0 / HALF_WIDTH)
    second = 2.0 * image - start_ref[...]
    kept_ref[...] = second
    lead_ref[...] = second[:, : lead_ref.shape[1]]
    rest_ref[...] = second[:, lead_ref.shape[1] :]
    width = sent_ref.shape[1]
    sent_ref[...] = jnp.where(place_ref[1] == 0, second[:, :width], second[:, width:])


def crossed_kernel(bonds, states, place_ref, own_ref, field_ref, *refs):
    hops, out_ref = refs[:-1], refs[-1]
    count = own_ref.shape[0]
    near = coupling(place_ref[0], 1) * hops[-1][...]
    theirs = jnp.where(place_ref[1] == 0, 0.0, near), jnp.where(place_ref[1] == 0, near, 0.0)
    theirs = jnp.concatenate(theirs, axis=1)
    for lead, rest in zip(hops, hops[bonds - 2 : -1]):
        theirs += HOP_SCALE * jnp.concatenate([lead[...], rest[...]], axis=1)
    crossed = product(stacked(field_ref[...]), stacked(theirs))
    out_ref[:, :count] = own_ref[:, :count] * (1.0 / states)
    projected = own_ref[:, count:] + crossed + crossed.T
    out_ref[:, count:] = projected * (1.0 / (HALF_WIDTH * states))


def local(vectors, tile_values, tile_cols, live_rows, boundary_map, field_levels):
    dev_count = lax.axis_size(AXES)
    bonds = dev_count.bit_length() - 2
    flip = (dev_count - 1) // 3
    position = lax.axis_index(AXES)
    parity = sum(bit(position, place) for place in range(0, bonds + 1, 2)) & 1
    place = jnp.stack([position ^ flip, parity]).astype(jnp.int32)
    table = jnp.concatenate([place, field_levels, tile_cols])
    vec_count, row_count = vectors.shape
    tile_size = tile_values.shape[1]
    block_count = row_count // tile_size
    per_block = tile_values.shape[0] // block_count
    tiles = tile_values.reshape(block_count, per_block, tile_size, tile_size)
    targets = boundary_map.reshape(1, row_count)
    params = pltpu.CompilerParams(vmem_limit_bytes=LIMIT)

    def coupled(here, bond):
        return bit(here ^ flip, bond) != bit(here ^ flip, bond + 1)

    def hop(value, bond):
        pairs = [(here, here ^ (3 << bond) if coupled(here, bond) else here) for here in range(dev_count)]
        return lax.ppermute(value, AXES, pairs)

    def one_way(value, bond, lead):
        pairs = []
        for here in range(dev_count):
            ahead = bit(here, bond) ^ bit(here, bond - 1) == lead
            if coupled(here, bond) and ahead:
                pairs.append((here, here ^ (3 << bond)))
            if bond == 2 and coupled(here, 0) and not ahead:
                pairs.append((here, here ^ 3))
        return lax.ppermute(value, AXES, pairs)

    def near(flipped):
        pairs = [(here, here ^ (1 if coupled(here, 0) else 2)) for here in range(dev_count)]
        return lax.ppermute(flipped, AXES, pairs)

    def exchange(value, mask):
        return lax.ppermute(value, AXES, [(source, source ^ mask) for source in range(dev_count)])

    inside = pl.BlockSpec(memory_space=pltpu.VMEM)
    own_cost = pl.CostEstimate(
        flops=8 * vec_count * row_count * per_block * tile_size,
        bytes_accessed=4 * tile_values.size + 12 * vec_count * row_count,
        transcendentals=0,
    )
    split = pltpu.VMEM((2 * vec_count, row_count), BF16)
    gram_shape = jax.ShapeDtypeStruct((vec_count, 2 * vec_count), F32)

    def rows_by(count, width):
        return jax.ShapeDtypeStruct((count, width), F32)

    full = rows_by(vec_count, row_count)

    def first_own_part(field, flipped):
        return pl.pallas_call(
            functools.partial(first_own_kernel, bonds + 1),
            out_shape=full,
            in_specs=[SMEM] + [inside] * 2 + [pl.BlockSpec(memory_space=pl.ANY), inside],
            out_specs=inside,
            scratch_shapes=[
                split,
                pltpu.VMEM(tiles.shape, F32),
                pltpu.SemaphoreType.DMA((STEPS,)),
            ],
            compiler_params=pltpu.CompilerParams(vmem_limit_bytes=FIRST_LIMIT),
            cost_estimate=own_cost,
            name="first_own",
        )(table, field, flipped, tiles, targets)

    def own_part(field, flipped):
        return pl.pallas_call(
            functools.partial(own_kernel, bonds + 1),
            out_shape=full,
            in_specs=[SMEM] + [inside] * 4,
            out_specs=inside,
            scratch_shapes=[split],
            compiler_params=params,
            cost_estimate=own_cost,
            name="own",
        )(table, field, flipped, tiles, targets)

    def own_gram(field, flipped):
        return pl.pallas_call(
            functools.partial(own_gram_kernel, bonds + 1),
            out_shape=[gram_shape, full],
            in_specs=[SMEM] * 2 + [inside] * 4,
            out_specs=[inside, pl.BlockSpec(memory_space=pl.ANY)],
            scratch_shapes=[split, pltpu.SemaphoreType.DMA(())],
            compiler_params=params,
            cost_estimate=own_cost,
            name="own_gram",
        )(table, live_rows, field, flipped, tiles, targets)

    three = [full, rows_by(vec_count // 2, row_count), rows_by(vec_count // 2, row_count)]

    def apply(own, field, first_half, second_half):
        legs = [(here, here ^ 2) for here in range(dev_count) if coupled(here, 1)]
        round_way = [(here, here ^ 4) for here in range(dev_count) if not coupled(here, 1)]
        flipped = exchange(field, 1)
        far = [hop(field, bond) for bond in reversed(range(2, bonds))]
        aside = lax.ppermute(lax.ppermute(second_half, AXES, legs), AXES, round_way)
        direct = hop(first_half, 1)
        closest = near(flipped)
        total = pl.pallas_call(
            functools.partial(far_kernel, bonds),
            out_shape=full,
            in_specs=[SMEM] + [inside] * (bonds - 1),
            out_specs=inside,
            input_output_aliases={1: 0},
            compiler_params=params,
            cost_estimate=pl.CostEstimate(flops=vec_count * row_count, bytes_accessed=12 * vec_count * row_count, transcendentals=0),
            name="far",
        )(table, own(field, flipped), *far)
        return total, [direct, aside, closest]

    start, *halves_of = pl.pallas_call(
        start_kernel,
        out_shape=three,
        in_specs=[SMEM, inside],
        out_specs=[inside] * 3,
        compiler_params=params,
        name="start",
    )(live_rows, vectors)
    own, hops = apply(first_own_part, start, *halves_of)
    first, *halves_of = pl.pallas_call(
        combine_kernel,
        out_shape=three,
        in_specs=[SMEM] * 2 + [inside] * 4,
        out_specs=[inside] * 3,
        compiler_params=params,
        name="combine",
    )(table, live_rows, own, *hops)
    own, hops = apply(own_part, first, *halves_of)
    cut = row_count * 3 // 4
    kept, sent, lead, rest = pl.pallas_call(
        filter_kernel,
        out_shape=[full] + [rows_by(vec_count, width) for width in (row_count // 2, cut, row_count - cut)],
        in_specs=[SMEM] * 2 + [inside] * 5,
        out_specs=[inside] * 4,
        compiler_params=params,
        name="filter",
    )(table, live_rows, own, start, *hops)
    flipped = exchange(kept, 1)
    hops = [one_way(lead, bond, 1) for bond in reversed(range(2, bonds))]
    flipped, sent, rest = lax.optimization_barrier((flipped, sent, rest))
    hops += [one_way(rest, bond, 0) for bond in reversed(range(2, bonds))]
    hops += [hop(sent, 1)]
    grams, second = own_gram(kept, flipped)
    sums = pl.pallas_call(
        functools.partial(crossed_kernel, bonds, dev_count * row_count),
        out_shape=gram_shape,
        in_specs=[SMEM] + [inside] * (2 * bonds - 1),
        out_specs=inside,
        compiler_params=params,
        name="crossed",
    )(table, grams, kept, *hops)
    sums = sums + exchange(sums, 1)
    for digit in range(1, bonds + 1, 2):
        near_mask, far_mask = 1 << digit, 2 << digit
        pair = sums + exchange(sums, near_mask)
        if far_mask < dev_count:
            pair = pair + (exchange(sums, far_mask) + exchange(sums, near_mask | far_mask))
        sums = pair
    return (second, sums[:, :vec_count], sums[:, vec_count:])


def solution(mesh):
    in_specs = (
        P(None, ("groups", "hi", "lo")),
        P(("groups", "hi", "lo"), None, None),
        P(("hi", "lo")),
        P(("hi", "lo")),
        P(("hi", "lo")),
        P("groups"),
    )
    out_specs = (P(None, ("groups", "hi", "lo")), P("groups", None), P("groups", None))
    return jax.shard_map(local, mesh=mesh, in_specs=in_specs, out_specs=out_specs, check_vma=False)
```

```python
import functools

import jax
import jax.numpy as jnp
from jax import lax
from jax.experimental import pallas as pl
from jax.experimental.pallas import tpu as pltpu
from jax.sharding import PartitionSpec as P

HOP_SCALE = 0.5
ANISOTROPY = 1.0
FIELD_STEP = 0.25
HALF_WIDTH = 4.0
AXES = ("hi", "lo")
STEPS = 4
F32, BF16 = jnp.float32, jnp.bfloat16
SMEM = pl.BlockSpec(memory_space=pltpu.SMEM)
LIMIT = 32 * 1024 * 1024
FIRST_LIMIT = 47 * 1024 * 1024


class Part:
    def __init__(self, ref, begin, count):
        self.ref, self.begin, self.shape = ref, begin, (count,)

    def __getitem__(self, index):
        return self.ref[self.begin + index]


def parts_of(table_ref, field_count):
    fields = Part(table_ref, 2, field_count)
    return table_ref, Part(table_ref, 2 + field_count, table_ref.shape[0] - 2 - field_count), fields


def bit(number, place):
    return (number >> place) & 1


def halves(value):
    head = value.astype(BF16)
    return head, (value - head.astype(F32)).astype(BF16)


def stacked(value):
    return jnp.concatenate(halves(value), axis=0)


def product(left, right):
    rows, columns = left.shape[0] // 2, right.shape[0] // 2
    whole = lax.dot_general(left, right, (((1,), (1,)), ((), ())), preferred_element_type=F32)
    tails = whole[:rows, columns:] + whole[rows:, :columns] + whole[rows:, columns:]
    return whole[:rows, :columns] + tails


def coupling(config, bond):
    differ = bit(config, bond) ^ bit(config, bond + 1)
    return jnp.where(differ == 1, HOP_SCALE, 0.0)


def onsite_of(config, fields_ref):
    count = fields_ref.shape[0]
    spins = [bit(config, place).astype(F32) - 0.5 for place in range(count)]
    total = jnp.float32(0.0)
    for place in range(count):
        total += fields_ref[place].astype(F32) * FIELD_STEP * spins[place]
    for place in range(count - 1):
        total += ANISOTROPY * spins[place] * spins[place + 1]
    return total


def alive_of(live_ref, first, count):
    rows = lax.broadcasted_iota(jnp.int32, (1, count), 1) + first
    return (rows < live_ref[0]).astype(F32)


def own_block(block, config, cols_ref, fields_ref, field_ref, split_ref, flipped_ref, tiles_ref, map_ref):
    per_block, tile = tiles_ref.shape[1], tiles_ref.shape[2]
    span = pl.ds(pl.multiple_of(block * tile, tile), tile)
    picked = []
    for which in range(per_block):
        column = cols_ref[block * per_block + which]
        picked.append(split_ref[:, pl.ds(pl.multiple_of(column * tile, tile), tile)])
    weights = jnp.concatenate([tiles_ref[block, which] for which in range(per_block)], axis=1)
    total = product(jnp.concatenate(picked, axis=1), stacked(weights))
    total += onsite_of(config, fields_ref) * field_ref[:, span]
    targets = jnp.broadcast_to(map_ref[:, span], (8, tile))
    inside, outside = targets & (tile - 1), targets // tile
    outside = jnp.where(targets < 0, -1, outside)
    groups = []
    for group in range(field_ref.shape[0] // 8):
        found = jnp.zeros((8, tile), F32)
        for source in range(field_ref.shape[1] // tile):
            values = flipped_ref[group * 8 : group * 8 + 8, source * tile : (source + 1) * tile]
            moved = jnp.take_along_axis(values, inside, axis=1)
            found = jnp.where(outside == source, moved, found)
        groups.append(found)
    return span, total + HOP_SCALE * jnp.concatenate(groups, axis=0)


def first_own_kernel(
    field_count, table_ref, field_ref, flipped_ref, far_tiles, map_ref, out_ref, tiles_ref, split_ref, sems
):
    place_ref, cols_ref, fields_ref = parts_of(table_ref, field_count)
    blocks = tiles_ref.shape[0] // STEPS

    def fetch(step):
        span = pl.ds(step * blocks, blocks)
        return pltpu.make_async_copy(far_tiles.at[span], tiles_ref.at[span], sems.at[step])

    for step in range(STEPS):
        fetch(step).start()
    split_ref[...] = stacked(field_ref[...])

    def body(step, carry):
        fetch(step).wait()
        for row in range(blocks):
            span, total = own_block(
                step * blocks + row, place_ref[0], cols_ref, fields_ref, field_ref, split_ref, flipped_ref, tiles_ref, map_ref
            )
            out_ref[:, span] = total
        return carry

    lax.fori_loop(0, STEPS, body, 0)


def own_kernel(field_count, table_ref, field_ref, flipped_ref, tiles_ref, map_ref, out_ref, split_ref):
    place_ref, cols_ref, fields_ref = parts_of(table_ref, field_count)
    blocks = tiles_ref.shape[0] // STEPS
    split_ref[...] = stacked(field_ref[...])

    def body(step, carry):
        for row in range(blocks):
            span, total = own_block(
                step * blocks + row, place_ref[0], cols_ref, fields_ref, field_ref, split_ref, flipped_ref, tiles_ref, map_ref
            )
            out_ref[:, span] = total
        return carry

    lax.fori_loop(0, STEPS, body, 0)


def own_gram_kernel(
    field_count, table_ref, live_ref, field_ref, flipped_ref, tiles_ref, map_ref, out_ref, copy_ref, split_ref, sem
):
    place_ref, cols_ref, fields_ref = parts_of(table_ref, field_count)
    blocks, tile = tiles_ref.shape[0] // STEPS, tiles_ref.shape[2]
    count, width = field_ref.shape[0], blocks * tile
    copy = pltpu.make_async_copy(field_ref, copy_ref, sem)
    copy.start()
    split_ref[...] = stacked(field_ref[...])
    out_ref[:, :count] = product(split_ref[...], split_ref[...])
    out_ref[:, count:] = jnp.zeros((count, count), F32)

    def body(step, carry):
        parts = []
        for row in range(blocks):
            block = step * blocks + row
            span, total = own_block(
                block, place_ref[0], cols_ref, fields_ref, field_ref, split_ref, flipped_ref, tiles_ref, map_ref
            )
            parts.append(alive_of(live_ref, block * tile, tile) * total)
        image = stacked(jnp.concatenate(parts, axis=1))
        span = pl.ds(pl.multiple_of(step * width, width), width)
        out_ref[:, count:] += product(split_ref[:, span], image)
        return carry

    lax.fori_loop(0, STEPS, body, 0)
    copy.wait()


def far_kernel(bonds, place_ref, own_ref, *refs):
    total = own_ref[...]
    for bond, ref in zip(reversed(range(2, bonds)), refs):
        total += coupling(place_ref[0], bond) * ref[...]
    refs[-1][...] = total


def hop_sum(config, refs):
    total = coupling(config, 0) * refs[-1][...]
    return total + coupling(config, 1) * jnp.concatenate([refs[0][...], refs[1][...]], axis=0)


def store_halves(value, out_ref, first_ref, second_ref):
    middle = first_ref.shape[0]
    out_ref[...] = value
    first_ref[...] = value[:middle]
    second_ref[...] = value[middle:]


def start_kernel(live_ref, vectors_ref, out_ref, first_ref, second_ref):
    start = vectors_ref[...] * alive_of(live_ref, 0, vectors_ref.shape[1])
    store_halves(start, out_ref, first_ref, second_ref)


def combine_kernel(place_ref, live_ref, own_ref, *refs):
    hops, outs = refs[:-3], refs[-3:]
    total = own_ref[...] + hop_sum(place_ref[0], hops)
    store_halves(alive_of(live_ref, 0, total.shape[1]) * total * (1.0 / HALF_WIDTH), *outs)


def filter_kernel(place_ref, live_ref, own_ref, start_ref, *refs):
    hops, (kept_ref, sent_ref, lead_ref, rest_ref) = refs[:-4], refs[-4:]
    total = own_ref[...] + hop_sum(place_ref[0], hops)
    image = alive_of(live_ref, 0, total.shape[1]) * total * (1.0 / HALF_WIDTH)
    second = 2.0 * image - start_ref[...]
    kept_ref[...] = second
    lead_ref[...] = second[:, : lead_ref.shape[1]]
    rest_ref[...] = second[:, lead_ref.shape[1] :]
    width = sent_ref.shape[1]
    sent_ref[...] = jnp.where(place_ref[1] == 0, second[:, :width], second[:, width:])


def crossed_kernel(bonds, states, place_ref, own_ref, field_ref, *refs):
    hops, out_ref = refs[:-1], refs[-1]
    count = own_ref.shape[0]
    near = coupling(place_ref[0], 1) * hops[-1][...]
    theirs = jnp.where(place_ref[1] == 0, 0.0, near), jnp.where(place_ref[1] == 0, near, 0.0)
    theirs = jnp.concatenate(theirs, axis=1)
    for lead, rest in zip(hops, hops[bonds - 2 : -1]):
        theirs += HOP_SCALE * jnp.concatenate([lead[...], rest[...]], axis=1)
    crossed = product(stacked(field_ref[...]), stacked(theirs))
    out_ref[:, :count] = own_ref[:, :count] * (1.0 / states)
    projected = own_ref[:, count:] + crossed + crossed.T
    out_ref[:, count:] = projected * (1.0 / (HALF_WIDTH * states))


def local(vectors, tile_values, tile_cols, live_rows, boundary_map, field_levels):
    dev_count = lax.axis_size(AXES)
    bonds = dev_count.bit_length() - 2
    flip = (dev_count - 1) // 3
    position = lax.axis_index(AXES)
    parity = sum(bit(position, place) for place in range(0, bonds + 1, 2)) & 1
    place = jnp.stack([position ^ flip, parity]).astype(jnp.int32)
    table = jnp.concatenate([place, field_levels, tile_cols])
    vec_count, row_count = vectors.shape
    tile_size = tile_values.shape[1]
    block_count = row_count // tile_size
    per_block = tile_values.shape[0] // block_count
    tiles = tile_values.reshape(block_count, per_block, tile_size, tile_size)
    targets = boundary_map.reshape(1, row_count)
    params = pltpu.CompilerParams(vmem_limit_bytes=LIMIT)

    def coupled(here, bond):
        return bit(here ^ flip, bond) != bit(here ^ flip, bond + 1)

    def hop(value, bond):
        pairs = [(here, here ^ (3 << bond) if coupled(here, bond) else here) for here in range(dev_count)]
        return lax.ppermute(value, AXES, pairs)

    def one_way(value, bond, lead):
        pairs = []
        for here in range(dev_count):
            ahead = bit(here, bond) ^ bit(here, bond - 1) == lead
            if coupled(here, bond) and ahead:
                pairs.append((here, here ^ (3 << bond)))
            if bond == 2 and coupled(here, 0) and not ahead:
                pairs.append((here, here ^ 3))
        return lax.ppermute(value, AXES, pairs)

    def near(flipped):
        pairs = [(here, here ^ (1 if coupled(here, 0) else 2)) for here in range(dev_count)]
        return lax.ppermute(flipped, AXES, pairs)

    def exchange(value, mask):
        return lax.ppermute(value, AXES, [(source, source ^ mask) for source in range(dev_count)])

    inside = pl.BlockSpec(memory_space=pltpu.VMEM)
    own_cost = pl.CostEstimate(
        flops=8 * vec_count * row_count * per_block * tile_size,
        bytes_accessed=4 * tile_values.size + 12 * vec_count * row_count,
        transcendentals=0,
    )
    split = pltpu.VMEM((2 * vec_count, row_count), BF16)
    gram_shape = jax.ShapeDtypeStruct((vec_count, 2 * vec_count), F32)

    def rows_by(count, width):
        return jax.ShapeDtypeStruct((count, width), F32)

    full = rows_by(vec_count, row_count)

    def first_own_part(field, flipped):
        return pl.pallas_call(
            functools.partial(first_own_kernel, bonds + 1),
            out_shape=[full, jax.ShapeDtypeStruct(tiles.shape, F32)],
            in_specs=[SMEM] + [inside] * 2 + [pl.BlockSpec(memory_space=pl.ANY), inside],
            out_specs=[inside, inside],
            scratch_shapes=[
                split,
                pltpu.SemaphoreType.DMA((STEPS,)),
            ],
            compiler_params=pltpu.CompilerParams(vmem_limit_bytes=FIRST_LIMIT),
            cost_estimate=own_cost,
            name="first_own",
        )(table, field, flipped, tiles, targets)

    def own_part(field, flipped, tiles):
        return pl.pallas_call(
            functools.partial(own_kernel, bonds + 1),
            out_shape=full,
            in_specs=[SMEM] + [inside] * 4,
            out_specs=inside,
            scratch_shapes=[split],
            compiler_params=params,
            cost_estimate=own_cost,
            name="own",
        )(table, field, flipped, tiles, targets)

    def own_gram(field, flipped, tiles):
        return pl.pallas_call(
            functools.partial(own_gram_kernel, bonds + 1),
            out_shape=[gram_shape, full],
            in_specs=[SMEM] * 2 + [inside] * 4,
            out_specs=[inside, pl.BlockSpec(memory_space=pl.ANY)],
            scratch_shapes=[split, pltpu.SemaphoreType.DMA(())],
            compiler_params=params,
            cost_estimate=own_cost,
            name="own_gram",
        )(table, live_rows, field, flipped, tiles, targets)

    three = [full, rows_by(vec_count // 2, row_count), rows_by(vec_count // 2, row_count)]

    def apply(own_of, field, first_half, second_half):
        legs = [(here, here ^ 2) for here in range(dev_count) if coupled(here, 1)]
        round_way = [(here, here ^ 4) for here in range(dev_count) if not coupled(here, 1)]
        flipped = exchange(field, 1)
        far = [hop(field, bond) for bond in reversed(range(2, bonds))]
        aside = lax.ppermute(lax.ppermute(second_half, AXES, legs), AXES, round_way)
        direct = hop(first_half, 1)
        closest = near(flipped)
        own, *kept_tiles = own_of(field, flipped)
        total = pl.pallas_call(
            functools.partial(far_kernel, bonds),
            out_shape=full,
            in_specs=[SMEM] + [inside] * (bonds - 1),
            out_specs=inside,
            input_output_aliases={1: 0},
            compiler_params=params,
            cost_estimate=pl.CostEstimate(flops=vec_count * row_count, bytes_accessed=12 * vec_count * row_count, transcendentals=0),
            name="far",
        )(table, own, *far)
        return total, [direct, aside, closest], kept_tiles

    start, *halves_of = pl.pallas_call(
        start_kernel,
        out_shape=three,
        in_specs=[SMEM, inside],
        out_specs=[inside] * 3,
        compiler_params=params,
        name="start",
    )(live_rows, vectors)
    own, hops, (close_tiles,) = apply(first_own_part, start, *halves_of)
    first, *halves_of = pl.pallas_call(
        combine_kernel,
        out_shape=three,
        in_specs=[SMEM] * 2 + [inside] * 4,
        out_specs=[inside] * 3,
        compiler_params=params,
        name="combine",
    )(table, live_rows, own, *hops)
    own, hops, _ = apply(lambda *arrays: (own_part(*arrays, close_tiles),), first, *halves_of)
    cut = row_count * 3 // 4
    kept, sent, lead, rest = pl.pallas_call(
        filter_kernel,
        out_shape=[full] + [rows_by(vec_count, width) for width in (row_count // 2, cut, row_count - cut)],
        in_specs=[SMEM] * 2 + [inside] * 5,
        out_specs=[inside] * 4,
        compiler_params=params,
        name="filter",
    )(table, live_rows, own, start, *hops)
    flipped = exchange(kept, 1)
    hops = [one_way(lead, bond, 1) for bond in reversed(range(2, bonds))]
    flipped, sent, rest = lax.optimization_barrier((flipped, sent, rest))
    hops += [one_way(rest, bond, 0) for bond in reversed(range(2, bonds))]
    hops += [hop(sent, 1)]
    grams, second = own_gram(kept, flipped, close_tiles)
    sums = pl.pallas_call(
        functools.partial(crossed_kernel, bonds, dev_count * row_count),
        out_shape=gram_shape,
        in_specs=[SMEM] + [inside] * (2 * bonds - 1),
        out_specs=inside,
        compiler_params=params,
        name="crossed",
    )(table, grams, kept, *hops)
    sums = sums + exchange(sums, 1)
    for digit in range(1, bonds + 1, 2):
        near_mask, far_mask = 1 << digit, 2 << digit
        pair = sums + exchange(sums, near_mask)
        if far_mask < dev_count:
            pair = pair + (exchange(sums, far_mask) + exchange(sums, near_mask | far_mask))
        sums = pair
    return (second, sums[:, :vec_count], sums[:, vec_count:])


def solution(mesh):
    in_specs = (
        P(None, ("groups", "hi", "lo")),
        P(("groups", "hi", "lo"), None, None),
        P(("hi", "lo")),
        P(("hi", "lo")),
        P(("hi", "lo")),
        P("groups"),
    )
    out_specs = (P(None, ("groups", "hi", "lo")), P("groups", None), P("groups", None))
    return jax.shard_map(local, mesh=mesh, in_specs=in_specs, out_specs=out_specs, check_vma=False)
```

```python
import functools

import jax
import jax.numpy as jnp
from jax import lax
from jax.experimental import pallas as pl
from jax.experimental.pallas import tpu as pltpu
from jax.sharding import PartitionSpec as P

HOP_SCALE = 0.5
ANISOTROPY = 1.0
FIELD_STEP = 0.25
HALF_WIDTH = 4.0
AXES = ("hi", "lo")
STEPS = 4
F32, BF16 = jnp.float32, jnp.bfloat16
SMEM = pl.BlockSpec(memory_space=pltpu.SMEM)
LIMIT = 32 * 1024 * 1024
FIRST_LIMIT = 47 * 1024 * 1024


class Part:
    def __init__(self, ref, begin, count):
        self.ref, self.begin, self.shape = ref, begin, (count,)

    def __getitem__(self, index):
        return self.ref[self.begin + index]


def parts_of(table_ref, field_count):
    fields = Part(table_ref, 2, field_count)
    return table_ref, Part(table_ref, 2 + field_count, table_ref.shape[0] - 2 - field_count), fields


def bit(number, place):
    return (number >> place) & 1


def halves(value):
    head = value.astype(BF16)
    return head, (value - head.astype(F32)).astype(BF16)


def stacked(value):
    return jnp.concatenate(halves(value), axis=0)


def product(left, right):
    rows, columns = left.shape[0] // 2, right.shape[0] // 2
    whole = lax.dot_general(left, right, (((1,), (1,)), ((), ())), preferred_element_type=F32)
    tails = whole[:rows, columns:] + whole[rows:, :columns] + whole[rows:, columns:]
    return whole[:rows, :columns] + tails


def coupling(config, bond):
    differ = bit(config, bond) ^ bit(config, bond + 1)
    return jnp.where(differ == 1, HOP_SCALE, 0.0)


def onsite_of(config, fields_ref):
    count = fields_ref.shape[0]
    spins = [bit(config, place).astype(F32) - 0.5 for place in range(count)]
    total = jnp.float32(0.0)
    for place in range(count):
        total += fields_ref[place].astype(F32) * FIELD_STEP * spins[place]
    for place in range(count - 1):
        total += ANISOTROPY * spins[place] * spins[place + 1]
    return total


def alive_of(live_ref, first, count):
    rows = lax.broadcasted_iota(jnp.int32, (1, count), 1) + first
    return (rows < live_ref[0]).astype(F32)


def own_block(block, config, cols_ref, fields_ref, field_ref, split_ref, flipped_ref, tiles_ref, map_ref):
    per_block, tile = tiles_ref.shape[1], tiles_ref.shape[2]
    span = pl.ds(pl.multiple_of(block * tile, tile), tile)
    picked = []
    for which in range(per_block):
        column = cols_ref[block * per_block + which]
        picked.append(split_ref[:, pl.ds(pl.multiple_of(column * tile, tile), tile)])
    weights = jnp.concatenate([tiles_ref[block, which] for which in range(per_block)], axis=1)
    total = product(jnp.concatenate(picked, axis=1), stacked(weights))
    total += onsite_of(config, fields_ref) * field_ref[:, span]
    targets = jnp.broadcast_to(map_ref[:, span], (8, tile))
    inside, outside = targets & (tile - 1), targets // tile
    outside = jnp.where(targets < 0, -1, outside)
    groups = []
    for group in range(field_ref.shape[0] // 8):
        found = jnp.zeros((8, tile), F32)
        for source in range(field_ref.shape[1] // tile):
            values = flipped_ref[group * 8 : group * 8 + 8, source * tile : (source + 1) * tile]
            moved = jnp.take_along_axis(values, inside, axis=1)
            found = jnp.where(outside == source, moved, found)
        groups.append(found)
    return span, total + HOP_SCALE * jnp.concatenate(groups, axis=0)


def first_own_kernel(
    field_count, table_ref, field_ref, flipped_ref, far_tiles, map_ref, out_ref, tiles_ref, split_ref, sems
):
    place_ref, cols_ref, fields_ref = parts_of(table_ref, field_count)
    blocks = tiles_ref.shape[0] // STEPS

    def fetch(step):
        span = pl.ds(step * blocks, blocks)
        return pltpu.make_async_copy(far_tiles.at[span], tiles_ref.at[span], sems.at[step])

    fetch(0).start()
    split_ref[...] = stacked(field_ref[...])

    def body(step, carry):
        @pl.when(step + 1 < STEPS)
        def _():
            fetch(step + 1).start()

        fetch(step).wait()
        for row in range(blocks):
            span, total = own_block(
                step * blocks + row, place_ref[0], cols_ref, fields_ref, field_ref, split_ref, flipped_ref, tiles_ref, map_ref
            )
            out_ref[:, span] = total
        return carry

    lax.fori_loop(0, STEPS, body, 0)


def own_kernel(field_count, table_ref, field_ref, flipped_ref, tiles_ref, map_ref, out_ref, split_ref):
    place_ref, cols_ref, fields_ref = parts_of(table_ref, field_count)
    blocks = tiles_ref.shape[0] // STEPS
    split_ref[...] = stacked(field_ref[...])

    def body(step, carry):
        for row in range(blocks):
            span, total = own_block(
                step * blocks + row, place_ref[0], cols_ref, fields_ref, field_ref, split_ref, flipped_ref, tiles_ref, map_ref
            )
            out_ref[:, span] = total
        return carry

    lax.fori_loop(0, STEPS, body, 0)


def own_gram_kernel(
    field_count, table_ref, live_ref, field_ref, flipped_ref, tiles_ref, map_ref, out_ref, copy_ref, split_ref, sem
):
    place_ref, cols_ref, fields_ref = parts_of(table_ref, field_count)
    blocks, tile = tiles_ref.shape[0] // STEPS, tiles_ref.shape[2]
    count, width = field_ref.shape[0], blocks * tile
    copy = pltpu.make_async_copy(field_ref, copy_ref, sem)
    copy.start()
    split_ref[...] = stacked(field_ref[...])
    out_ref[:, :count] = product(split_ref[...], split_ref[...])
    out_ref[:, count:] = jnp.zeros((count, count), F32)

    def body(step, carry):
        parts = []
        for row in range(blocks):
            block = step * blocks + row
            span, total = own_block(
                block, place_ref[0], cols_ref, fields_ref, field_ref, split_ref, flipped_ref, tiles_ref, map_ref
            )
            parts.append(alive_of(live_ref, block * tile, tile) * total)
        image = stacked(jnp.concatenate(parts, axis=1))
        span = pl.ds(pl.multiple_of(step * width, width), width)
        out_ref[:, count:] += product(split_ref[:, span], image)
        return carry

    lax.fori_loop(0, STEPS, body, 0)
    copy.wait()


def far_kernel(bonds, place_ref, own_ref, *refs):
    total = own_ref[...]
    for bond, ref in zip(reversed(range(2, bonds)), refs):
        total += coupling(place_ref[0], bond) * ref[...]
    refs[-1][...] = total


def hop_sum(config, refs):
    total = coupling(config, 0) * refs[-1][...]
    return total + coupling(config, 1) * jnp.concatenate([refs[0][...], refs[1][...]], axis=0)


def store_halves(value, out_ref, first_ref, second_ref):
    middle = first_ref.shape[0]
    out_ref[...] = value
    first_ref[...] = value[:middle]
    second_ref[...] = value[middle:]


def start_kernel(live_ref, vectors_ref, out_ref, first_ref, second_ref):
    start = vectors_ref[...] * alive_of(live_ref, 0, vectors_ref.shape[1])
    store_halves(start, out_ref, first_ref, second_ref)


def combine_kernel(place_ref, live_ref, own_ref, *refs):
    hops, outs = refs[:-3], refs[-3:]
    total = own_ref[...] + hop_sum(place_ref[0], hops)
    store_halves(alive_of(live_ref, 0, total.shape[1]) * total * (1.0 / HALF_WIDTH), *outs)


def filter_kernel(place_ref, live_ref, own_ref, start_ref, *refs):
    hops, (kept_ref, sent_ref, lead_ref, rest_ref) = refs[:-4], refs[-4:]
    total = own_ref[...] + hop_sum(place_ref[0], hops)
    image = alive_of(live_ref, 0, total.shape[1]) * total * (1.0 / HALF_WIDTH)
    second = 2.0 * image - start_ref[...]
    kept_ref[...] = second
    lead_ref[...] = second[:, : lead_ref.shape[1]]
    rest_ref[...] = second[:, lead_ref.shape[1] :]
    width = sent_ref.shape[1]
    sent_ref[...] = jnp.where(place_ref[1] == 0, second[:, :width], second[:, width:])


def crossed_kernel(bonds, states, place_ref, own_ref, field_ref, *refs):
    hops, out_ref = refs[:-1], refs[-1]
    count = own_ref.shape[0]
    near = coupling(place_ref[0], 1) * hops[-1][...]
    theirs = jnp.where(place_ref[1] == 0, 0.0, near), jnp.where(place_ref[1] == 0, near, 0.0)
    theirs = jnp.concatenate(theirs, axis=1)
    for lead, rest in zip(hops, hops[bonds - 2 : -1]):
        theirs += HOP_SCALE * jnp.concatenate([lead[...], rest[...]], axis=1)
    crossed = product(stacked(field_ref[...]), stacked(theirs))
    out_ref[:, :count] = own_ref[:, :count] * (1.0 / states)
    projected = own_ref[:, count:] + crossed + crossed.T
    out_ref[:, count:] = projected * (1.0 / (HALF_WIDTH * states))


def local(vectors, tile_values, tile_cols, live_rows, boundary_map, field_levels):
    dev_count = lax.axis_size(AXES)
    bonds = dev_count.bit_length() - 2
    flip = (dev_count - 1) // 3
    position = lax.axis_index(AXES)
    parity = sum(bit(position, place) for place in range(0, bonds + 1, 2)) & 1
    place = jnp.stack([position ^ flip, parity]).astype(jnp.int32)
    table = jnp.concatenate([place, field_levels, tile_cols])
    vec_count, row_count = vectors.shape
    tile_size = tile_values.shape[1]
    block_count = row_count // tile_size
    per_block = tile_values.shape[0] // block_count
    tiles = tile_values.reshape(block_count, per_block, tile_size, tile_size)
    targets = boundary_map.reshape(1, row_count)
    params = pltpu.CompilerParams(vmem_limit_bytes=LIMIT)

    def coupled(here, bond):
        return bit(here ^ flip, bond) != bit(here ^ flip, bond + 1)

    def hop(value, bond):
        pairs = [(here, here ^ (3 << bond) if coupled(here, bond) else here) for here in range(dev_count)]
        return lax.ppermute(value, AXES, pairs)

    def one_way(value, bond, lead):
        pairs = []
        for here in range(dev_count):
            ahead = bit(here, bond) ^ bit(here, bond - 1) == lead
            if coupled(here, bond) and ahead:
                pairs.append((here, here ^ (3 << bond)))
            if bond == 2 and coupled(here, 0) and not ahead:
                pairs.append((here, here ^ 3))
        return lax.ppermute(value, AXES, pairs)

    def near(flipped):
        pairs = [(here, here ^ (1 if coupled(here, 0) else 2)) for here in range(dev_count)]
        return lax.ppermute(flipped, AXES, pairs)

    def exchange(value, mask):
        return lax.ppermute(value, AXES, [(source, source ^ mask) for source in range(dev_count)])

    inside = pl.BlockSpec(memory_space=pltpu.VMEM)
    own_cost = pl.CostEstimate(
        flops=8 * vec_count * row_count * per_block * tile_size,
        bytes_accessed=4 * tile_values.size + 12 * vec_count * row_count,
        transcendentals=0,
    )
    split = pltpu.VMEM((2 * vec_count, row_count), BF16)
    gram_shape = jax.ShapeDtypeStruct((vec_count, 2 * vec_count), F32)

    def rows_by(count, width):
        return jax.ShapeDtypeStruct((count, width), F32)

    full = rows_by(vec_count, row_count)

    def first_own_part(field, flipped):
        return pl.pallas_call(
            functools.partial(first_own_kernel, bonds + 1),
            out_shape=[full, jax.ShapeDtypeStruct(tiles.shape, F32)],
            in_specs=[SMEM] + [inside] * 2 + [pl.BlockSpec(memory_space=pl.ANY), inside],
            out_specs=[inside, inside],
            scratch_shapes=[
                split,
                pltpu.SemaphoreType.DMA((STEPS,)),
            ],
            compiler_params=pltpu.CompilerParams(vmem_limit_bytes=FIRST_LIMIT),
            cost_estimate=own_cost,
            name="first_own",
        )(table, field, flipped, tiles, targets)

    def own_part(field, flipped, tiles):
        return pl.pallas_call(
            functools.partial(own_kernel, bonds + 1),
            out_shape=full,
            in_specs=[SMEM] + [inside] * 4,
            out_specs=inside,
            scratch_shapes=[split],
            compiler_params=params,
            cost_estimate=own_cost,
            name="own",
        )(table, field, flipped, tiles, targets)

    def own_gram(field, flipped, tiles):
        return pl.pallas_call(
            functools.partial(own_gram_kernel, bonds + 1),
            out_shape=[gram_shape, full],
            in_specs=[SMEM] * 2 + [inside] * 4,
            out_specs=[inside, pl.BlockSpec(memory_space=pl.ANY)],
            scratch_shapes=[split, pltpu.SemaphoreType.DMA(())],
            compiler_params=params,
            cost_estimate=own_cost,
            name="own_gram",
        )(table, live_rows, field, flipped, tiles, targets)

    three = [full, rows_by(vec_count // 2, row_count), rows_by(vec_count // 2, row_count)]

    def apply(own_of, field, first_half, second_half):
        legs = [(here, here ^ 2) for here in range(dev_count) if coupled(here, 1)]
        round_way = [(here, here ^ 4) for here in range(dev_count) if not coupled(here, 1)]
        flipped = exchange(field, 1)
        far = [hop(field, bond) for bond in reversed(range(2, bonds))]
        aside = lax.ppermute(lax.ppermute(second_half, AXES, legs), AXES, round_way)
        direct = hop(first_half, 1)
        closest = near(flipped)
        own, *kept_tiles = own_of(field, flipped)
        total = pl.pallas_call(
            functools.partial(far_kernel, bonds),
            out_shape=full,
            in_specs=[SMEM] + [inside] * (bonds - 1),
            out_specs=inside,
            input_output_aliases={1: 0},
            compiler_params=params,
            cost_estimate=pl.CostEstimate(flops=vec_count * row_count, bytes_accessed=12 * vec_count * row_count, transcendentals=0),
            name="far",
        )(table, own, *far)
        return total, [direct, aside, closest], kept_tiles

    start, *halves_of = pl.pallas_call(
        start_kernel,
        out_shape=three,
        in_specs=[SMEM, inside],
        out_specs=[inside] * 3,
        compiler_params=params,
        name="start",
    )(live_rows, vectors)
    own, hops, (close_tiles,) = apply(first_own_part, start, *halves_of)
    first, *halves_of = pl.pallas_call(
        combine_kernel,
        out_shape=three,
        in_specs=[SMEM] * 2 + [inside] * 4,
        out_specs=[inside] * 3,
        compiler_params=params,
        name="combine",
    )(table, live_rows, own, *hops)
    own, hops, _ = apply(lambda *arrays: (own_part(*arrays, close_tiles),), first, *halves_of)
    cut = row_count * 3 // 4
    kept, sent, lead, rest = pl.pallas_call(
        filter_kernel,
        out_shape=[full] + [rows_by(vec_count, width) for width in (row_count // 2, cut, row_count - cut)],
        in_specs=[SMEM] * 2 + [inside] * 5,
        out_specs=[inside] * 4,
        compiler_params=params,
        name="filter",
    )(table, live_rows, own, start, *hops)
    flipped = exchange(kept, 1)
    hops = [one_way(lead, bond, 1) for bond in reversed(range(2, bonds))]
    flipped, sent, rest = lax.optimization_barrier((flipped, sent, rest))
    hops += [one_way(rest, bond, 0) for bond in reversed(range(2, bonds))]
    hops += [hop(sent, 1)]
    grams, second = own_gram(kept, flipped, close_tiles)
    sums = pl.pallas_call(
        functools.partial(crossed_kernel, bonds, dev_count * row_count),
        out_shape=gram_shape,
        in_specs=[SMEM] + [inside] * (2 * bonds - 1),
        out_specs=inside,
        compiler_params=params,
        name="crossed",
    )(table, grams, kept, *hops)
    sums = sums + exchange(sums, 1)
    for digit in range(1, bonds + 1, 2):
        near_mask, far_mask = 1 << digit, 2 << digit
        pair = sums + exchange(sums, near_mask)
        if far_mask < dev_count:
            pair = pair + (exchange(sums, far_mask) + exchange(sums, near_mask | far_mask))
        sums = pair
    return (second, sums[:, :vec_count], sums[:, vec_count:])


def solution(mesh):
    in_specs = (
        P(None, ("groups", "hi", "lo")),
        P(("groups", "hi", "lo"), None, None),
        P(("hi", "lo")),
        P(("hi", "lo")),
        P(("hi", "lo")),
        P("groups"),
    )
    out_specs = (P(None, ("groups", "hi", "lo")), P("groups", None), P("groups", None))
    return jax.shard_map(local, mesh=mesh, in_specs=in_specs, out_specs=out_specs, check_vma=False)
```

```python
import functools

import jax
import jax.numpy as jnp
from jax import lax
from jax.experimental import pallas as pl
from jax.experimental.pallas import tpu as pltpu
from jax.sharding import PartitionSpec as P

HOP_SCALE = 0.5
ANISOTROPY = 1.0
FIELD_STEP = 0.25
HALF_WIDTH = 4.0
AXES = ("hi", "lo")
STEPS = 4
F32, BF16 = jnp.float32, jnp.bfloat16
SMEM = pl.BlockSpec(memory_space=pltpu.SMEM)
LIMIT = 32 * 1024 * 1024
FIRST_LIMIT = 50 * 1024 * 1024


class Part:
    def __init__(self, ref, begin, count):
        self.ref, self.begin, self.shape = ref, begin, (count,)

    def __getitem__(self, index):
        return self.ref[self.begin + index]


def parts_of(table_ref, field_count):
    fields = Part(table_ref, 2, field_count)
    return table_ref, Part(table_ref, 2 + field_count, table_ref.shape[0] - 2 - field_count), fields


def bit(number, place):
    return (number >> place) & 1


def halves(value):
    head = value.astype(BF16)
    return head, (value - head.astype(F32)).astype(BF16)


def stacked(value):
    return jnp.concatenate(halves(value), axis=0)


def product(left, right):
    rows, columns = left.shape[0] // 2, right.shape[0] // 2
    whole = lax.dot_general(left, right, (((1,), (1,)), ((), ())), preferred_element_type=F32)
    tails = whole[:rows, columns:] + whole[rows:, :columns] + whole[rows:, columns:]
    return whole[:rows, :columns] + tails


def coupling(config, bond):
    differ = bit(config, bond) ^ bit(config, bond + 1)
    return jnp.where(differ == 1, HOP_SCALE, 0.0)


def onsite_of(config, fields_ref):
    count = fields_ref.shape[0]
    spins = [bit(config, place).astype(F32) - 0.5 for place in range(count)]
    total = jnp.float32(0.0)
    for place in range(count):
        total += fields_ref[place].astype(F32) * FIELD_STEP * spins[place]
    for place in range(count - 1):
        total += ANISOTROPY * spins[place] * spins[place + 1]
    return total


def alive_of(live_ref, first, count):
    rows = lax.broadcasted_iota(jnp.int32, (1, count), 1) + first
    return (rows < live_ref[0]).astype(F32)


def own_block(block, config, cols_ref, fields_ref, field_ref, split_ref, flipped_ref, tiles_ref, map_ref):
    per_block, tile = tiles_ref.shape[1], tiles_ref.shape[2]
    span = pl.ds(pl.multiple_of(block * tile, tile), tile)
    picked = []
    for which in range(per_block):
        column = cols_ref[block * per_block + which]
        picked.append(split_ref[:, pl.ds(pl.multiple_of(column * tile, tile), tile)])
    weights = jnp.concatenate([tiles_ref[block, which] for which in range(per_block)], axis=1)
    total = product(jnp.concatenate(picked, axis=1), stacked(weights))
    total += onsite_of(config, fields_ref) * field_ref[:, span]
    targets = jnp.broadcast_to(map_ref[:, span], (8, tile))
    inside, outside = targets & (tile - 1), targets // tile
    outside = jnp.where(targets < 0, -1, outside)
    groups = []
    for group in range(field_ref.shape[0] // 8):
        found = jnp.zeros((8, tile), F32)
        for source in range(field_ref.shape[1] // tile):
            values = flipped_ref[group * 8 : group * 8 + 8, source * tile : (source + 1) * tile]
            moved = jnp.take_along_axis(values, inside, axis=1)
            found = jnp.where(outside == source, moved, found)
        groups.append(found)
    return span, total + HOP_SCALE * jnp.concatenate(groups, axis=0)


def first_own_kernel(
    field_count, table_ref, field_ref, flipped_ref, far_tiles, map_ref, out_ref, split_ref, tiles_ref, sems
):
    place_ref, cols_ref, fields_ref = parts_of(table_ref, field_count)
    blocks = tiles_ref.shape[0] // STEPS
    fetched = []
    for step in range(STEPS):
        span = pl.ds(step * blocks, blocks)
        fetched.append(pltpu.make_async_copy(far_tiles.at[span], tiles_ref.at[span], sems.at[step]))
    for copy in fetched:
        copy.start()
    split_ref[...] = stacked(field_ref[...])
    for step in range(STEPS):
        fetched[step].wait()
        for row in range(blocks):
            span, total = own_block(
                step * blocks + row, place_ref[0], cols_ref, fields_ref, field_ref, split_ref, flipped_ref, tiles_ref, map_ref
            )
            out_ref[:, span] = total


def own_kernel(field_count, table_ref, field_ref, flipped_ref, tiles_ref, map_ref, out_ref, split_ref):
    place_ref, cols_ref, fields_ref = parts_of(table_ref, field_count)
    blocks = tiles_ref.shape[0] // STEPS
    split_ref[...] = stacked(field_ref[...])

    def body(step, carry):
        for row in range(blocks):
            span, total = own_block(
                step * blocks + row, place_ref[0], cols_ref, fields_ref, field_ref, split_ref, flipped_ref, tiles_ref, map_ref
            )
            out_ref[:, span] = total
        return carry

    lax.fori_loop(0, STEPS, body, 0)


def own_gram_kernel(
    field_count, table_ref, live_ref, field_ref, flipped_ref, tiles_ref, map_ref, out_ref, copy_ref, split_ref, sem
):
    place_ref, cols_ref, fields_ref = parts_of(table_ref, field_count)
    blocks, tile = tiles_ref.shape[0] // STEPS, tiles_ref.shape[2]
    count, width = field_ref.shape[0], blocks * tile
    copy = pltpu.make_async_copy(field_ref, copy_ref, sem)
    copy.start()
    split_ref[...] = stacked(field_ref[...])
    out_ref[:, :count] = product(split_ref[...], split_ref[...])
    out_ref[:, count:] = jnp.zeros((count, count), F32)

    def body(step, carry):
        parts = []
        for row in range(blocks):
            block = step * blocks + row
            span, total = own_block(
                block, place_ref[0], cols_ref, fields_ref, field_ref, split_ref, flipped_ref, tiles_ref, map_ref
            )
            parts.append(alive_of(live_ref, block * tile, tile) * total)
        image = stacked(jnp.concatenate(parts, axis=1))
        span = pl.ds(pl.multiple_of(step * width, width), width)
        out_ref[:, count:] += product(split_ref[:, span], image)
        return carry

    lax.fori_loop(0, STEPS, body, 0)
    copy.wait()


def far_kernel(bonds, place_ref, own_ref, *refs):
    total = own_ref[...]
    for place, bond in enumerate(reversed(range(2, bonds))):
        both = jnp.concatenate([refs[2 * place][...], refs[2 * place + 1][...]], axis=0)
        total += coupling(place_ref[0], bond) * both
    refs[-1][...] = total


def hop_sum(config, refs):
    total = coupling(config, 0) * refs[-1][...]
    return total + coupling(config, 1) * jnp.concatenate([refs[0][...], refs[1][...]], axis=0)


def store_halves(value, out_ref, first_ref, second_ref):
    middle = first_ref.shape[0]
    out_ref[...] = value
    first_ref[...] = value[:middle]
    second_ref[...] = value[middle:]


def start_kernel(live_ref, vectors_ref, out_ref, first_ref, second_ref):
    start = vectors_ref[...] * alive_of(live_ref, 0, vectors_ref.shape[1])
    store_halves(start, out_ref, first_ref, second_ref)


def combine_kernel(place_ref, live_ref, own_ref, *refs):
    hops, outs = refs[:-3], refs[-3:]
    total = own_ref[...] + hop_sum(place_ref[0], hops)
    store_halves(alive_of(live_ref, 0, total.shape[1]) * total * (1.0 / HALF_WIDTH), *outs)


def filter_kernel(place_ref, live_ref, own_ref, start_ref, *refs):
    hops, (kept_ref, sent_ref, lead_ref, rest_ref) = refs[:-4], refs[-4:]
    total = own_ref[...] + hop_sum(place_ref[0], hops)
    image = alive_of(live_ref, 0, total.shape[1]) * total * (1.0 / HALF_WIDTH)
    second = 2.0 * image - start_ref[...]
    kept_ref[...] = second
    lead_ref[...] = second[:, : lead_ref.shape[1]]
    rest_ref[...] = second[:, lead_ref.shape[1] :]
    width = sent_ref.shape[1]
    sent_ref[...] = jnp.where(place_ref[1] == 0, second[:, :width], second[:, width:])


def crossed_kernel(bonds, states, place_ref, own_ref, field_ref, *refs):
    hops, out_ref = refs[:-1], refs[-1]
    count = own_ref.shape[0]
    near = coupling(place_ref[0], 1) * hops[-1][...]
    theirs = jnp.where(place_ref[1] == 0, 0.0, near), jnp.where(place_ref[1] == 0, near, 0.0)
    theirs = jnp.concatenate(theirs, axis=1)
    for lead, rest in zip(hops, hops[bonds - 2 : -1]):
        theirs += HOP_SCALE * jnp.concatenate([lead[...], rest[...]], axis=1)
    crossed = product(stacked(field_ref[...]), stacked(theirs))
    out_ref[:, :count] = own_ref[:, :count] * (1.0 / states)
    projected = own_ref[:, count:] + crossed + crossed.T
    out_ref[:, count:] = projected * (1.0 / (HALF_WIDTH * states))


def local(vectors, tile_values, tile_cols, live_rows, boundary_map, field_levels):
    dev_count = lax.axis_size(AXES)
    bonds = dev_count.bit_length() - 2
    flip = (dev_count - 1) // 3
    position = lax.axis_index(AXES)
    parity = sum(bit(position, place) for place in range(0, bonds + 1, 2)) & 1
    place = jnp.stack([position ^ flip, parity]).astype(jnp.int32)
    table = jnp.concatenate([place, field_levels, tile_cols])
    vec_count, row_count = vectors.shape
    tile_size = tile_values.shape[1]
    block_count = row_count // tile_size
    per_block = tile_values.shape[0] // block_count
    tiles = tile_values.reshape(block_count, per_block, tile_size, tile_size)
    targets = boundary_map.reshape(1, row_count)
    params = pltpu.CompilerParams(vmem_limit_bytes=LIMIT)

    def coupled(here, bond):
        return bit(here ^ flip, bond) != bit(here ^ flip, bond + 1)

    def hop(value, bond):
        pairs = [(here, here ^ (3 << bond) if coupled(here, bond) else here) for here in range(dev_count)]
        return lax.ppermute(value, AXES, pairs)

    def one_way(value, bond, lead):
        pairs = []
        for here in range(dev_count):
            ahead = bit(here, bond) ^ bit(here, bond - 1) == lead
            if coupled(here, bond) and ahead:
                pairs.append((here, here ^ (3 << bond)))
            if bond == 2 and coupled(here, 0) and not ahead:
                pairs.append((here, here ^ 3))
        return lax.ppermute(value, AXES, pairs)

    def near(flipped):
        pairs = [(here, here ^ (1 if coupled(here, 0) else 2)) for here in range(dev_count)]
        return lax.ppermute(flipped, AXES, pairs)

    def exchange(value, mask):
        return lax.ppermute(value, AXES, [(source, source ^ mask) for source in range(dev_count)])

    inside = pl.BlockSpec(memory_space=pltpu.VMEM)
    own_cost = pl.CostEstimate(
        flops=8 * vec_count * row_count * per_block * tile_size,
        bytes_accessed=4 * tile_values.size + 12 * vec_count * row_count,
        transcendentals=0,
    )
    split = pltpu.VMEM((2 * vec_count, row_count), BF16)
    gram_shape = jax.ShapeDtypeStruct((vec_count, 2 * vec_count), F32)

    def rows_by(count, width):
        return jax.ShapeDtypeStruct((count, width), F32)

    full = rows_by(vec_count, row_count)

    def first_own_part(field, flipped):
        return pl.pallas_call(
            functools.partial(first_own_kernel, bonds + 1),
            out_shape=full,
            in_specs=[SMEM] + [inside] * 2 + [pl.BlockSpec(memory_space=pl.ANY), inside],
            out_specs=inside,
            scratch_shapes=[
                split,
                pltpu.VMEM(tiles.shape, F32),
                pltpu.SemaphoreType.DMA((STEPS,)),
            ],
            compiler_params=pltpu.CompilerParams(vmem_limit_bytes=FIRST_LIMIT),
            cost_estimate=own_cost,
            name="first_own",
        )(table, field, flipped, tiles, targets)

    def own_part(field, flipped):
        return pl.pallas_call(
            functools.partial(own_kernel, bonds + 1),
            out_shape=full,
            in_specs=[SMEM] + [inside] * 4,
            out_specs=inside,
            scratch_shapes=[split],
            compiler_params=params,
            cost_estimate=own_cost,
            name="own",
        )(table, field, flipped, tiles, targets)

    def own_gram(field, flipped):
        return pl.pallas_call(
            functools.partial(own_gram_kernel, bonds + 1),
            out_shape=[gram_shape, full],
            in_specs=[SMEM] * 2 + [inside] * 4,
            out_specs=[inside, pl.BlockSpec(memory_space=pl.ANY)],
            scratch_shapes=[split, pltpu.SemaphoreType.DMA(())],
            compiler_params=params,
            cost_estimate=own_cost,
            name="own_gram",
        )(table, live_rows, field, flipped, tiles, targets)

    three = [full, rows_by(vec_count // 2, row_count), rows_by(vec_count // 2, row_count)]

    def apply(own, field, first_half, second_half):
        legs = [(here, here ^ 2) for here in range(dev_count) if coupled(here, 1)]
        round_way = [(here, here ^ 4) for here in range(dev_count) if not coupled(here, 1)]
        flipped = exchange(field, 1)
        far = [hop(half, bond) for bond in reversed(range(2, bonds)) for half in (first_half, second_half)]
        aside = lax.ppermute(lax.ppermute(second_half, AXES, legs), AXES, round_way)
        direct = hop(first_half, 1)
        closest = near(flipped)
        total = pl.pallas_call(
            functools.partial(far_kernel, bonds),
            out_shape=full,
            in_specs=[SMEM] + [inside] * (2 * bonds - 3),
            out_specs=inside,
            input_output_aliases={1: 0},
            compiler_params=params,
            cost_estimate=pl.CostEstimate(flops=vec_count * row_count, bytes_accessed=12 * vec_count * row_count, transcendentals=0),
            name="far",
        )(table, own(field, flipped), *far)
        return total, [direct, aside, closest]

    start, *halves_of = pl.pallas_call(
        start_kernel,
        out_shape=three,
        in_specs=[SMEM, inside],
        out_specs=[inside] * 3,
        compiler_params=params,
        name="start",
    )(live_rows, vectors)
    own, hops = apply(first_own_part, start, *halves_of)
    first, *halves_of = pl.pallas_call(
        combine_kernel,
        out_shape=three,
        in_specs=[SMEM] * 2 + [inside] * 4,
        out_specs=[inside] * 3,
        compiler_params=params,
        name="combine",
    )(table, live_rows, own, *hops)
    own, hops = apply(own_part, first, *halves_of)
    cut = row_count * 3 // 4
    kept, sent, lead, rest = pl.pallas_call(
        filter_kernel,
        out_shape=[full] + [rows_by(vec_count, width) for width in (row_count // 2, cut, row_count - cut)],
        in_specs=[SMEM] * 2 + [inside] * 5,
        out_specs=[inside] * 4,
        compiler_params=params,
        name="filter",
    )(table, live_rows, own, start, *hops)
    flipped = exchange(kept, 1)
    hops = [one_way(lead, bond, 1) for bond in reversed(range(2, bonds))]
    flipped, sent, rest = lax.optimization_barrier((flipped, sent, rest))
    hops += [one_way(rest, bond, 0) for bond in reversed(range(2, bonds))]
    hops += [hop(sent, 1)]
    grams, second = own_gram(kept, flipped)
    sums = pl.pallas_call(
        functools.partial(crossed_kernel, bonds, dev_count * row_count),
        out_shape=gram_shape,
        in_specs=[SMEM] + [inside] * (2 * bonds - 1),
        out_specs=inside,
        compiler_params=params,
        name="crossed",
    )(table, grams, kept, *hops)
    sums = sums + exchange(sums, 1)
    for digit in range(1, bonds + 1, 2):
        near_mask, far_mask = 1 << digit, 2 << digit
        pair = sums + exchange(sums, near_mask)
        if far_mask < dev_count:
            pair = pair + (exchange(sums, far_mask) + exchange(sums, near_mask | far_mask))
        sums = pair
    return (second, sums[:, :vec_count], sums[:, vec_count:])


def solution(mesh):
    in_specs = (
        P(None, ("groups", "hi", "lo")),
        P(("groups", "hi", "lo"), None, None),
        P(("hi", "lo")),
        P(("hi", "lo")),
        P(("hi", "lo")),
        P("groups"),
    )
    out_specs = (P(None, ("groups", "hi", "lo")), P("groups", None), P("groups", None))
    return jax.shard_map(local, mesh=mesh, in_specs=in_specs, out_specs=out_specs, check_vma=False)
```

```python
import functools

import jax
import jax.numpy as jnp
from jax import lax
from jax.experimental import pallas as pl
from jax.experimental.pallas import tpu as pltpu
from jax.sharding import PartitionSpec as P

HOP_SCALE = 0.5
ANISOTROPY = 1.0
FIELD_STEP = 0.25
HALF_WIDTH = 4.0
AXES = ("hi", "lo")
STEPS = 4
F32, BF16 = jnp.float32, jnp.bfloat16
SMEM = pl.BlockSpec(memory_space=pltpu.SMEM)
LIMIT = 32 * 1024 * 1024
FIRST_LIMIT = 50 * 1024 * 1024


class Part:
    def __init__(self, ref, begin, count):
        self.ref, self.begin, self.shape = ref, begin, (count,)

    def __getitem__(self, index):
        return self.ref[self.begin + index]


def parts_of(table_ref, field_count):
    fields = Part(table_ref, 2, field_count)
    return table_ref, Part(table_ref, 2 + field_count, table_ref.shape[0] - 2 - field_count), fields


def bit(number, place):
    return (number >> place) & 1


def halves(value):
    head = value.astype(BF16)
    return head, (value - head.astype(F32)).astype(BF16)


def stacked(value):
    return jnp.concatenate(halves(value), axis=0)


def product(left, right):
    rows, columns = left.shape[0] // 2, right.shape[0] // 2
    whole = lax.dot_general(left, right, (((1,), (1,)), ((), ())), preferred_element_type=F32)
    tails = whole[:rows, columns:] + whole[rows:, :columns] + whole[rows:, columns:]
    return whole[:rows, :columns] + tails


def coupling(config, bond):
    differ = bit(config, bond) ^ bit(config, bond + 1)
    return jnp.where(differ == 1, HOP_SCALE, 0.0)


def onsite_of(config, fields_ref):
    count = fields_ref.shape[0]
    spins = [bit(config, place).astype(F32) - 0.5 for place in range(count)]
    total = jnp.float32(0.0)
    for place in range(count):
        total += fields_ref[place].astype(F32) * FIELD_STEP * spins[place]
    for place in range(count - 1):
        total += ANISOTROPY * spins[place] * spins[place + 1]
    return total


def alive_of(live_ref, first, count):
    rows = lax.broadcasted_iota(jnp.int32, (1, count), 1) + first
    return (rows < live_ref[0]).astype(F32)


def own_block(block, config, cols_ref, fields_ref, field_ref, split_ref, flipped_ref, tiles_ref, map_ref):
    per_block, tile = tiles_ref.shape[1], tiles_ref.shape[2]
    span = pl.ds(pl.multiple_of(block * tile, tile), tile)
    picked = []
    for which in range(per_block):
        column = cols_ref[block * per_block + which]
        picked.append(split_ref[:, pl.ds(pl.multiple_of(column * tile, tile), tile)])
    weights = jnp.concatenate([tiles_ref[block, which] for which in range(per_block)], axis=1)
    total = product(jnp.concatenate(picked, axis=1), stacked(weights))
    total += onsite_of(config, fields_ref) * field_ref[:, span]
    targets = jnp.broadcast_to(map_ref[:, span], (8, tile))
    inside, outside = targets & (tile - 1), targets // tile
    outside = jnp.where(targets < 0, -1, outside)
    groups = []
    for group in range(field_ref.shape[0] // 8):
        found = jnp.zeros((8, tile), F32)
        for source in range(field_ref.shape[1] // tile):
            values = flipped_ref[group * 8 : group * 8 + 8, source * tile : (source + 1) * tile]
            moved = jnp.take_along_axis(values, inside, axis=1)
            found = jnp.where(outside == source, moved, found)
        groups.append(found)
    return span, total + HOP_SCALE * jnp.concatenate(groups, axis=0)


def first_own_kernel(
    field_count, table_ref, field_ref, flipped_ref, far_tiles, map_ref, out_ref, split_ref, tiles_ref, sems
):
    place_ref, cols_ref, fields_ref = parts_of(table_ref, field_count)
    blocks = tiles_ref.shape[0] // STEPS
    fetched = []
    for step in range(STEPS):
        span = pl.ds(step * blocks, blocks)
        fetched.append(pltpu.make_async_copy(far_tiles.at[span], tiles_ref.at[span], sems.at[step]))
    for copy in fetched:
        copy.start()
    split_ref[...] = stacked(field_ref[...])
    for step in range(STEPS):
        fetched[step].wait()
        for row in range(blocks):
            span, total = own_block(
                step * blocks + row, place_ref[0], cols_ref, fields_ref, field_ref, split_ref, flipped_ref, tiles_ref, map_ref
            )
            out_ref[:, span] = total


def own_kernel(field_count, table_ref, field_ref, flipped_ref, tiles_ref, map_ref, out_ref, split_ref):
    place_ref, cols_ref, fields_ref = parts_of(table_ref, field_count)
    blocks = tiles_ref.shape[0] // STEPS
    split_ref[...] = stacked(field_ref[...])

    def body(step, carry):
        for row in range(blocks):
            span, total = own_block(
                step * blocks + row, place_ref[0], cols_ref, fields_ref, field_ref, split_ref, flipped_ref, tiles_ref, map_ref
            )
            out_ref[:, span] = total
        return carry

    lax.fori_loop(0, STEPS, body, 0)


def own_gram_kernel(
    field_count, table_ref, live_ref, field_ref, flipped_ref, tiles_ref, map_ref, out_ref, copy_ref, split_ref, sem
):
    place_ref, cols_ref, fields_ref = parts_of(table_ref, field_count)
    blocks, tile = tiles_ref.shape[0] // STEPS, tiles_ref.shape[2]
    count, width = field_ref.shape[0], blocks * tile
    copy = pltpu.make_async_copy(field_ref, copy_ref, sem)
    copy.start()
    split_ref[...] = stacked(field_ref[...])
    out_ref[:, :count] = product(split_ref[...], split_ref[...])
    out_ref[:, count:] = jnp.zeros((count, count), F32)

    def body(step, carry):
        parts = []
        for row in range(blocks):
            block = step * blocks + row
            span, total = own_block(
                block, place_ref[0], cols_ref, fields_ref, field_ref, split_ref, flipped_ref, tiles_ref, map_ref
            )
            parts.append(alive_of(live_ref, block * tile, tile) * total)
        image = stacked(jnp.concatenate(parts, axis=1))
        span = pl.ds(pl.multiple_of(step * width, width), width)
        out_ref[:, count:] += product(split_ref[:, span], image)
        return carry

    lax.fori_loop(0, STEPS, body, 0)
    copy.wait()


def far_kernel(bonds, place_ref, own_ref, *refs):
    total = own_ref[...]
    for bond, ref in zip(reversed(range(2, bonds)), refs):
        total += coupling(place_ref[0], bond) * ref[...]
    refs[-1][...] = total


def hop_sum(config, refs):
    total = coupling(config, 0) * refs[-1][...]
    return total + coupling(config, 1) * jnp.concatenate([refs[0][...], refs[1][...]], axis=0)


def store_halves(value, out_ref, first_ref, second_ref):
    middle = first_ref.shape[0]
    out_ref[...] = value
    first_ref[...] = value[:middle]
    second_ref[...] = value[middle:]


def start_kernel(live_ref, vectors_ref, out_ref, first_ref, second_ref):
    start = vectors_ref[...] * alive_of(live_ref, 0, vectors_ref.shape[1])
    store_halves(start, out_ref, first_ref, second_ref)


def combine_kernel(place_ref, live_ref, own_ref, *refs):
    hops, outs = refs[:-3], refs[-3:]
    total = own_ref[...] + hop_sum(place_ref[0], hops)
    store_halves(alive_of(live_ref, 0, total.shape[1]) * total * (1.0 / HALF_WIDTH), *outs)


def filter_kernel(place_ref, live_ref, own_ref, start_ref, *refs):
    hops, (kept_ref, sent_ref, lead_ref, rest_ref) = refs[:-4], refs[-4:]
    total = own_ref[...] + hop_sum(place_ref[0], hops)
    image = alive_of(live_ref, 0, total.shape[1]) * total * (1.0 / HALF_WIDTH)
    second = 2.0 * image - start_ref[...]
    kept_ref[...] = second
    lead_ref[...] = second[:, : lead_ref.shape[1]]
    rest_ref[...] = second[:, lead_ref.shape[1] :]
    width = sent_ref.shape[1]
    sent_ref[...] = jnp.where(place_ref[1] == 0, second[:, :width], second[:, width:])


def crossed_kernel(bonds, states, place_ref, own_ref, field_ref, *refs):
    hops, out_ref = refs[:-1], refs[-1]
    count = own_ref.shape[0]
    near = coupling(place_ref[0], 1) * hops[-1][...]
    theirs = jnp.where(place_ref[1] == 0, 0.0, near), jnp.where(place_ref[1] == 0, near, 0.0)
    theirs = jnp.concatenate(theirs, axis=1)
    for lead, rest in zip(hops, hops[bonds - 2 : -1]):
        theirs += HOP_SCALE * jnp.concatenate([lead[...], rest[...]], axis=1)
    crossed = product(stacked(field_ref[...]), stacked(theirs))
    out_ref[:, :count] = own_ref[:, :count] * (1.0 / states)
    projected = own_ref[:, count:] + crossed + crossed.T
    out_ref[:, count:] = projected * (1.0 / (HALF_WIDTH * states))


def local(vectors, tile_values, tile_cols, live_rows, boundary_map, field_levels):
    dev_count = lax.axis_size(AXES)
    bonds = dev_count.bit_length() - 2
    flip = (dev_count - 1) // 3
    position = lax.axis_index(AXES)
    parity = sum(bit(position, place) for place in range(0, bonds + 1, 2)) & 1
    place = jnp.stack([position ^ flip, parity]).astype(jnp.int32)
    table = jnp.concatenate([place, field_levels, tile_cols])
    vec_count, row_count = vectors.shape
    tile_size = tile_values.shape[1]
    block_count = row_count // tile_size
    per_block = tile_values.shape[0] // block_count
    tiles = tile_values.reshape(block_count, per_block, tile_size, tile_size)
    targets = boundary_map.reshape(1, row_count)
    params = pltpu.CompilerParams(vmem_limit_bytes=LIMIT)

    def coupled(here, bond):
        return bit(here ^ flip, bond) != bit(here ^ flip, bond + 1)

    def hop(value, bond):
        pairs = [(here, here ^ (3 << bond) if coupled(here, bond) else here) for here in range(dev_count)]
        return lax.ppermute(value, AXES, pairs)

    def one_way(value, bond, lead):
        pairs = []
        for here in range(dev_count):
            ahead = bit(here, bond) ^ bit(here, bond - 1) == lead
            if coupled(here, bond) and ahead:
                pairs.append((here, here ^ (3 << bond)))
            if bond == 2 and coupled(here, 0) and not ahead:
                pairs.append((here, here ^ 3))
        return lax.ppermute(value, AXES, pairs)

    def near(flipped):
        pairs = [(here, here ^ (1 if coupled(here, 0) else 2)) for here in range(dev_count)]
        return lax.ppermute(flipped, AXES, pairs)

    def exchange(value, mask):
        return lax.ppermute(value, AXES, [(source, source ^ mask) for source in range(dev_count)])

    inside = pl.BlockSpec(memory_space=pltpu.VMEM)
    own_cost = pl.CostEstimate(
        flops=8 * vec_count * row_count * per_block * tile_size,
        bytes_accessed=4 * tile_values.size + 12 * vec_count * row_count,
        transcendentals=0,
    )
    split = pltpu.VMEM((2 * vec_count, row_count), BF16)
    gram_shape = jax.ShapeDtypeStruct((vec_count, 2 * vec_count), F32)

    def rows_by(count, width):
        return jax.ShapeDtypeStruct((count, width), F32)

    full = rows_by(vec_count, row_count)

    def first_own_part(field, flipped):
        return pl.pallas_call(
            functools.partial(first_own_kernel, bonds + 1),
            out_shape=full,
            in_specs=[SMEM] + [inside] * 2 + [pl.BlockSpec(memory_space=pl.ANY), inside],
            out_specs=inside,
            scratch_shapes=[
                split,
                pltpu.VMEM(tiles.shape, F32),
                pltpu.SemaphoreType.DMA((STEPS,)),
            ],
            compiler_params=pltpu.CompilerParams(vmem_limit_bytes=FIRST_LIMIT),
            cost_estimate=own_cost,
            name="first_own",
        )(table, field, flipped, tiles, targets)

    def own_part(field, flipped):
        return pl.pallas_call(
            functools.partial(own_kernel, bonds + 1),
            out_shape=full,
            in_specs=[SMEM] + [inside] * 4,
            out_specs=inside,
            scratch_shapes=[split],
            compiler_params=params,
            cost_estimate=own_cost,
            name="own",
        )(table, field, flipped, tiles, targets)

    def own_gram(field, flipped):
        return pl.pallas_call(
            functools.partial(own_gram_kernel, bonds + 1),
            out_shape=[gram_shape, full],
            in_specs=[SMEM] * 2 + [inside] * 4,
            out_specs=[inside, pl.BlockSpec(memory_space=pl.ANY)],
            scratch_shapes=[split, pltpu.SemaphoreType.DMA(())],
            compiler_params=params,
            cost_estimate=own_cost,
            name="own_gram",
        )(table, live_rows, field, flipped, tiles, targets)

    three = [full, rows_by(vec_count // 2, row_count), rows_by(vec_count // 2, row_count)]

    def apply(own_of, late, field, first_half, second_half):
        legs = [(here, here ^ 2) for here in range(dev_count) if coupled(here, 1)]
        round_way = [(here, here ^ 4) for here in range(dev_count) if not coupled(here, 1)]
        flipped = exchange(field, 1)
        far = [hop(field, bond) for bond in reversed(range(2, bonds))]
        aside = lax.ppermute(lax.ppermute(second_half, AXES, legs), AXES, round_way)
        direct = hop(first_half, 1)
        own = own_of(field, flipped)
        if late:
            own, flipped = lax.optimization_barrier((own, flipped))
        closest = near(flipped)
        total = pl.pallas_call(
            functools.partial(far_kernel, bonds),
            out_shape=full,
            in_specs=[SMEM] + [inside] * (bonds - 1),
            out_specs=inside,
            input_output_aliases={1: 0},
            compiler_params=params,
            cost_estimate=pl.CostEstimate(flops=vec_count * row_count, bytes_accessed=12 * vec_count * row_count, transcendentals=0),
            name="far",
        )(table, own, *far)
        return total, [direct, aside, closest]

    start, *halves_of = pl.pallas_call(
        start_kernel,
        out_shape=three,
        in_specs=[SMEM, inside],
        out_specs=[inside] * 3,
        compiler_params=params,
        name="start",
    )(live_rows, vectors)
    own, hops = apply(first_own_part, False, start, *halves_of)
    first, *halves_of = pl.pallas_call(
        combine_kernel,
        out_shape=three,
        in_specs=[SMEM] * 2 + [inside] * 4,
        out_specs=[inside] * 3,
        compiler_params=params,
        name="combine",
    )(table, live_rows, own, *hops)
    own, hops = apply(own_part, True, first, *halves_of)
    cut = row_count * 3 // 4
    kept, sent, lead, rest = pl.pallas_call(
        filter_kernel,
        out_shape=[full] + [rows_by(vec_count, width) for width in (row_count // 2, cut, row_count - cut)],
        in_specs=[SMEM] * 2 + [inside] * 5,
        out_specs=[inside] * 4,
        compiler_params=params,
        name="filter",
    )(table, live_rows, own, start, *hops)
    flipped = exchange(kept, 1)
    hops = [one_way(lead, bond, 1) for bond in reversed(range(2, bonds))]
    flipped, sent, rest = lax.optimization_barrier((flipped, sent, rest))
    hops += [one_way(rest, bond, 0) for bond in reversed(range(2, bonds))]
    hops += [hop(sent, 1)]
    grams, second = own_gram(kept, flipped)
    sums = pl.pallas_call(
        functools.partial(crossed_kernel, bonds, dev_count * row_count),
        out_shape=gram_shape,
        in_specs=[SMEM] + [inside] * (2 * bonds - 1),
        out_specs=inside,
        compiler_params=params,
        name="crossed",
    )(table, grams, kept, *hops)
    sums = sums + exchange(sums, 1)
    for digit in range(1, bonds + 1, 2):
        near_mask, far_mask = 1 << digit, 2 << digit
        pair = sums + exchange(sums, near_mask)
        if far_mask < dev_count:
            pair = pair + (exchange(sums, far_mask) + exchange(sums, near_mask | far_mask))
        sums = pair
    return (second, sums[:, :vec_count], sums[:, vec_count:])


def solution(mesh):
    in_specs = (
        P(None, ("groups", "hi", "lo")),
        P(("groups", "hi", "lo"), None, None),
        P(("hi", "lo")),
        P(("hi", "lo")),
        P(("hi", "lo")),
        P("groups"),
    )
    out_specs = (P(None, ("groups", "hi", "lo")), P("groups", None), P("groups", None))
    return jax.shard_map(local, mesh=mesh, in_specs=in_specs, out_specs=out_specs, check_vma=False)
```

```python
import functools

import jax
import jax.numpy as jnp
from jax import lax
from jax.experimental import pallas as pl
from jax.experimental.pallas import tpu as pltpu
from jax.sharding import PartitionSpec as P

HOP_SCALE = 0.5
ANISOTROPY = 1.0
FIELD_STEP = 0.25
HALF_WIDTH = 4.0
AXES = ("hi", "lo")
STEPS = 4
F32, BF16 = jnp.float32, jnp.bfloat16
SMEM = pl.BlockSpec(memory_space=pltpu.SMEM)
LIMIT = 32 * 1024 * 1024
FIRST_LIMIT = 50 * 1024 * 1024


class Part:
    def __init__(self, ref, begin, count):
        self.ref, self.begin, self.shape = ref, begin, (count,)

    def __getitem__(self, index):
        return self.ref[self.begin + index]


def parts_of(table_ref, field_count):
    fields = Part(table_ref, 2, field_count)
    return table_ref, Part(table_ref, 2 + field_count, table_ref.shape[0] - 2 - field_count), fields


def bit(number, place):
    return (number >> place) & 1


def halves(value):
    head = value.astype(BF16)
    return head, (value - head.astype(F32)).astype(BF16)


def stacked(value):
    return jnp.concatenate(halves(value), axis=0)


def product(left, right):
    rows, columns = left.shape[0] // 2, right.shape[0] // 2
    whole = lax.dot_general(left, right, (((1,), (1,)), ((), ())), preferred_element_type=F32)
    tails = whole[:rows, columns:] + whole[rows:, :columns] + whole[rows:, columns:]
    return whole[:rows, :columns] + tails


def coupling(config, bond):
    differ = bit(config, bond) ^ bit(config, bond + 1)
    return jnp.where(differ == 1, HOP_SCALE, 0.0)


def onsite_of(config, fields_ref):
    count = fields_ref.shape[0]
    spins = [bit(config, place).astype(F32) - 0.5 for place in range(count)]
    total = jnp.float32(0.0)
    for place in range(count):
        total += fields_ref[place].astype(F32) * FIELD_STEP * spins[place]
    for place in range(count - 1):
        total += ANISOTROPY * spins[place] * spins[place + 1]
    return total


def alive_of(live_ref, first, count):
    rows = lax.broadcasted_iota(jnp.int32, (1, count), 1) + first
    return (rows < live_ref[0]).astype(F32)


def own_block(block, config, cols_ref, fields_ref, field_ref, split_ref, flipped_ref, tiles_ref, map_ref):
    per_block, tile = tiles_ref.shape[1], tiles_ref.shape[2]
    span = pl.ds(pl.multiple_of(block * tile, tile), tile)
    picked = []
    for which in range(per_block):
        column = cols_ref[block * per_block + which]
        picked.append(split_ref[:, pl.ds(pl.multiple_of(column * tile, tile), tile)])
    weights = jnp.concatenate([tiles_ref[block, which] for which in range(per_block)], axis=1)
    total = product(jnp.concatenate(picked, axis=1), stacked(weights))
    total += onsite_of(config, fields_ref) * field_ref[:, span]
    targets = jnp.broadcast_to(map_ref[:, span], (8, tile))
    inside, outside = targets & (tile - 1), targets // tile
    outside = jnp.where(targets < 0, -1, outside)
    groups = []
    for group in range(field_ref.shape[0] // 8):
        found = jnp.zeros((8, tile), F32)
        for source in range(field_ref.shape[1] // tile):
            values = flipped_ref[group * 8 : group * 8 + 8, source * tile : (source + 1) * tile]
            moved = jnp.take_along_axis(values, inside, axis=1)
            found = jnp.where(outside == source, moved, found)
        groups.append(found)
    return span, total + HOP_SCALE * jnp.concatenate(groups, axis=0)


def first_own_kernel(
    field_count, table_ref, field_ref, flipped_ref, far_tiles, map_ref, out_ref, split_ref, tiles_ref, sems
):
    place_ref, cols_ref, fields_ref = parts_of(table_ref, field_count)
    blocks = tiles_ref.shape[0] // STEPS
    fetched = []
    for step in range(STEPS):
        span = pl.ds(step * blocks, blocks)
        fetched.append(pltpu.make_async_copy(far_tiles.at[span], tiles_ref.at[span], sems.at[step]))
    for copy in fetched:
        copy.start()
    split_ref[...] = stacked(field_ref[...])
    for step in range(STEPS):
        fetched[step].wait()
        for row in range(blocks):
            span, total = own_block(
                step * blocks + row, place_ref[0], cols_ref, fields_ref, field_ref, split_ref, flipped_ref, tiles_ref, map_ref
            )
            out_ref[:, span] = total


def own_kernel(field_count, table_ref, field_ref, flipped_ref, tiles_ref, map_ref, out_ref, split_ref):
    place_ref, cols_ref, fields_ref = parts_of(table_ref, field_count)
    blocks = tiles_ref.shape[0] // STEPS
    split_ref[...] = stacked(field_ref[...])

    def body(step, carry):
        for row in range(blocks):
            span, total = own_block(
                step * blocks + row, place_ref[0], cols_ref, fields_ref, field_ref, split_ref, flipped_ref, tiles_ref, map_ref
            )
            out_ref[:, span] = total
        return carry

    lax.fori_loop(0, STEPS, body, 0)


def own_gram_kernel(
    field_count, table_ref, live_ref, field_ref, flipped_ref, tiles_ref, map_ref, out_ref, copy_ref, split_ref, sem
):
    place_ref, cols_ref, fields_ref = parts_of(table_ref, field_count)
    blocks, tile = tiles_ref.shape[0] // STEPS, tiles_ref.shape[2]
    count, width = field_ref.shape[0], blocks * tile
    copy = pltpu.make_async_copy(field_ref, copy_ref, sem)
    copy.start()
    split_ref[...] = stacked(field_ref[...])
    out_ref[:, :count] = product(split_ref[...], split_ref[...])
    out_ref[:, count:] = jnp.zeros((count, count), F32)

    def body(step, carry):
        parts = []
        for row in range(blocks):
            block = step * blocks + row
            span, total = own_block(
                block, place_ref[0], cols_ref, fields_ref, field_ref, split_ref, flipped_ref, tiles_ref, map_ref
            )
            parts.append(alive_of(live_ref, block * tile, tile) * total)
        image = stacked(jnp.concatenate(parts, axis=1))
        span = pl.ds(pl.multiple_of(step * width, width), width)
        out_ref[:, count:] += product(split_ref[:, span], image)
        return carry

    lax.fori_loop(0, STEPS, body, 0)
    copy.wait()


def far_kernel(bonds, place_ref, own_ref, *refs):
    total = own_ref[...]
    for bond, ref in zip(reversed(range(2, bonds)), refs):
        total += coupling(place_ref[0], bond) * ref[...]
    refs[-1][...] = total


def hop_sum(config, refs):
    total = coupling(config, 0) * refs[-1][...]
    return total + coupling(config, 1) * jnp.concatenate([refs[0][...], refs[1][...]], axis=0)


def store_halves(value, out_ref, first_ref, second_ref):
    middle = first_ref.shape[0]
    out_ref[...] = value
    first_ref[...] = value[:middle]
    second_ref[...] = value[middle:]


def start_kernel(live_ref, vectors_ref, out_ref, first_ref, second_ref):
    start = vectors_ref[...] * alive_of(live_ref, 0, vectors_ref.shape[1])
    store_halves(start, out_ref, first_ref, second_ref)


def combine_kernel(place_ref, live_ref, own_ref, *refs):
    hops, outs = refs[:-3], refs[-3:]
    total = own_ref[...] + hop_sum(place_ref[0], hops)
    store_halves(alive_of(live_ref, 0, total.shape[1]) * total * (1.0 / HALF_WIDTH), *outs)


def filter_kernel(place_ref, live_ref, own_ref, start_ref, *refs):
    hops, (kept_ref, sent_ref, lead_ref, rest_ref) = refs[:-4], refs[-4:]
    total = own_ref[...] + hop_sum(place_ref[0], hops)
    image = alive_of(live_ref, 0, total.shape[1]) * total * (1.0 / HALF_WIDTH)
    second = 2.0 * image - start_ref[...]
    kept_ref[...] = second
    lead_ref[...] = second[:, : lead_ref.shape[1]]
    rest_ref[...] = second[:, lead_ref.shape[1] :]
    width = sent_ref.shape[1]
    sent_ref[...] = jnp.where(place_ref[1] == 0, second[:, :width], second[:, width:])


def crossed_kernel(bonds, states, place_ref, own_ref, field_ref, *refs):
    hops, out_ref = refs[:-1], refs[-1]
    count = own_ref.shape[0]
    near = coupling(place_ref[0], 1) * hops[-1][...]
    theirs = jnp.where(place_ref[1] == 0, 0.0, near), jnp.where(place_ref[1] == 0, near, 0.0)
    theirs = jnp.concatenate(theirs, axis=1)
    for lead, rest in zip(hops, hops[bonds - 2 : -1]):
        theirs += HOP_SCALE * jnp.concatenate([lead[...], rest[...]], axis=1)
    crossed = product(stacked(field_ref[...]), stacked(theirs))
    out_ref[:, :count] = own_ref[:, :count] * (1.0 / states)
    projected = own_ref[:, count:] + crossed + crossed.T
    out_ref[:, count:] = projected * (1.0 / (HALF_WIDTH * states))


def local(vectors, tile_values, tile_cols, live_rows, boundary_map, field_levels):
    dev_count = lax.axis_size(AXES)
    bonds = dev_count.bit_length() - 2
    flip = (dev_count - 1) // 3
    position = lax.axis_index(AXES)
    parity = sum(bit(position, place) for place in range(0, bonds + 1, 2)) & 1
    place = jnp.stack([position ^ flip, parity]).astype(jnp.int32)
    table = jnp.concatenate([place, field_levels, tile_cols])
    vec_count, row_count = vectors.shape
    tile_size = tile_values.shape[1]
    block_count = row_count // tile_size
    per_block = tile_values.shape[0] // block_count
    tiles = tile_values.reshape(block_count, per_block, tile_size, tile_size)
    targets = boundary_map.reshape(1, row_count)
    params = pltpu.CompilerParams(vmem_limit_bytes=LIMIT)

    def coupled(here, bond):
        return bit(here ^ flip, bond) != bit(here ^ flip, bond + 1)

    def hop(value, bond):
        pairs = [(here, here ^ (3 << bond) if coupled(here, bond) else here) for here in range(dev_count)]
        return lax.ppermute(value, AXES, pairs)

    def one_way(value, bond, lead):
        pairs = []
        for here in range(dev_count):
            ahead = bit(here, bond) ^ bit(here, bond - 1) == lead
            if coupled(here, bond) and ahead:
                pairs.append((here, here ^ (3 << bond)))
            if bond == 2 and coupled(here, 0) and not ahead:
                pairs.append((here, here ^ 3))
        return lax.ppermute(value, AXES, pairs)

    def near(flipped):
        pairs = [(here, here ^ (1 if coupled(here, 0) else 2)) for here in range(dev_count)]
        return lax.ppermute(flipped, AXES, pairs)

    def exchange(value, mask):
        return lax.ppermute(value, AXES, [(source, source ^ mask) for source in range(dev_count)])

    inside = pl.BlockSpec(memory_space=pltpu.VMEM)
    own_cost = pl.CostEstimate(
        flops=8 * vec_count * row_count * per_block * tile_size,
        bytes_accessed=4 * tile_values.size + 12 * vec_count * row_count,
        transcendentals=0,
    )
    split = pltpu.VMEM((2 * vec_count, row_count), BF16)
    gram_shape = jax.ShapeDtypeStruct((vec_count, 2 * vec_count), F32)

    def rows_by(count, width):
        return jax.ShapeDtypeStruct((count, width), F32)

    full = rows_by(vec_count, row_count)

    def first_own_part(field, flipped):
        return pl.pallas_call(
            functools.partial(first_own_kernel, bonds + 1),
            out_shape=full,
            in_specs=[SMEM] + [inside] * 2 + [pl.BlockSpec(memory_space=pl.ANY), inside],
            out_specs=inside,
            scratch_shapes=[
                split,
                pltpu.VMEM(tiles.shape, F32),
                pltpu.SemaphoreType.DMA((STEPS,)),
            ],
            compiler_params=pltpu.CompilerParams(vmem_limit_bytes=FIRST_LIMIT),
            cost_estimate=own_cost,
            name="first_own",
        )(table, field, flipped, tiles, targets)

    def own_part(field, flipped):
        return pl.pallas_call(
            functools.partial(own_kernel, bonds + 1),
            out_shape=full,
            in_specs=[SMEM] + [inside] * 4,
            out_specs=inside,
            scratch_shapes=[split],
            compiler_params=params,
            cost_estimate=own_cost,
            name="own",
        )(table, field, flipped, tiles, targets)

    def own_gram(field, flipped):
        return pl.pallas_call(
            functools.partial(own_gram_kernel, bonds + 1),
            out_shape=[gram_shape, full],
            in_specs=[SMEM] * 2 + [inside] * 4,
            out_specs=[inside, pl.BlockSpec(memory_space=pl.ANY)],
            scratch_shapes=[split, pltpu.SemaphoreType.DMA(())],
            compiler_params=params,
            cost_estimate=own_cost,
            name="own_gram",
        )(table, live_rows, field, flipped, tiles, targets)

    three = [full, rows_by(vec_count // 2, row_count), rows_by(vec_count // 2, row_count)]

    def apply(own, field, first_half, second_half):
        legs = [(here, here ^ 2) for here in range(dev_count) if coupled(here, 1)]
        round_way = [(here, here ^ 4) for here in range(dev_count) if not coupled(here, 1)]
        flipped = exchange(field, 1)
        far = [hop(field, bond) for bond in reversed(range(2, bonds))]
        aside = lax.ppermute(lax.ppermute(second_half, AXES, legs), AXES, round_way)
        direct = hop(first_half, 1)
        closest = near(flipped)
        total = pl.pallas_call(
            functools.partial(far_kernel, bonds),
            out_shape=full,
            in_specs=[SMEM] + [inside] * (bonds - 1),
            out_specs=inside,
            input_output_aliases={1: 0},
            compiler_params=params,
            cost_estimate=pl.CostEstimate(flops=vec_count * row_count, bytes_accessed=12 * vec_count * row_count, transcendentals=0),
            name="far",
        )(table, own(field, flipped), *far)
        return total, [direct, aside, closest]

    start, *halves_of = pl.pallas_call(
        start_kernel,
        out_shape=three,
        in_specs=[SMEM, inside],
        out_specs=[inside] * 3,
        compiler_params=params,
        name="start",
    )(live_rows, vectors)
    own, hops = apply(first_own_part, start, *halves_of)
    first, *halves_of = pl.pallas_call(
        combine_kernel,
        out_shape=three,
        in_specs=[SMEM] * 2 + [inside] * 4,
        out_specs=[inside] * 3,
        compiler_params=params,
        name="combine",
    )(table, live_rows, own, *hops)
    own, hops = apply(own_part, first, *halves_of)
    cut = row_count * 3 // 4
    kept, sent, lead, rest = pl.pallas_call(
        filter_kernel,
        out_shape=[full] + [rows_by(vec_count, width) for width in (row_count // 2, cut, row_count - cut)],
        in_specs=[SMEM] * 2 + [inside] * 5,
        out_specs=[inside] * 4,
        compiler_params=params,
        name="filter",
    )(table, live_rows, own, start, *hops)
    flipped = exchange(kept, 1)
    hops = [one_way(lead, bond, 1) for bond in reversed(range(2, bonds))]
    flipped, sent, rest = lax.optimization_barrier((flipped, sent, rest))
    hops += [one_way(rest, bond, 0) for bond in reversed(range(2, bonds))]
    hops += [hop(sent, 1)]
    grams, second = own_gram(kept, flipped)
    sums = pl.pallas_call(
        functools.partial(crossed_kernel, bonds, dev_count * row_count),
        out_shape=gram_shape,
        in_specs=[SMEM] + [inside] * (2 * bonds - 1),
        out_specs=inside,
        compiler_params=params,
        name="crossed",
    )(table, grams, kept, *hops)
    for digit in range(0, bonds + 1, 2):
        near_mask, far_mask = 1 << digit, 2 << digit
        pair = sums + exchange(sums, near_mask)
        if far_mask < dev_count:
            pair = pair + (exchange(sums, far_mask) + exchange(sums, near_mask | far_mask))
        sums = pair
    return (second, sums[:, :vec_count], sums[:, vec_count:])


def solution(mesh):
    in_specs = (
        P(None, ("groups", "hi", "lo")),
        P(("groups", "hi", "lo"), None, None),
        P(("hi", "lo")),
        P(("hi", "lo")),
        P(("hi", "lo")),
        P("groups"),
    )
    out_specs = (P(None, ("groups", "hi", "lo")), P("groups", None), P("groups", None))
    return jax.shard_map(local, mesh=mesh, in_specs=in_specs, out_specs=out_specs, check_vma=False)
```
